32 devices in a mesh: rep: 4 (over y, x), grp: 8 (over z, core).
Axes of the slice: x: 2, y: 2, z: 4, core: 2. Of those that a mesh axis runs over, the one named last changes fastest.
Arguments:
- tokens: bfloat16 [8192, 2048], P(('rep', 'grp')), may hold values from -12 to 12
- block_map: int32 [8, 16], P('rep'), may hold values from 0 to 15, each once within a row
- w_qkvg: bfloat16 [2048, 6144], P('grp'), may hold values from -0.125 to 0.125
- w_out: bfloat16 [2048, 2048], P('grp'), may hold values from -0.75 to 0.75
- w_in: bfloat16 [2048, 2, 6144], P('grp'), may hold values from -0.125 to 0.125
- w_down: bfloat16 [6144, 2048], P('grp'), may hold values from -0.078125 to 0.078125
- norm_attn: bfloat16 [2048], P('grp'), may hold values from 0.099609375 to 1.8984375
- norm_query: bfloat16 [128], P('grp'), may hold values from 0.796875 to 1.796875
- norm_key: bfloat16 [128], P('grp'), may hold values from 0.796875 to 1.796875
- norm_mlp: bfloat16 [2048], P('grp'), may hold values from 0.099609375 to 1.8984375
- cotangent: bfloat16 [8192, 2048], P(('rep', 'grp')), may hold values from -6 to 6
Outputs:
- output: bfloat16 [8192, 2048], P(('rep', 'grp'))
- grad_tokens: bfloat16 [8192, 2048], P(('rep', 'grp'))
- grad_w_qkvg: float32 [2048, 6144], P('grp')
- grad_w_out: float32 [2048, 2048], P('grp')
- grad_w_in: float32 [2048, 2, 6144], P('grp')
- grad_w_down: float32 [6144, 2048], P('grp')
- grad_norm_attn: float32 [2048], P('grp')
- grad_norm_query: float32 [128], P('grp')
- grad_norm_key: float32 [128], P('grp')
- grad_norm_mlp: float32 [2048], P('grp')
The draws below stay inside these ranges and needn't reach their ends.
Inputs may be any that keep to these rules, and one draw needn't show every extreme that they name: `block_map`: each row is a permutation of the 16 blocks of one sequence.
All inputs are finite; a program needn't handle non-finite values.
Results may differ from the reference program's by a relative error of at most 0.02.
Values may be sent and summed in bfloat16 or wider, within the bound.
A program may use at most 512 MiB of HBM per device.

```python
import math
import jax
import jax.numpy as jnp
from jax import lax

D = 2048
QUERY_HEADS = 16
KEY_VALUE_HEADS = 8
HEAD_SIZE = 128
FF = 6144
BLOCK_TOKENS = 64
GROUP_SEQUENCES = 2
QKVG = 6144
BLOCKS = 16
SEQ_LEN = 1024
NSEQ = 8
TOKENS = 8192
N_REP = 4
N_GRP = 8


def draw_tokens(key, part):
    first_key, second_key = jax.random.split(key)
    spread = jnp.exp(jax.random.uniform(second_key, (D,), jnp.float32, jnp.log(0.3), jnp.log(3.0)))
    base_values = jax.random.normal(first_key, (TOKENS, D), jnp.float32)
    return jnp.clip(base_values * spread[None, :], -12.0, 12.0).astype(jnp.bfloat16)


def steps_of(key, shape, shards, least, largest):
    def one(position, shards_of):
        heights = jax.random.uniform(jax.random.fold_in(jax.random.fold_in(key, 6), position), (shards_of,), jnp.float32, least / len(shards), largest / len(shards))
        return jnp.repeat(jnp.exp(heights), shape[position] // shards_of).reshape((-1,) + (1,) * (len(shape) - position - 1))

    loudness = one(*shards[0])
    for cut in shards[1:]:
        loudness = loudness * one(*cut)
    return loudness


def bell_draw(rng, extent, scale, reach, cuts=(), held_as=jnp.bfloat16):
    loudness = steps_of(rng, extent, cuts, -0.22, 0.18) if cuts else 1.0
    drawn = jax.random.normal(rng, extent, jnp.float32) * scale * loudness
    return jnp.minimum(jnp.maximum(drawn, -reach), reach).astype(held_as)


def setup_inputs(seed: int = 0) -> dict:
    arg_keys = jax.random.split(jax.random.key(seed), 12)
    return {
        "tokens": draw_tokens(jax.random.fold_in(arg_keys[11], 71), 0),
        "block_map": jax.vmap(lambda own: jax.random.permutation(own, BLOCKS))(jax.random.split(arg_keys[1], NSEQ)).reshape((NSEQ, BLOCKS)).astype(jnp.int32),
        "w_qkvg": bell_draw(arg_keys[2], (D, QKVG), D ** -0.5, 0.125, ((0, 8),)),
        "w_out": bell_draw(arg_keys[3], (QUERY_HEADS * HEAD_SIZE, D), (HEAD_SIZE // 2) ** -0.5, 0.75, ((0, 8),)),
        "w_in": bell_draw(arg_keys[4], (D, 2, FF), D ** -0.5, 0.125, ((0, 8),)),
        "w_down": bell_draw(arg_keys[5], (FF, D), FF ** -0.5, 0.078125, ((0, 8),)),
        "norm_attn": jnp.clip(1.0 + 0.18 * jax.random.normal(arg_keys[6], (D,), jnp.float32), 0.099609375, 1.8984375).astype(jnp.bfloat16),
        "norm_query": jnp.clip(jnp.exp(math.log(1.796875) - 0.8131065 * jax.random.uniform(arg_keys[7], (HEAD_SIZE,), jnp.float32) ** steps_of(arg_keys[7], (HEAD_SIZE,), ((0, 8),), -0.2, 0.2)), 0.796875, 1.796875).astype(jnp.bfloat16),
        "norm_key": jnp.clip(jnp.exp(math.log(1.796875) - 0.8131065 * jax.random.uniform(arg_keys[8], (HEAD_SIZE,), jnp.float32) ** steps_of(arg_keys[8], (HEAD_SIZE,), ((0, 8),), -0.2, 0.2)), 0.796875, 1.796875).astype(jnp.bfloat16),
        "norm_mlp": jnp.clip(1.0 + 0.18 * jax.random.normal(arg_keys[9], (D,), jnp.float32), 0.099609375, 1.8984375).astype(jnp.bfloat16),
        "cotangent": bell_draw(arg_keys[10], (TOKENS, D), 1.0, 6.0, ((0, 32),)),
    }


HIGH_PRECISION = lax.Precision.HIGHEST
norm_epsilon = 1e-06
rotary_base = 1000000.0
masked_value = -1e+30

@jax.custom_vjp
def low(v):
    return lax.optimization_barrier(v.astype(jnp.bfloat16)).astype(jnp.float32)

@jax.custom_vjp
def low_back(v):
    return v

def low_keep(v):
    return (low(v), None)

def low_pass(kept, grad):
    return (grad,)

def back_keep(v):
    return (v, None)

def back_low(kept, grad):
    return (low(grad),)
low.defvjp(low_keep, low_pass)
low_back.defvjp(back_keep, back_low)

def row_scale(values):
    return lax.rsqrt(lax.optimization_barrier(jnp.mean(values * values, axis=-1, keepdims=True)) + norm_epsilon)

def rotate_half(values):
    middle = values.shape[-1] // 2
    return jnp.concatenate([-values[..., middle:], values[..., :middle]], axis=-1)

def rotary_tables(positions):
    exponent = jnp.arange(HEAD_SIZE // 2, dtype=jnp.float32) * (2.0 / HEAD_SIZE)
    inverse = jnp.power(jnp.float32(rotary_base), -exponent)
    angles = positions.astype(jnp.float32)[..., None] * inverse
    angles = jnp.concatenate([angles, angles], axis=-1)
    return (jnp.cos(angles), jnp.sin(angles))

def sequence_positions(mapping):
    offsets = jnp.arange(BLOCK_TOKENS, dtype=jnp.int32)
    position_table = mapping.astype(jnp.int32)[:, :, None] * BLOCK_TOKENS + offsets[None, None, :]
    return position_table.reshape(mapping.shape[0], -1).astype(jnp.int32)

def attend_sequence(bundle):
    query_rows, key_row_block, value_rows, positions = bundle
    sequence_length = query_rows.shape[0]
    heads_grouped = query_rows.reshape(sequence_length, KEY_VALUE_HEADS, QUERY_HEADS // KEY_VALUE_HEADS, HEAD_SIZE)
    scores = jnp.einsum('qhgd,khd->hgqk', heads_grouped, key_row_block, precision=HIGH_PRECISION) * HEAD_SIZE ** (-0.5)
    scores = low_back(scores)
    allowed = positions[None, :] <= positions[:, None]
    probability = jax.nn.softmax(jnp.where(allowed, scores, masked_value), axis=-1)
    probability = low(probability)
    attended = jnp.einsum('hgqk,khd->qhgd', probability, value_rows, precision=HIGH_PRECISION)
    return low_back(attended.reshape(sequence_length, QUERY_HEADS * HEAD_SIZE))

def split_sequences(values, head_count):
    shaped = values.reshape(N_GRP, GROUP_SEQUENCES, 2 * BLOCK_TOKENS, head_count, HEAD_SIZE)
    return jnp.swapaxes(shaped, 0, 1).reshape(GROUP_SEQUENCES, SEQ_LEN, head_count, HEAD_SIZE)

def group_forward(group_rows, mapping, w_qkvg, w_out, w_in, w_down, norm_attn, norm_query, norm_key, norm_mlp):
    tokens_here = group_rows.reshape(-1, D)
    attn_input = low(tokens_here * row_scale(tokens_here) * norm_attn)
    projected = jnp.dot(attn_input, w_qkvg, precision=HIGH_PRECISION)
    query_cols = QUERY_HEADS * HEAD_SIZE
    key_column_span = KEY_VALUE_HEADS * HEAD_SIZE
    query_raw = low_back(projected[:, :query_cols])
    gate_raw = low_back(projected[:, query_cols:2 * query_cols])
    key_unnormed = low_back(projected[:, 2 * query_cols:2 * query_cols + key_column_span])
    value_complete = low(low_back(projected[:, 2 * query_cols + key_column_span:]))
    query_heads = query_raw.reshape(-1, QUERY_HEADS, HEAD_SIZE)
    query_normed = query_heads * row_scale(query_heads) * norm_query
    key_head_split = key_unnormed.reshape(-1, KEY_VALUE_HEADS, HEAD_SIZE)
    key_after_norm = key_head_split * row_scale(key_head_split) * norm_key
    positions = sequence_positions(mapping)
    cosine_lookup, sine_lookup = rotary_tables(positions)
    cosine_lookup = cosine_lookup[:, :, None, :]
    sine_lookup = sine_lookup[:, :, None, :]
    query_seq = split_sequences(query_normed, QUERY_HEADS)
    query_rotated = low(query_seq * cosine_lookup + rotate_half(query_seq) * sine_lookup)
    key_sequence = split_sequences(key_after_norm, KEY_VALUE_HEADS)
    key_rot = low(key_sequence * cosine_lookup + rotate_half(key_sequence) * sine_lookup)
    value_sequence = split_sequences(value_complete, KEY_VALUE_HEADS)
    attended = lax.map(jax.checkpoint(attend_sequence), (query_rotated, key_rot, value_sequence, positions))
    attended = jnp.swapaxes(attended.reshape(GROUP_SEQUENCES, N_GRP, 2 * BLOCK_TOKENS, query_cols), 0, 1).reshape(-1, query_cols)
    attn_out = low(attended * jax.nn.sigmoid(gate_raw))
    branch = low_back(jnp.dot(attn_out, w_out, precision=HIGH_PRECISION))
    hidden = tokens_here + branch
    mlp_input = low(hidden * row_scale(hidden) * norm_mlp)
    gate_up = jnp.einsum('td,dcf->tcf', mlp_input, w_in, precision=HIGH_PRECISION)
    gate_value = low_back(gate_up[:, 0])
    up_value = low_back(gate_up[:, 1])
    activated = low(jax.nn.silu(gate_value) * up_value)
    mlp_out = low_back(jnp.dot(activated, w_down, precision=HIGH_PRECISION))
    return (hidden + mlp_out).reshape(group_rows.shape)

def reference(tokens, block_map, w_qkvg, w_out, w_in, w_down, norm_attn, norm_query, norm_key, norm_mlp, cotangent):
    groups = tokens.astype(jnp.float32).reshape(N_REP, N_GRP, GROUP_SEQUENCES, 2 * BLOCK_TOKENS, D)
    group_maps = block_map.reshape(N_REP, GROUP_SEQUENCES, BLOCKS).astype(jnp.int32)

    def forward(group_tokens, qkvg_float, out_float, in_float, down_float, attn_gain, query_gain, key_gain, mlp_gain):

        def one_group(bundle):
            return group_forward(bundle[0], bundle[1], qkvg_float, out_float, in_float, down_float, attn_gain, query_gain, key_gain, mlp_gain)
        return lax.map(jax.checkpoint(one_group), (group_tokens, group_maps))
    result, pullback = jax.vjp(forward, groups, w_qkvg.astype(jnp.float32), w_out.astype(jnp.float32), w_in.astype(jnp.float32), w_down.astype(jnp.float32), norm_attn.astype(jnp.float32), norm_query.astype(jnp.float32), norm_key.astype(jnp.float32), norm_mlp.astype(jnp.float32))
    grads = pullback(cotangent.astype(jnp.float32).reshape(result.shape))
    return (result.reshape(TOKENS, D).astype(jnp.bfloat16), grads[0].reshape(TOKENS, D).astype(jnp.bfloat16), grads[1], grads[2], grads[3], grads[4], grads[5], grads[6], grads[7], grads[8])
```

```python
import jax
import jax.numpy as jnp
from jax import lax
from jax.sharding import PartitionSpec as P

QUERY_HEADS = 16
KEY_VALUE_HEADS = 8
HEAD_SIZE = 128
BLOCK_TOKENS = 64
GROUP_SEQUENCES = 2


norm_epsilon = 1e-06
rotary_base = 1000000.0
masked_value = -1e30


def row_scale(values):
    return lax.rsqrt(jnp.mean(values * values, axis=-1, keepdims=True) + norm_epsilon)


def rotate_half(values):
    middle = values.shape[-1] // 2
    return jnp.concatenate([-values[..., middle:], values[..., :middle]], axis=-1)


def rotary_tables(positions):
    exponent = jnp.arange(HEAD_SIZE // 2, dtype=jnp.float32) * (2.0 / HEAD_SIZE)
    inverse = jnp.power(jnp.float32(rotary_base), -exponent)
    angles = positions.astype(jnp.float32)[..., None] * inverse
    angles = jnp.concatenate([angles, angles], axis=-1)
    return (jnp.cos(angles), jnp.sin(angles))


def unrotate_pairs(gradient, cosine_lookup, sine_lookup):
    return gradient * cosine_lookup - rotate_half(gradient * sine_lookup)


def norm_back(grad_out, normed, scale_rows, gain_vector):
    weighted = grad_out * gain_vector
    grad_in = scale_rows * (weighted - normed * jnp.mean(weighted * normed, axis=-1, keepdims=True))
    return (grad_in, grad_out * normed)


def positions_of(block_ids):
    offsets = jnp.arange(BLOCK_TOKENS, dtype=jnp.int32)
    return (block_ids[:, :, None] * BLOCK_TOKENS + offsets[None, None, :]).reshape(
        block_ids.shape[0], -1
    )


def to_columns(piece):
    reps = lax.axis_size("rep")
    rows, owners, columns = piece.shape
    share = rows // reps
    mine = lax.dynamic_slice_in_dim(piece, lax.axis_index("rep") * share, share, 0)
    swapped = lax.all_to_all(mine, "grp", 1, 0, tiled=True)
    swapped = swapped.reshape(owners, share, columns)
    whole = lax.all_gather(swapped, "rep", axis=1, tiled=True)
    return whole.reshape(owners * rows, columns)


def to_rows(gradient):
    reps = lax.axis_size("rep")
    owners = lax.axis_size("grp")
    rows = gradient.shape[0] // owners
    shaped = gradient.reshape(owners, reps, rows // reps, -1)
    shaped = jnp.swapaxes(shaped, 0, 1).reshape(gradient.shape)
    share = lax.psum_scatter(shaped, "rep", scatter_dimension=0, tiled=True)
    share = share.reshape(owners, rows // reps, -1)
    swapped = lax.all_to_all(share, "grp", 0, 0, tiled=True)
    return lax.all_gather(jnp.swapaxes(swapped, 0, 1), "rep", axis=0, tiled=True)


def sum_rep(gradient):
    share = lax.psum_scatter(gradient, "rep", scatter_dimension=0, tiled=True)
    return lax.all_gather(share, "rep", axis=0, tiled=True)


def body(
    tokens,
    block_map,
    w_qkvg,
    w_out,
    w_in,
    w_down,
    norm_attn,
    norm_query,
    norm_key,
    norm_mlp,
    cotangent,
):
    owners = lax.axis_size("grp")
    me = lax.axis_index("grp")
    heads = QUERY_HEADS // owners
    sharers = max(1, owners // KEY_VALUE_HEADS)
    kv_heads = KEY_VALUE_HEADS * sharers // owners
    per_kv = heads // kv_heads
    q_cols = heads * HEAD_SIZE
    kv_cols = kv_heads * HEAD_SIZE
    rows_here, width = tokens.shape
    shard = w_qkvg.shape[0]
    block_rows = 2 * BLOCK_TOKENS
    seq_len = owners * block_rows
    all_q = QUERY_HEADS * HEAD_SIZE
    all_kv = KEY_VALUE_HEADS * HEAD_SIZE
    hidden_units = w_down.shape[0]

    def by_owner(part, repeat):
        split = part.reshape(shard, owners // repeat, -1)
        return jnp.repeat(split, repeat, axis=1) if repeat > 1 else split

    qkvg_pieces = jnp.concatenate(
        [
            by_owner(w_qkvg[:, :all_q], 1),
            by_owner(w_qkvg[:, all_q : 2 * all_q], 1),
            by_owner(w_qkvg[:, 2 * all_q : 2 * all_q + all_kv], sharers),
            by_owner(w_qkvg[:, 2 * all_q + all_kv :], sharers),
        ],
        axis=2,
    )
    in_pieces = jnp.swapaxes(w_in.reshape(shard, 2, owners, hidden_units), 1, 2).reshape(
        shard, owners, 2 * hidden_units
    )
    tokens_all = lax.all_gather(tokens, "grp", axis=0, tiled=True)
    qkvg_cols = to_columns(qkvg_pieces)
    small = jnp.concatenate([norm_attn, norm_mlp, norm_query, norm_key])
    small_all = lax.all_gather(small, "grp", axis=0, tiled=False).astype(jnp.float32)
    head_part = norm_query.shape[0]
    gain_attn = small_all[:, :shard].reshape(-1)
    gain_mlp = small_all[:, shard : 2 * shard].reshape(-1)
    gain_query = small_all[:, 2 * shard : 2 * shard + head_part].reshape(-1)
    gain_key = small_all[:, 2 * shard + head_part :].reshape(-1)
    in_cols = to_columns(in_pieces)
    cotangent_all = lax.all_gather(cotangent, "grp", axis=0, tiled=True)

    positions = positions_of(block_map)
    cosine, sine = rotary_tables(positions)
    cosine = cosine[:, None]
    sine = sine[:, None]

    def to_heads(values):
        count = values.shape[-1] // HEAD_SIZE
        shaped = values.reshape(owners, GROUP_SEQUENCES, block_rows, count, HEAD_SIZE)
        return shaped.transpose(1, 3, 0, 2, 4).reshape(
            GROUP_SEQUENCES, count, seq_len, HEAD_SIZE
        )

    def from_heads(values):
        count = values.shape[1]
        shaped = values.reshape(GROUP_SEQUENCES, count, owners, block_rows, HEAD_SIZE)
        return shaped.transpose(2, 0, 3, 1, 4).reshape(-1, count * HEAD_SIZE)

    wide_tokens = tokens_all.astype(jnp.float32)
    normed_first = wide_tokens * row_scale(wide_tokens)
    attn_input = (normed_first * gain_attn).astype(jnp.bfloat16)
    projected = jnp.dot(attn_input, qkvg_cols, preferred_element_type=jnp.float32)
    query_heads = to_heads(projected[:, :q_cols])
    gate_raw = projected[:, q_cols : 2 * q_cols]
    key_heads = to_heads(projected[:, 2 * q_cols : 2 * q_cols + kv_cols])
    value_heads = to_heads(projected[:, 2 * q_cols + kv_cols :]).astype(jnp.bfloat16)
    query_scale = row_scale(query_heads)
    query_normed = query_heads * query_scale
    key_scale = row_scale(key_heads)
    key_normed = key_heads * key_scale

    def rotate(values):
        return (values * cosine + rotate_half(values) * sine).astype(jnp.bfloat16)

    query_rot = rotate(query_normed * gain_query).reshape(
        GROUP_SEQUENCES, kv_heads, per_kv, seq_len, HEAD_SIZE
    )
    key_rot = rotate(key_normed * gain_key)
    scores = jnp.einsum(
        "shgqd,shkd->shgqk", query_rot, key_rot, preferred_element_type=jnp.float32
    ) * HEAD_SIZE ** (-0.5)
    allowed = (positions[:, None, :] <= positions[:, :, None])[:, None, None]
    scores = jnp.where(allowed, scores, masked_value)
    top_score = jnp.max(scores, axis=-1, keepdims=True)
    exp_scores = jnp.exp(scores - top_score)
    exp_total = jnp.sum(exp_scores, axis=-1, keepdims=True)
    exact = exp_scores / exp_total
    probability = exact.astype(jnp.bfloat16)
    attended = jnp.einsum(
        "shgqk,shkd->shgqd", probability, value_heads, preferred_element_type=jnp.float32
    ).reshape(GROUP_SEQUENCES, heads, seq_len, HEAD_SIZE)
    attended = from_heads(attended)
    gate_sig = jax.nn.sigmoid(gate_raw)
    attn_out = (attended * gate_sig).astype(jnp.bfloat16)

    def scatter_sum(terms):
        return lax.psum_scatter(
            terms.astype(jnp.bfloat16), "grp", scatter_dimension=0, tiled=True
        ).astype(jnp.float32)

    branch = scatter_sum(jnp.dot(attn_out, w_out, preferred_element_type=jnp.float32))
    hidden = tokens.astype(jnp.float32) + branch
    scale_second = row_scale(hidden)
    normed_second = hidden * scale_second
    mlp_input = lax.all_gather(
        (normed_second * gain_mlp).astype(jnp.bfloat16), "grp", axis=0, tiled=True
    )
    gate_up = jnp.dot(mlp_input, in_cols, preferred_element_type=jnp.float32)
    gate_value = gate_up[:, :hidden_units]
    up_value = gate_up[:, hidden_units:]
    gate_sigmoid = jax.nn.sigmoid(gate_value)
    activated = (gate_value * gate_sigmoid * up_value).astype(jnp.bfloat16)
    grad_activated = jnp.dot(cotangent_all, w_down.T, preferred_element_type=jnp.float32)
    grad_gate = (
        grad_activated * up_value * gate_sigmoid * (1.0 + gate_value * (1.0 - gate_sigmoid))
    ).astype(jnp.bfloat16)
    grad_up = (grad_activated * gate_value * gate_sigmoid).astype(jnp.bfloat16)
    grad_gate_up = jnp.concatenate([grad_gate, grad_up], axis=1)
    grad_mlp_input = scatter_sum(
        jnp.dot(grad_gate_up, in_cols.T, preferred_element_type=jnp.float32)
    )
    mlp_out = scatter_sum(jnp.dot(activated, w_down, preferred_element_type=jnp.float32))
    output = (hidden + mlp_out).astype(jnp.bfloat16)
    term_in = jnp.dot(mlp_input.T, grad_gate_up, preferred_element_type=jnp.float32)
    term_down = jnp.dot(activated.T, cotangent_all, preferred_element_type=jnp.float32)
    grad_hidden_norm, gain_rows_mlp = norm_back(
        grad_mlp_input, normed_second, scale_second, gain_mlp
    )
    grad_hidden = cotangent.astype(jnp.float32) + grad_hidden_norm
    grad_branch = lax.all_gather(
        grad_hidden.astype(jnp.bfloat16), "grp", axis=0, tiled=True
    )
    shard_down = sum_rep(term_down.astype(jnp.bfloat16)).astype(jnp.float32)
    rows_in = to_rows(term_in.astype(jnp.bfloat16)).astype(jnp.float32)
    shard_in = jnp.swapaxes(rows_in.reshape(shard, owners, 2, hidden_units), 1, 2).reshape(
        w_in.shape
    )
    grad_attn_out = jnp.dot(grad_branch, w_out.T, preferred_element_type=jnp.float32)
    attended_gradient = (grad_attn_out * gate_sig).astype(jnp.bfloat16)
    grad_gate_raw = (grad_attn_out * attended * gate_sig * (1.0 - gate_sig)).astype(jnp.bfloat16)
    term_out = jnp.dot(attn_out.T, grad_branch, preferred_element_type=jnp.float32)
    shard_out = sum_rep(term_out.astype(jnp.bfloat16)).astype(jnp.float32)
    head_gradient = to_heads(attended_gradient).reshape(query_rot.shape)
    grad_value = jnp.einsum(
        "shgqk,shgqd->shkd", probability, head_gradient, preferred_element_type=jnp.float32
    )
    grad_probs = jnp.einsum(
        "shgqd,shkd->shgqk", head_gradient, value_heads, preferred_element_type=jnp.float32
    )
    inner_sum = jnp.sum(exact * grad_probs, axis=-1, keepdims=True)
    grad_scores = (exact * (grad_probs - inner_sum)).astype(jnp.bfloat16)
    grad_query = jnp.einsum(
        "shgqk,shkd->shgqd", grad_scores, key_rot, preferred_element_type=jnp.float32
    ).reshape(query_heads.shape) * HEAD_SIZE ** (-0.5)
    grad_key = jnp.einsum(
        "shgqk,shgqd->shkd", grad_scores, query_rot, preferred_element_type=jnp.float32
    ) * HEAD_SIZE ** (-0.5)
    grad_query_raw, gain_rows_query = norm_back(
        unrotate_pairs(grad_query, cosine, sine), query_normed, query_scale, gain_query
    )
    grad_key_raw, gain_rows_key = norm_back(
        unrotate_pairs(grad_key, cosine, sine), key_normed, key_scale, gain_key
    )
    grad_projected = jnp.concatenate(
        [
            from_heads(grad_query_raw.astype(jnp.bfloat16)),
            grad_gate_raw,
            from_heads(grad_key_raw.astype(jnp.bfloat16)),
            from_heads(grad_value.astype(jnp.bfloat16)),
        ],
        axis=-1,
    )
    term_qkvg = jnp.dot(attn_input.T, grad_projected, preferred_element_type=jnp.float32)
    grad_attn_input = scatter_sum(
        jnp.dot(grad_projected, qkvg_cols.T, preferred_element_type=jnp.float32)
    )
    own_tokens = tokens.astype(jnp.float32)
    own_scale = row_scale(own_tokens)
    grad_residual_norm, gain_rows_attn = norm_back(
        grad_attn_input, own_tokens * own_scale, own_scale, gain_attn
    )
    grad_tokens = (grad_hidden + grad_residual_norm).astype(jnp.bfloat16)
    rows_qkvg = to_rows(term_qkvg.astype(jnp.bfloat16)).astype(jnp.float32)

    def joined(part, repeat):
        if repeat > 1:
            part = part.reshape(shard, owners // repeat, repeat, -1).sum(2)
        return part.reshape(shard, -1)

    shard_qkvg = jnp.concatenate(
        [
            joined(rows_qkvg[:, :, :q_cols], 1),
            joined(rows_qkvg[:, :, q_cols : 2 * q_cols], 1),
            joined(rows_qkvg[:, :, 2 * q_cols : 2 * q_cols + kv_cols], sharers),
            joined(rows_qkvg[:, :, 2 * q_cols + kv_cols :], sharers),
        ],
        axis=1,
    )
    gains = lax.psum(
        jnp.concatenate(
            [
                jnp.sum(gain_rows_attn, axis=0),
                jnp.sum(gain_rows_mlp, axis=0),
                jnp.sum(gain_rows_query, axis=(0, 1, 2)),
                jnp.sum(gain_rows_key, axis=(0, 1, 2)),
            ]
        ),
        ("rep", "grp"),
    )
    return (
        output,
        grad_tokens,
        shard_qkvg,
        shard_out,
        shard_in,
        shard_down,
        lax.dynamic_slice_in_dim(gains, me * shard, shard),
        lax.dynamic_slice_in_dim(gains, 2 * width + me * head_part, head_part),
        lax.dynamic_slice_in_dim(gains, 2 * width + HEAD_SIZE + me * head_part, head_part),
        lax.dynamic_slice_in_dim(gains, width + me * shard, shard),
    )


def solution(mesh):
    placed = (
        P(("rep", "grp"), None),
        P("rep", None),
        P("grp", None),
        P("grp", None),
        P("grp", None, None),
        P("grp", None),
        P("grp"),
        P("grp"),
        P("grp"),
        P("grp"),
        P(("rep", "grp"), None),
    )
    return jax.shard_map(
        body,
        mesh=mesh,
        in_specs=placed,
        out_specs=(
            P(("rep", "grp"), None),
            P(("rep", "grp"), None),
            P("grp", None),
            P("grp", None),
            P("grp", None, None),
            P("grp", None),
            P("grp"),
            P("grp"),
            P("grp"),
            P("grp"),
        ),
        check_vma=False,
    )
```

```python
import functools

import jax
import jax.numpy as jnp
from jax import lax
from jax.experimental import pallas as pl
from jax.experimental.pallas import tpu as pltpu
from jax.sharding import PartitionSpec as P

QUERY_HEADS = 16
KEY_VALUE_HEADS = 8
HEAD_SIZE = 128
BLOCK_TOKENS = 64
GROUP_SEQUENCES = 2


norm_epsilon = 1e-06
rotary_base = 1000000.0
masked_value = -1e30


def row_scale(values):
    return lax.rsqrt(jnp.mean(values * values, axis=-1, keepdims=True) + norm_epsilon)


def rotate_half(values):
    middle = values.shape[-1] // 2
    return jnp.concatenate([-values[..., middle:], values[..., :middle]], axis=-1)


def rotary_tables(positions):
    exponent = jnp.arange(HEAD_SIZE // 2, dtype=jnp.float32) * (2.0 / HEAD_SIZE)
    inverse = jnp.power(jnp.float32(rotary_base), -exponent)
    angles = positions.astype(jnp.float32)[..., None] * inverse
    angles = jnp.concatenate([angles, angles], axis=-1)
    return (jnp.cos(angles), jnp.sin(angles))


def unrotate_pairs(gradient, cosine_lookup, sine_lookup):
    return gradient * cosine_lookup - jnp.roll(gradient, HEAD_SIZE // 2, -1) * sine_lookup


def norm_back(grad_out, normed, scale_rows, gain_vector):
    weighted = grad_out * gain_vector
    grad_in = scale_rows * (weighted - normed * jnp.mean(weighted * normed, axis=-1, keepdims=True))
    return (grad_in, grad_out * normed)


MESH = pl.DeviceIdType.MESH
F32 = jnp.float32
BF16 = jnp.bfloat16


def nearest(place, step, chips):
    low = jnp.minimum(place, chips - 1 - place)
    near = (step + 1) // 2
    both = jnp.where(step % 2 == 1, place - near, place + near)
    past = step - low
    rest = jnp.where(place > chips - 1 - place, place - past, place + past)
    return jnp.where(step <= 2 * low, both, rest)


def meet(owners, reps):
    barrier = pltpu.get_barrier_semaphore()
    me, rep = lax.axis_index("grp"), lax.axis_index("rep")
    for ahead in range(1, owners):
        pl.semaphore_signal(
            barrier, 1, device_id={"grp": lax.rem(me + ahead, owners)}, device_id_type=MESH
        )
    for ahead in range(1, reps):
        pl.semaphore_signal(
            barrier, 1, device_id={"rep": lax.rem(rep + ahead, reps)}, device_id_type=MESH
        )
    pl.semaphore_wait(barrier, owners + reps - 2)


def to_grp(source, target, send, recv, device):
    return pltpu.make_async_remote_copy(
        src_ref=source,
        dst_ref=target,
        send_sem=send,
        recv_sem=recv,
        device_id={"grp": device},
        device_id_type=MESH,
    )


def to_rep(source, target, send, recv, device):
    return pltpu.make_async_remote_copy(
        src_ref=source,
        dst_ref=target,
        send_sem=send,
        recv_sem=recv,
        device_id={"rep": device},
        device_id_type=MESH,
    )


def arrived(ref, sem):
    pltpu.make_async_copy(ref, ref, sem).wait()


def dot(a, b):
    return jnp.dot(a, b, preferred_element_type=F32)


def dot_nt(a, b):
    return lax.dot_general(a, b, (((1,), (1,)), ((), ())), preferred_element_type=F32)


def dot_tn(a, b):
    return lax.dot_general(a, b, (((0,), (0,)), ((), ())), preferred_element_type=F32)


class Gather:
    def __init__(self, owners, buf, send, recv):
        self.owners, self.chips = owners, owners // 2
        self.me = lax.axis_index("grp")
        self.place, self.core = self.me // 2, self.me % 2
        self.buf, self.send, self.recv = buf, send, recv

    def copies(self, block, source=None):
        src = self.buf.at[block] if source is None else source
        at = block // 2
        ways = (
            ((at <= self.place) & (self.place < self.chips - 1), self.me + 2),
            ((at >= self.place) & (self.place > 0), self.me - 2),
            (None, self.me + 1 - 2 * self.core),
        )
        return [
            (
                when,
                to_grp(src, self.buf.at[block], self.send.at[way, at], self.recv.at[block], device),
            )
            for way, (when, device) in enumerate(ways)
        ]

    def forward(self, block, source=None):
        for when, copy in self.copies(block, source):
            if when is None:
                copy.start()
            else:
                pl.when(when)(copy.start)

    def step(self, k):
        block = 2 * nearest(self.place, k, self.chips) + self.core
        arrived(self.buf.at[block], self.recv.at[block])
        self.forward(block)

    def sibling(self, k):
        block = 2 * nearest(self.place, k, self.chips) + 1 - self.core
        arrived(self.buf.at[block], self.recv.at[block])

    def finish(self):
        def one(at, _):
            for when, copy in self.copies(2 * at + self.core):
                if when is None:
                    copy.wait_send()
                else:
                    pl.when(when)(copy.wait_send)
            return 0

        lax.fori_loop(0, self.chips, one, 0)

    @staticmethod
    def scratch(owners):
        return [
            pltpu.SemaphoreType.DMA((3, owners // 2)),
            pltpu.SemaphoreType.DMA((owners,)),
        ]


class Reshard:
    def __init__(self, owners, reps, buf, sems):
        self.owners, self.reps = owners, reps
        self.me, self.rep = lax.axis_index("grp"), lax.axis_index("rep")
        self.buf = buf
        self.send1, self.recv1, self.send2, self.recv2 = sems

    def start(self, pieces):
        for source, columns in pieces(self.me):
            pltpu.make_async_copy(
                source, self.buf.at[self.me, self.rep, :, columns], self.recv1.at[self.me]
            ).start()

        def one(ahead, _):
            device = lax.rem(self.me + ahead, self.owners)
            for source, columns in pieces(device):
                to_grp(
                    source,
                    self.buf.at[self.me, self.rep, :, columns],
                    self.send1.at[device],
                    self.recv1.at[self.me],
                    device,
                ).start()
            return 0

        lax.fori_loop(1, self.owners, one, 0)

    def relay(self):
        def one(ahead, _):
            owner = lax.rem(self.me + ahead, self.owners)
            part = self.buf.at[owner, self.rep]
            arrived(part, self.recv1.at[owner])
            for other in range(1, self.reps):
                to_rep(
                    part,
                    part,
                    self.send2.at[other],
                    self.recv2.at[other],
                    lax.rem(self.rep + other, self.reps),
                ).start()
            return 0

        lax.fori_loop(0, self.owners, one, 0)

    def wait(self):
        for other in range(1, self.reps):
            source = lax.rem(self.rep + self.reps - other, self.reps)
            arrived(self.buf.at[:, source], self.recv2.at[other])

    def finish(self):
        def one(ahead, _):
            device = lax.rem(self.me + ahead, self.owners)
            arrived(self.buf.at[device, self.rep], self.send1.at[device])
            return 0

        lax.fori_loop(1, self.owners, one, 0)
        for other in range(1, self.reps):
            arrived(self.buf.at[:, self.rep], self.send2.at[other])

    @staticmethod
    def scratch(owners, reps):
        return [
            pltpu.SemaphoreType.DMA((owners,)),
            pltpu.SemaphoreType.DMA((owners,)),
            pltpu.SemaphoreType.DMA((reps,)),
            pltpu.SemaphoreType.DMA((reps,)),
        ]


def head_norm(values):
    scale = lax.rsqrt(jnp.mean(values * values, axis=-1, keepdims=True) + norm_epsilon)
    return values * scale, scale


def turn(values, cosine, sine):
    return values * cosine + pltpu.roll(values, HEAD_SIZE // 2, 1) * sine


def turn_back(values, cosine, sine):
    return values * cosine - pltpu.roll(values, HEAD_SIZE // 2, 1) * sine


def first_kernel(
    owners,
    reps,
    heads,
    kv_heads,
    sharers,
    tokens_ref,
    weight_ref,
    small_ref,
    cosine_ref,
    sine_ref,
    input_out,
    query_out,
    gate_out,
    key_out,
    value_out,
    query_rot_out,
    key_rot_out,
    columns_out,
    small_out,
    buf,
    weight_buf,
    small_send,
    small_recv,
    local_sem,
    out_sem,
    g_send,
    g_recv,
    *r_sems,
):
    me, rep = lax.axis_index("grp"), lax.axis_index("rep")
    rows, width = tokens_ref.shape
    shard = weight_ref.shape[0]
    share = shard // reps
    q_cols, kv_cols = heads * HEAD_SIZE, kv_heads * HEAD_SIZE
    all_q = QUERY_HEADS * HEAD_SIZE
    all_kv = KEY_VALUE_HEADS * HEAD_SIZE
    gather = Gather(owners, buf, g_send, g_recv)
    reshard = Reshard(owners, reps, weight_buf, r_sems)
    my_rows = pl.ds(pl.multiple_of(rep * share, share), share)

    def pieces(owner):
        out = []
        at = 0
        for base, cols, step in (
            (0, q_cols, owner),
            (all_q, q_cols, owner),
            (2 * all_q, kv_cols, owner // sharers),
            (2 * all_q + all_kv, kv_cols, owner // sharers),
        ):
            first = pl.multiple_of(base + step * cols, HEAD_SIZE)
            out.append((weight_ref.at[my_rows, pl.ds(first, cols)], pl.ds(at, cols)))
            at += cols
        return out

    own = pltpu.make_async_copy(tokens_ref, buf.at[me], local_sem)
    own.start()
    small_out[me] = small_ref[...]
    meet(owners, reps)
    reshard.start(pieces)

    def small_copy(device, index):
        return to_grp(
            small_ref, small_out.at[me], small_send.at[index], small_recv.at[index], device
        )

    for ahead in range(1, owners):
        small_copy(lax.rem(me + ahead, owners), ahead).start()
    gather.forward(me, tokens_ref)
    reshard.relay()
    for ahead in range(1, owners):
        source = lax.rem(me + owners - ahead, owners)
        arrived(small_out.at[source], small_recv.at[ahead])
    own.wait()
    middle = (gather.place > 0) & (gather.place < gather.chips - 1)
    early = jnp.where(middle, gather.chips, gather.chips - 1)

    def step(k, _):
        gather.step(k)
        return 0

    lax.fori_loop(1, early, step, 0)
    reshard.wait()
    columns_copy = pltpu.make_async_copy(weight_buf, columns_out, out_sem)
    columns_copy.start()

    gain = jnp.concatenate([small_out[e][:, :shard] for e in range(owners)], axis=1)
    heads_gain = small_out[0][:, 2 * shard :]
    for e in range(1, owners):
        heads_gain = heads_gain + small_out[e][:, 2 * shard :]
    gain_query = heads_gain[:, :HEAD_SIZE]
    gain_key = heads_gain[:, HEAD_SIZE:]
    total_cols = 2 * q_cols + 2 * kv_cols
    weight = weight_buf.reshape(width, total_cols)

    def block(k, _):
        @pl.when(k >= early)
        def _():
            gather.step(k)

        def core(which, _):
            mine = which == 0

            @pl.when(which == 1)
            def _():
                gather.sibling(k)

            at = 2 * nearest(gather.place, k, gather.chips) + jnp.where(
                mine, gather.core, 1 - gather.core
            )
            values = buf[at].astype(F32)
            normed, _unused = head_norm(values)
            entry = (normed * gain).astype(BF16)
            input_out[at] = entry
            projected = dot(entry, weight[...])
            cosine, sine = cosine_ref[at], sine_ref[at]
            for h in range(heads):
                span = slice(h * HEAD_SIZE, (h + 1) * HEAD_SIZE)
                raw = projected[:, span]
                query_out[at, :, span] = raw
                query_rot_out[at, :, span] = turn(
                    head_norm(raw)[0] * gain_query, cosine, sine
                ).astype(BF16)
            gate_out[at] = projected[:, q_cols : 2 * q_cols]
            for h in range(kv_heads):
                span = slice(h * HEAD_SIZE, (h + 1) * HEAD_SIZE)
                raw = projected[:, 2 * q_cols + h * HEAD_SIZE : 2 * q_cols + (h + 1) * HEAD_SIZE]
                key_out[at, :, span] = raw
                key_rot_out[at, :, span] = turn(
                    head_norm(raw)[0] * gain_key, cosine, sine
                ).astype(BF16)
            value_out[at] = projected[:, 2 * q_cols + kv_cols :].astype(BF16)
            return 0

        lax.fori_loop(0, 2, core, 0)
        return 0

    lax.fori_loop(0, gather.chips, block, 0)
    columns_copy.wait()
    gather.finish()
    reshard.finish()
    for ahead in range(1, owners):
        small_copy(lax.rem(me + ahead, owners), ahead).wait_send()


def vmem():
    return pl.BlockSpec(memory_space=pltpu.VMEM)


def anywhere():
    return pl.BlockSpec(memory_space=pl.ANY)


def first(owners, reps, heads, kv_heads, sharers, tokens, w_qkvg, small, cosine, sine):
    rows, width = tokens.shape
    shard = w_qkvg.shape[0]
    q_cols, kv_cols = heads * HEAD_SIZE, kv_heads * HEAD_SIZE
    cols = 2 * q_cols + 2 * kv_cols
    shape = jax.ShapeDtypeStruct
    outs = (
        shape((owners, rows, width), BF16),
        shape((owners, rows, q_cols), F32),
        shape((owners, rows, q_cols), F32),
        shape((owners, rows, kv_cols), F32),
        shape((owners, rows, kv_cols), BF16),
        shape((owners, rows, q_cols), BF16),
        shape((owners, rows, kv_cols), BF16),
        shape((owners, reps, shard // reps, cols), BF16),
        shape((owners,) + small.shape, F32),
    )
    flops = 2 * owners * rows * width * cols
    return pl.pallas_call(
        functools.partial(first_kernel, owners, reps, heads, kv_heads, sharers),
        out_shape=outs,
        in_specs=[anywhere(), anywhere(), vmem(), vmem(), vmem()],
        out_specs=(vmem(),) * 7 + (anywhere(), vmem()),
        scratch_shapes=[
            pltpu.VMEM((owners, rows, width), BF16),
            pltpu.VMEM((owners, reps, shard // reps, cols), BF16),
            pltpu.SemaphoreType.DMA((owners,)),
            pltpu.SemaphoreType.DMA((owners,)),
            pltpu.SemaphoreType.DMA,
            pltpu.SemaphoreType.DMA,
        ]
        + Gather.scratch(owners)
        + Reshard.scratch(owners, reps),
        compiler_params=pltpu.CompilerParams(
            collective_id=0, has_side_effects=True, vmem_limit_bytes=60 * 2**20
        ),
        cost_estimate=pl.CostEstimate(
            flops=flops, bytes_accessed=40 * 2**20, transcendentals=0
        ),
        name="first",
    )(tokens, w_qkvg, small, cosine, sine)


def positions_of(block_ids):
    offsets = jnp.arange(BLOCK_TOKENS, dtype=jnp.int32)
    return (block_ids[:, :, None] * BLOCK_TOKENS + offsets[None, None, :]).reshape(
        block_ids.shape[0], -1
    )


def to_columns(piece):
    reps = lax.axis_size("rep")
    rows, owners, columns = piece.shape
    share = rows // reps
    mine = lax.dynamic_slice_in_dim(piece, lax.axis_index("rep") * share, share, 0)
    swapped = lax.all_to_all(mine, "grp", 1, 0, tiled=True)
    swapped = swapped.reshape(owners, share, columns)
    whole = lax.all_gather(swapped, "rep", axis=1, tiled=True)
    return whole.reshape(owners * rows, columns)


def to_rows(gradient):
    reps = lax.axis_size("rep")
    owners = lax.axis_size("grp")
    rows = gradient.shape[0] // owners
    shaped = gradient.reshape(owners, reps, rows // reps, -1)
    shaped = jnp.swapaxes(shaped, 0, 1).reshape(gradient.shape)
    share = lax.psum_scatter(shaped, "rep", scatter_dimension=0, tiled=True)
    share = share.reshape(owners, rows // reps, -1)
    swapped = lax.all_to_all(share, "grp", 0, 0, tiled=True)
    return lax.all_gather(jnp.swapaxes(swapped, 0, 1), "rep", axis=0, tiled=True)


def sum_rep(gradient):
    share = lax.psum_scatter(gradient, "rep", scatter_dimension=0, tiled=True)
    return lax.all_gather(share, "rep", axis=0, tiled=True)


def body(
    tokens,
    block_map,
    w_qkvg,
    w_out,
    w_in,
    w_down,
    norm_attn,
    norm_query,
    norm_key,
    norm_mlp,
    cotangent,
):
    owners = lax.axis_size("grp")
    me = lax.axis_index("grp")
    heads = QUERY_HEADS // owners
    sharers = max(1, owners // KEY_VALUE_HEADS)
    kv_heads = KEY_VALUE_HEADS * sharers // owners
    per_kv = heads // kv_heads
    q_cols = heads * HEAD_SIZE
    kv_cols = kv_heads * HEAD_SIZE
    rows_here, width = tokens.shape
    shard = w_qkvg.shape[0]
    block_rows = 2 * BLOCK_TOKENS
    seq_len = owners * block_rows
    all_q = QUERY_HEADS * HEAD_SIZE
    all_kv = KEY_VALUE_HEADS * HEAD_SIZE
    hidden_units = w_down.shape[0]

    in_pieces = jnp.swapaxes(w_in.reshape(shard, 2, owners, hidden_units), 1, 2).reshape(
        shard, owners, 2 * hidden_units
    )
    reps = lax.axis_size("rep")
    head_part = norm_query.shape[0]
    spread = jnp.zeros((2, HEAD_SIZE), jnp.float32)
    spread = lax.dynamic_update_slice(
        spread, jnp.stack([norm_query, norm_key]).astype(jnp.float32), (0, me * head_part)
    )
    small = jnp.concatenate(
        [norm_attn.astype(jnp.float32), norm_mlp.astype(jnp.float32), spread.reshape(-1)]
    )[None]
    in_cols = to_columns(in_pieces)
    cotangent_all = lax.all_gather(cotangent, "grp", axis=0, tiled=True)

    positions = positions_of(block_map)
    cosine, sine = rotary_tables(positions)
    sine = sine * jnp.where(jnp.arange(HEAD_SIZE) < HEAD_SIZE // 2, -1.0, 1.0)

    def by_block(table):
        shaped = table.reshape(GROUP_SEQUENCES, owners, block_rows, HEAD_SIZE)
        return jnp.swapaxes(shaped, 0, 1).reshape(owners, rows_here, HEAD_SIZE)

    (
        attn_input,
        query_raw,
        gate_raw,
        key_raw,
        value_rows,
        query_rot,
        key_rot,
        qkvg_cols,
        small_all,
    ) = first(
        owners,
        reps,
        heads,
        kv_heads,
        sharers,
        tokens,
        w_qkvg,
        small,
        by_block(cosine),
        by_block(sine),
    )
    cosine = cosine[:, None]
    sine = sine[:, None]
    small_all = small_all[:, 0]
    gain_attn = small_all[:, :shard].reshape(-1)
    gain_mlp = small_all[:, shard : 2 * shard].reshape(-1)
    spread = jnp.sum(small_all[:, 2 * shard :], axis=0)
    gain_query = spread[:HEAD_SIZE]
    gain_key = spread[HEAD_SIZE:]
    attn_input = attn_input.reshape(-1, width)
    gate_raw = gate_raw.reshape(-1, q_cols)
    qkvg_cols = qkvg_cols.reshape(width, -1)

    def to_heads(values):
        count = values.shape[-1] // HEAD_SIZE
        shaped = values.reshape(owners, GROUP_SEQUENCES, block_rows, count, HEAD_SIZE)
        return shaped.transpose(1, 3, 0, 2, 4).reshape(
            GROUP_SEQUENCES, count, seq_len, HEAD_SIZE
        )

    def from_heads(values):
        count = values.shape[1]
        shaped = values.reshape(GROUP_SEQUENCES, count, owners, block_rows, HEAD_SIZE)
        return shaped.transpose(2, 0, 3, 1, 4).reshape(-1, count * HEAD_SIZE)

    query_heads = to_heads(query_raw)
    key_heads = to_heads(key_raw)
    value_heads = to_heads(value_rows)
    query_scale = row_scale(query_heads)
    query_normed = query_heads * query_scale
    key_scale = row_scale(key_heads)
    key_normed = key_heads * key_scale

    query_rot = to_heads(query_rot).reshape(
        GROUP_SEQUENCES, kv_heads, per_kv, seq_len, HEAD_SIZE
    )
    key_rot = to_heads(key_rot)
    scores = jnp.einsum(
        "shgqd,shkd->shgqk", query_rot, key_rot, preferred_element_type=jnp.float32
    ) * HEAD_SIZE ** (-0.5)
    allowed = (positions[:, None, :] <= positions[:, :, None])[:, None, None]
    scores = jnp.where(allowed, scores, masked_value)
    top_score = jnp.max(scores, axis=-1, keepdims=True)
    exp_scores = jnp.exp(scores - top_score)
    exp_total = jnp.sum(exp_scores, axis=-1, keepdims=True)
    exact = exp_scores / exp_total
    probability = exact.astype(jnp.bfloat16)
    attended = jnp.einsum(
        "shgqk,shkd->shgqd", probability, value_heads, preferred_element_type=jnp.float32
    ).reshape(GROUP_SEQUENCES, heads, seq_len, HEAD_SIZE)
    attended = from_heads(attended)
    gate_sig = jax.nn.sigmoid(gate_raw)
    attn_out = (attended * gate_sig).astype(jnp.bfloat16)

    def scatter_sum(terms):
        return lax.psum_scatter(
            terms.astype(jnp.bfloat16), "grp", scatter_dimension=0, tiled=True
        ).astype(jnp.float32)

    branch = scatter_sum(jnp.dot(attn_out, w_out, preferred_element_type=jnp.float32))
    hidden = tokens.astype(jnp.float32) + branch
    scale_second = row_scale(hidden)
    normed_second = hidden * scale_second
    mlp_input = lax.all_gather(
        (normed_second * gain_mlp).astype(jnp.bfloat16), "grp", axis=0, tiled=True
    )
    gate_up = jnp.dot(mlp_input, in_cols, preferred_element_type=jnp.float32)
    gate_value = gate_up[:, :hidden_units]
    up_value = gate_up[:, hidden_units:]
    gate_sigmoid = jax.nn.sigmoid(gate_value)
    activated = (gate_value * gate_sigmoid * up_value).astype(jnp.bfloat16)
    grad_activated = jnp.dot(cotangent_all, w_down.T, preferred_element_type=jnp.float32)
    grad_gate = (
        grad_activated * up_value * gate_sigmoid * (1.0 + gate_value * (1.0 - gate_sigmoid))
    ).astype(jnp.bfloat16)
    grad_up = (grad_activated * gate_value * gate_sigmoid).astype(jnp.bfloat16)
    grad_gate_up = jnp.concatenate([grad_gate, grad_up], axis=1)
    grad_mlp_input = scatter_sum(
        jnp.dot(grad_gate_up, in_cols.T, preferred_element_type=jnp.float32)
    )
    mlp_out = scatter_sum(jnp.dot(activated, w_down, preferred_element_type=jnp.float32))
    output = (hidden + mlp_out).astype(jnp.bfloat16)
    term_in = jnp.dot(mlp_input.T, grad_gate_up, preferred_element_type=jnp.float32)
    term_down = jnp.dot(activated.T, cotangent_all, preferred_element_type=jnp.float32)
    grad_hidden_norm, gain_rows_mlp = norm_back(
        grad_mlp_input, normed_second, scale_second, gain_mlp
    )
    grad_hidden = cotangent.astype(jnp.float32) + grad_hidden_norm
    grad_branch = lax.all_gather(
        grad_hidden.astype(jnp.bfloat16), "grp", axis=0, tiled=True
    )
    shard_down = sum_rep(term_down.astype(jnp.bfloat16)).astype(jnp.float32)
    rows_in = to_rows(term_in.astype(jnp.bfloat16)).astype(jnp.float32)
    shard_in = jnp.swapaxes(rows_in.reshape(shard, owners, 2, hidden_units), 1, 2).reshape(
        w_in.shape
    )
    grad_attn_out = jnp.dot(grad_branch, w_out.T, preferred_element_type=jnp.float32)
    attended_gradient = (grad_attn_out * gate_sig).astype(jnp.bfloat16)
    grad_gate_raw = (grad_attn_out * attended * gate_sig * (1.0 - gate_sig)).astype(jnp.bfloat16)
    term_out = jnp.dot(attn_out.T, grad_branch, preferred_element_type=jnp.float32)
    shard_out = sum_rep(term_out.astype(jnp.bfloat16)).astype(jnp.float32)
    head_gradient = to_heads(attended_gradient).reshape(query_rot.shape)
    grad_value = jnp.einsum(
        "shgqk,shgqd->shkd", probability, head_gradient, preferred_element_type=jnp.float32
    )
    grad_probs = jnp.einsum(
        "shgqd,shkd->shgqk", head_gradient, value_heads, preferred_element_type=jnp.float32
    )
    inner_sum = jnp.sum(exact * grad_probs, axis=-1, keepdims=True)
    grad_scores = (exact * (grad_probs - inner_sum)).astype(jnp.bfloat16)
    grad_query = jnp.einsum(
        "shgqk,shkd->shgqd", grad_scores, key_rot, preferred_element_type=jnp.float32
    ).reshape(query_heads.shape) * HEAD_SIZE ** (-0.5)
    grad_key = jnp.einsum(
        "shgqk,shgqd->shkd", grad_scores, query_rot, preferred_element_type=jnp.float32
    ) * HEAD_SIZE ** (-0.5)
    grad_query_raw, gain_rows_query = norm_back(
        unrotate_pairs(grad_query, cosine, sine), query_normed, query_scale, gain_query
    )
    grad_key_raw, gain_rows_key = norm_back(
        unrotate_pairs(grad_key, cosine, sine), key_normed, key_scale, gain_key
    )
    grad_projected = jnp.concatenate(
        [
            from_heads(grad_query_raw.astype(jnp.bfloat16)),
            grad_gate_raw,
            from_heads(grad_key_raw.astype(jnp.bfloat16)),
            from_heads(grad_value.astype(jnp.bfloat16)),
        ],
        axis=-1,
    )
    term_qkvg = jnp.dot(attn_input.T, grad_projected, preferred_element_type=jnp.float32)
    grad_attn_input = scatter_sum(
        jnp.dot(grad_projected, qkvg_cols.T, preferred_element_type=jnp.float32)
    )
    own_tokens = tokens.astype(jnp.float32)
    own_scale = row_scale(own_tokens)
    grad_residual_norm, gain_rows_attn = norm_back(
        grad_attn_input, own_tokens * own_scale, own_scale, gain_attn
    )
    grad_tokens = (grad_hidden + grad_residual_norm).astype(jnp.bfloat16)
    rows_qkvg = to_rows(term_qkvg.astype(jnp.bfloat16)).astype(jnp.float32)

    def joined(part, repeat):
        if repeat > 1:
            part = part.reshape(shard, owners // repeat, repeat, -1).sum(2)
        return part.reshape(shard, -1)

    shard_qkvg = jnp.concatenate(
        [
            joined(rows_qkvg[:, :, :q_cols], 1),
            joined(rows_qkvg[:, :, q_cols : 2 * q_cols], 1),
            joined(rows_qkvg[:, :, 2 * q_cols : 2 * q_cols + kv_cols], sharers),
            joined(rows_qkvg[:, :, 2 * q_cols + kv_cols :], sharers),
        ],
        axis=1,
    )
    gains = lax.psum(
        jnp.concatenate(
            [
                jnp.sum(gain_rows_attn, axis=0),
                jnp.sum(gain_rows_mlp, axis=0),
                jnp.sum(gain_rows_query, axis=(0, 1, 2)),
                jnp.sum(gain_rows_key, axis=(0, 1, 2)),
            ]
        ),
        ("rep", "grp"),
    )
    return (
        output,
        grad_tokens,
        shard_qkvg,
        shard_out,
        shard_in,
        shard_down,
        lax.dynamic_slice_in_dim(gains, me * shard, shard),
        lax.dynamic_slice_in_dim(gains, 2 * width + me * head_part, head_part),
        lax.dynamic_slice_in_dim(gains, 2 * width + HEAD_SIZE + me * head_part, head_part),
        lax.dynamic_slice_in_dim(gains, width + me * shard, shard),
    )


def solution(mesh):
    placed = (
        P(("rep", "grp"), None),
        P("rep", None),
        P("grp", None),
        P("grp", None),
        P("grp", None, None),
        P("grp", None),
        P("grp"),
        P("grp"),
        P("grp"),
        P("grp"),
        P(("rep", "grp"), None),
    )
    return jax.shard_map(
        body,
        mesh=mesh,
        in_specs=placed,
        out_specs=(
            P(("rep", "grp"), None),
            P(("rep", "grp"), None),
            P("grp", None),
            P("grp", None),
            P("grp", None, None),
            P("grp", None),
            P("grp"),
            P("grp"),
            P("grp"),
            P("grp"),
        ),
        check_vma=False,
    )
```

```python
import functools

import jax
import jax.numpy as jnp
from jax import lax
from jax.experimental import pallas as pl
from jax.experimental.pallas import tpu as pltpu
from jax.sharding import PartitionSpec as P

QUERY_HEADS = 16
KEY_VALUE_HEADS = 8
HEAD_SIZE = 128
BLOCK_TOKENS = 64
GROUP_SEQUENCES = 2


norm_epsilon = 1e-06
rotary_base = 1000000.0
masked_value = -1e30


def row_scale(values):
    return lax.rsqrt(jnp.mean(values * values, axis=-1, keepdims=True) + norm_epsilon)


def rotate_half(values):
    middle = values.shape[-1] // 2
    return jnp.concatenate([-values[..., middle:], values[..., :middle]], axis=-1)


def rotary_tables(positions):
    exponent = jnp.arange(HEAD_SIZE // 2, dtype=jnp.float32) * (2.0 / HEAD_SIZE)
    inverse = jnp.power(jnp.float32(rotary_base), -exponent)
    angles = positions.astype(jnp.float32)[..., None] * inverse
    angles = jnp.concatenate([angles, angles], axis=-1)
    return (jnp.cos(angles), jnp.sin(angles))


def unrotate_pairs(gradient, cosine_lookup, sine_lookup):
    return gradient * cosine_lookup - jnp.roll(gradient, HEAD_SIZE // 2, -1) * sine_lookup


def norm_back(grad_out, normed, scale_rows, gain_vector):
    weighted = grad_out * gain_vector
    grad_in = scale_rows * (weighted - normed * jnp.mean(weighted * normed, axis=-1, keepdims=True))
    return (grad_in, grad_out * normed)


MESH = pl.DeviceIdType.MESH
F32 = jnp.float32
BF16 = jnp.bfloat16


def nearest(place, step, chips):
    low = jnp.minimum(place, chips - 1 - place)
    near = (step + 1) // 2
    both = jnp.where(step % 2 == 1, place - near, place + near)
    past = step - low
    rest = jnp.where(place > chips - 1 - place, place - past, place + past)
    return jnp.where(step <= 2 * low, both, rest)


def meet(owners, reps):
    barrier = pltpu.get_barrier_semaphore()
    me, rep = lax.axis_index("grp"), lax.axis_index("rep")
    for ahead in range(1, owners):
        pl.semaphore_signal(
            barrier, 1, device_id={"grp": lax.rem(me + ahead, owners)}, device_id_type=MESH
        )
    for ahead in range(1, reps):
        pl.semaphore_signal(
            barrier, 1, device_id={"rep": lax.rem(rep + ahead, reps)}, device_id_type=MESH
        )
    pl.semaphore_wait(barrier, owners + reps - 2)


def to_grp(source, target, send, recv, device):
    return pltpu.make_async_remote_copy(
        src_ref=source,
        dst_ref=target,
        send_sem=send,
        recv_sem=recv,
        device_id={"grp": device},
        device_id_type=MESH,
    )


def to_rep(source, target, send, recv, device):
    return pltpu.make_async_remote_copy(
        src_ref=source,
        dst_ref=target,
        send_sem=send,
        recv_sem=recv,
        device_id={"rep": device},
        device_id_type=MESH,
    )


def arrived(ref, sem):
    pltpu.make_async_copy(ref, ref, sem).wait()


def dot(a, b):
    return jnp.dot(a, b, preferred_element_type=F32)


def dot_nt(a, b):
    return lax.dot_general(a, b, (((1,), (1,)), ((), ())), preferred_element_type=F32)


def dot_tn(a, b):
    return lax.dot_general(a, b, (((0,), (0,)), ((), ())), preferred_element_type=F32)


class Gather:
    def __init__(self, owners, buf, send, recv, half=0):
        self.owners, self.chips = owners, owners // 2
        self.me = lax.axis_index("grp")
        self.place, self.core = self.me // 2, self.me % 2
        self.buf, self.send, self.recv, self.half = buf, send, recv, half

    def of(self, block):
        return self.buf.at[block, self.half] if len(self.buf.shape) == 4 else self.buf.at[block]

    def sent(self, way, at):
        return self.send.at[self.half, way, at]

    def got(self, block):
        return self.recv.at[self.half, block]

    def copies(self, block, source=None):
        src = self.of(block) if source is None else source
        at = block // 2
        ways = (
            ((at <= self.place) & (self.place < self.chips - 1), self.me + 2),
            ((at >= self.place) & (self.place > 0), self.me - 2),
            (None, self.me + 1 - 2 * self.core),
        )
        return [
            (
                when,
                to_grp(src, self.of(block), self.sent(way, at), self.got(block), device),
            )
            for way, (when, device) in enumerate(ways)
        ]

    def forward(self, block, source=None):
        for when, copy in self.copies(block, source):
            if when is None:
                copy.start()
            else:
                pl.when(when)(copy.start)

    def step(self, k):
        block = 2 * nearest(self.place, k, self.chips) + self.core
        arrived(self.of(block), self.got(block))
        self.forward(block)

    def sibling(self, k):
        block = 2 * nearest(self.place, k, self.chips) + 1 - self.core
        arrived(self.of(block), self.got(block))

    def finish(self):
        def one(at, _):
            for when, copy in self.copies(2 * at + self.core):
                if when is None:
                    copy.wait_send()
                else:
                    pl.when(when)(copy.wait_send)
            return 0

        lax.fori_loop(0, self.chips, one, 0)

    @staticmethod
    def scratch(owners, halves=1):
        return [
            pltpu.SemaphoreType.DMA((halves, 3, owners // 2)),
            pltpu.SemaphoreType.DMA((halves, owners)),
        ]


class Reshard:
    def __init__(self, owners, reps, buf, sems):
        self.owners, self.reps = owners, reps
        self.me, self.rep = lax.axis_index("grp"), lax.axis_index("rep")
        self.buf = buf
        self.send1, self.recv1, self.send2, self.recv2 = sems

    def start(self, pieces):
        for source, columns in pieces(self.me):
            pltpu.make_async_copy(
                source, self.buf.at[self.me, self.rep, :, columns], self.recv1.at[self.me]
            ).start()

        def one(ahead, _):
            device = lax.rem(self.me + ahead, self.owners)
            for source, columns in pieces(device):
                to_grp(
                    source,
                    self.buf.at[self.me, self.rep, :, columns],
                    self.send1.at[device],
                    self.recv1.at[self.me],
                    device,
                ).start()
            return 0

        lax.fori_loop(1, self.owners, one, 0)

    def relay(self):
        def one(ahead, _):
            owner = lax.rem(self.me + ahead, self.owners)
            part = self.buf.at[owner, self.rep]
            arrived(part, self.recv1.at[owner])
            for other in range(1, self.reps):
                to_rep(
                    part,
                    part,
                    self.send2.at[other],
                    self.recv2.at[other],
                    lax.rem(self.rep + other, self.reps),
                ).start()
            return 0

        lax.fori_loop(0, self.owners, one, 0)

    def wait(self):
        for other in range(1, self.reps):
            source = lax.rem(self.rep + self.reps - other, self.reps)
            arrived(self.buf.at[:, source], self.recv2.at[other])

    def finish(self):
        def one(ahead, _):
            device = lax.rem(self.me + ahead, self.owners)
            arrived(self.buf.at[device, self.rep], self.send1.at[device])
            return 0

        lax.fori_loop(1, self.owners, one, 0)
        for other in range(1, self.reps):
            arrived(self.buf.at[:, self.rep], self.send2.at[other])

    @staticmethod
    def scratch(owners, reps):
        return [
            pltpu.SemaphoreType.DMA((owners,)),
            pltpu.SemaphoreType.DMA((owners,)),
            pltpu.SemaphoreType.DMA((reps,)),
            pltpu.SemaphoreType.DMA((reps,)),
        ]


def head_norm(values):
    scale = lax.rsqrt(jnp.mean(values * values, axis=-1, keepdims=True) + norm_epsilon)
    return values * scale, scale


def turn(values, cosine, sine):
    return values * cosine + pltpu.roll(values, HEAD_SIZE // 2, 1) * sine


def turn_back(values, cosine, sine):
    return values * cosine - pltpu.roll(values, HEAD_SIZE // 2, 1) * sine


def first_kernel(
    owners,
    reps,
    heads,
    kv_heads,
    sharers,
    tokens_ref,
    weight_ref,
    small_ref,
    cosine_ref,
    sine_ref,
    input_out,
    query_out,
    gate_out,
    key_out,
    value_out,
    query_rot_out,
    key_rot_out,
    columns_out,
    small_out,
    buf,
    weight_buf,
    small_send,
    small_recv,
    local_sem,
    out_sem,
    g_send,
    g_recv,
    *r_sems,
):
    me, rep = lax.axis_index("grp"), lax.axis_index("rep")
    rows, width = tokens_ref.shape
    shard = weight_ref.shape[0]
    share = shard // reps
    q_cols, kv_cols = heads * HEAD_SIZE, kv_heads * HEAD_SIZE
    all_q = QUERY_HEADS * HEAD_SIZE
    all_kv = KEY_VALUE_HEADS * HEAD_SIZE
    gather = Gather(owners, buf, g_send, g_recv)
    reshard = Reshard(owners, reps, weight_buf, r_sems)
    my_rows = pl.ds(pl.multiple_of(rep * share, share), share)

    def pieces(owner):
        out = []
        at = 0
        for base, cols, step in (
            (0, q_cols, owner),
            (all_q, q_cols, owner),
            (2 * all_q, kv_cols, owner // sharers),
            (2 * all_q + all_kv, kv_cols, owner // sharers),
        ):
            first = pl.multiple_of(base + step * cols, HEAD_SIZE)
            out.append((weight_ref.at[my_rows, pl.ds(first, cols)], pl.ds(at, cols)))
            at += cols
        return out

    own = pltpu.make_async_copy(tokens_ref, buf.at[me], local_sem)
    own.start()
    small_out[me] = small_ref[...]
    meet(owners, reps)
    reshard.start(pieces)

    def small_copy(device, index):
        return to_grp(
            small_ref, small_out.at[me], small_send.at[index], small_recv.at[index], device
        )

    for ahead in range(1, owners):
        small_copy(lax.rem(me + ahead, owners), ahead).start()
    gather.forward(me, tokens_ref)
    reshard.relay()
    for ahead in range(1, owners):
        source = lax.rem(me + owners - ahead, owners)
        arrived(small_out.at[source], small_recv.at[ahead])
    own.wait()
    middle = (gather.place > 0) & (gather.place < gather.chips - 1)
    early = jnp.where(middle, gather.chips, gather.chips - 1)

    def step(k, _):
        gather.step(k)
        return 0

    lax.fori_loop(1, early, step, 0)
    reshard.wait()
    columns_copy = pltpu.make_async_copy(weight_buf, columns_out, out_sem)
    columns_copy.start()

    gain = jnp.concatenate([small_out[e][:, :shard] for e in range(owners)], axis=1)
    heads_gain = small_out[0][:, 2 * shard :]
    for e in range(1, owners):
        heads_gain = heads_gain + small_out[e][:, 2 * shard :]
    gain_query = heads_gain[:, :HEAD_SIZE]
    gain_key = heads_gain[:, HEAD_SIZE:]
    total_cols = 2 * q_cols + 2 * kv_cols
    weight = weight_buf.reshape(width, total_cols)

    def block(k, _):
        @pl.when(k >= early)
        def _():
            gather.step(k)

        def core(which, _):
            mine = which == 0

            @pl.when(which == 1)
            def _():
                gather.sibling(k)

            at = 2 * nearest(gather.place, k, gather.chips) + jnp.where(
                mine, gather.core, 1 - gather.core
            )
            values = buf[at].astype(F32)
            normed, _unused = head_norm(values)
            entry = (normed * gain).astype(BF16)
            input_out[at] = entry
            projected = dot(entry, weight[...])
            cosine, sine = cosine_ref[at], sine_ref[at]
            for h in range(heads):
                span = slice(h * HEAD_SIZE, (h + 1) * HEAD_SIZE)
                raw = projected[:, span]
                query_out[at, :, span] = raw
                query_rot_out[at, :, span] = turn(
                    head_norm(raw)[0] * gain_query, cosine, sine
                ).astype(BF16)
            gate_out[at] = projected[:, q_cols : 2 * q_cols]
            for h in range(kv_heads):
                span = slice(h * HEAD_SIZE, (h + 1) * HEAD_SIZE)
                raw = projected[:, 2 * q_cols + h * HEAD_SIZE : 2 * q_cols + (h + 1) * HEAD_SIZE]
                key_out[at, :, span] = raw
                key_rot_out[at, :, span] = turn(
                    head_norm(raw)[0] * gain_key, cosine, sine
                ).astype(BF16)
            value_out[at] = projected[:, 2 * q_cols + kv_cols :].astype(BF16)
            return 0

        lax.fori_loop(0, 2, core, 0)
        return 0

    lax.fori_loop(0, gather.chips, block, 0)
    columns_copy.wait()
    gather.finish()
    reshard.finish()
    for ahead in range(1, owners):
        small_copy(lax.rem(me + ahead, owners), ahead).wait_send()


def vmem():
    return pl.BlockSpec(memory_space=pltpu.VMEM)


def anywhere():
    return pl.BlockSpec(memory_space=pl.ANY)


def first(owners, reps, heads, kv_heads, sharers, tokens, w_qkvg, small, cosine, sine):
    rows, width = tokens.shape
    shard = w_qkvg.shape[0]
    q_cols, kv_cols = heads * HEAD_SIZE, kv_heads * HEAD_SIZE
    cols = 2 * q_cols + 2 * kv_cols
    shape = jax.ShapeDtypeStruct
    outs = (
        shape((owners, rows, width), BF16),
        shape((owners, rows, q_cols), F32),
        shape((owners, rows, q_cols), F32),
        shape((owners, rows, kv_cols), F32),
        shape((owners, rows, kv_cols), BF16),
        shape((owners, rows, q_cols), BF16),
        shape((owners, rows, kv_cols), BF16),
        shape((owners, reps, shard // reps, cols), BF16),
        shape((owners,) + small.shape, F32),
    )
    flops = 2 * owners * rows * width * cols
    return pl.pallas_call(
        functools.partial(first_kernel, owners, reps, heads, kv_heads, sharers),
        out_shape=outs,
        in_specs=[anywhere(), anywhere(), vmem(), vmem(), vmem()],
        out_specs=(vmem(),) * 7 + (anywhere(), vmem()),
        scratch_shapes=[
            pltpu.VMEM((owners, rows, width), BF16),
            pltpu.VMEM((owners, reps, shard // reps, cols), BF16),
            pltpu.SemaphoreType.DMA((owners,)),
            pltpu.SemaphoreType.DMA((owners,)),
            pltpu.SemaphoreType.DMA,
            pltpu.SemaphoreType.DMA,
        ]
        + Gather.scratch(owners)
        + Reshard.scratch(owners, reps),
        compiler_params=pltpu.CompilerParams(
            collective_id=0, has_side_effects=True, vmem_limit_bytes=60 * 2**20
        ),
        cost_estimate=pl.CostEstimate(
            flops=flops, bytes_accessed=40 * 2**20, transcendentals=0
        ),
        name="first",
    )(tokens, w_qkvg, small, cosine, sine)


def by_distance(place, step, chips):
    return nearest(place, chips - 1 - step, chips)


class Scatter:
    def __init__(self, owners, bufs, sems, order, parts, half=0):
        self.owners, self.chips = owners, owners // 2
        self.me = lax.axis_index("grp")
        self.place, self.core = self.me // 2, self.me % 2
        self.stage, self.near, self.line, self.both = bufs
        self.acc = self.both.at[self.core]
        self.near_send, self.near_recv, self.line_send, self.line_recv = sems
        self.order, self.parts, self.half = order, parts, half
        self.part = self.both.shape[1] // parts

    def at(self, k):
        return self.order(self.place, k, self.chips)

    def near_copy(self, k):
        at = self.at(k)
        return to_grp(
            self.stage.at[self.half, k % 2],
            self.near.at[self.half, at],
            self.near_send.at[self.half, k % 2],
            self.near_recv.at[self.half, at],
            self.me + 1 - 2 * self.core,
        )

    def rows(self, s):
        return pl.ds(s * self.part, self.part)

    def line_copy(self, at, s):
        target = self.place + jnp.where(at > self.place, 1, -1)
        slot = jnp.where((target == at) & (at < self.place), self.chips, at)
        return to_grp(
            self.near.at[self.half, at, self.rows(s)],
            self.line.at[self.half, slot, self.rows(s)],
            self.line_send.at[self.half, at, s],
            self.line_recv.at[self.half, slot, s],
            2 * target + self.core,
        )

    def prepare(self, k, term):
        @pl.when(k >= 2)
        def _():
            self.near_copy(k - 2).wait_send()

        self.both[...] = term(self.at(k)).reshape(self.both.shape)
        self.stage[self.half, k % 2] = self.both[1 - self.core].astype(BF16)
        self.near_copy(k).start()

    def add(self, slot, s):
        part = self.line.at[self.half, slot, self.rows(s)]
        arrived(part, self.line_recv.at[self.half, slot, s])
        self.acc[self.rows(s)] += part[...].astype(F32)

    def combine(self, k):
        at = self.at(k)
        arrived(self.near.at[self.half, at], self.near_recv.at[self.half, at])
        self.acc[...] += self.near[self.half, at].astype(F32)
        below = self.place > 0
        above = self.place < self.chips - 1

        def one(s, _):
            @pl.when(((at >= self.place) & below) | ((at < self.place) & above))
            def _():
                self.add(at, s)

            @pl.when((at == self.place) & above)
            def _():
                self.add(self.chips, s)

            @pl.when(at != self.place)
            def _():
                self.near[self.half, at, self.rows(s)] = self.acc[self.rows(s)].astype(BF16)
                self.line_copy(at, s).start()

            return 0

        lax.fori_loop(0, self.parts, one, 0)

    def finish(self):
        self.near_copy(self.chips - 2).wait_send()
        self.near_copy(self.chips - 1).wait_send()

        def one(at, _):
            @pl.when(at != self.place)
            def _():
                for s in range(self.parts):
                    self.line_copy(at, s).wait_send()

            return 0

        lax.fori_loop(0, self.chips, one, 0)

    @staticmethod
    def scratch(owners, rows, width, parts, halves=1):
        chips = owners // 2
        rows //= halves
        return [
            pltpu.VMEM((halves, 2, rows, width), BF16),
            pltpu.VMEM((halves, chips, rows, width), BF16),
            pltpu.VMEM((halves, chips + 1, rows, width), BF16),
            pltpu.VMEM((2, rows, width), F32),
            pltpu.SemaphoreType.DMA((halves, 2)),
            pltpu.SemaphoreType.DMA((halves, chips)),
            pltpu.SemaphoreType.DMA((halves, chips, parts)),
            pltpu.SemaphoreType.DMA((halves, chips + 1, parts)),
        ]


PARTS = 4


class RepSum:
    def __init__(self, owners, reps, units, along, held, came, result, sems):
        self.owners, self.reps, self.units, self.along = owners, reps, units, along
        self.me, self.rep = lax.axis_index("grp"), lax.axis_index("rep")
        self.bits = reps.bit_length() - 1
        self.held, self.came, self.result = held, came, result
        self.down_send, self.down_recv, self.own_send, self.own_recv, self.up_send, self.up_recv = sems

    def weight(self, t, j):
        which = (t + j) % self.bits
        return sum(jnp.where(which == b, 1 << b, 0) for b in range(self.bits))

    @staticmethod
    def flip(index, weight):
        return index + weight * (1 - 2 * ((index // weight) % 2))

    def spread(self, index, t, bits):
        out = [index]
        for j in bits:
            out += [self.flip(i, self.weight(t, j)) for i in out]
        return out

    def unit(self, t):
        return lax.rem(self.me + t, self.owners) if self.along else t

    def source(self, t):
        return lax.rem(self.me + self.owners - t, self.owners) if self.along else t

    def downs(self, t, j):
        u = self.unit(t)
        first_index = sum(1 << (self.bits - 1 - i) for i in range(j))
        partner = self.flip(self.rep, self.weight(t, j))
        return [
            to_rep(
                self.held.at[u, s],
                self.came.at[u, first_index + c],
                self.down_send.at[u, first_index + c],
                self.down_recv.at[u, first_index + c],
                partner,
            )
            for c, s in enumerate(self.spread(partner, t, range(j + 1, self.bits)))
        ]

    def ups(self, t, j):
        e = self.source(t)
        held = self.spread(self.rep, t, range(self.bits - 1, self.bits - 1 - j, -1))
        partner = self.flip(self.rep, self.weight(t, self.bits - 1 - j))
        return [
            to_rep(
                self.result.at[e, s],
                self.result.at[e, s],
                self.up_send.at[e, (1 << j) - 1 + c],
                self.up_recv.at[e, s],
                partner,
            )
            for c, s in enumerate(held)
        ]

    def deliver(self, t, do_local, do_remote):
        u = self.unit(t)
        source = self.held.at[u, self.rep]
        slot = self.me if self.along else u
        local = pltpu.make_async_copy(source, self.result.at[slot, self.rep], self.own_recv.at[slot])
        if not self.along:
            do_local(local)
            return
        remote = to_grp(
            source,
            self.result.at[slot, self.rep],
            self.own_send.at[u],
            self.own_recv.at[slot],
            u,
        )
        pl.when(u == self.me)(lambda: do_local(local))
        pl.when(u != self.me)(lambda: do_remote(remote))

    def tick(self, t, term):
        def phase(lag):
            return (t >= lag) & (t < self.units + lag)

        @pl.when(phase(0))
        def _():
            u = self.unit(t)
            self.held[u] = term(t, u).astype(BF16).reshape(self.held.shape[1:])
            for copy in self.downs(t, 0):
                copy.start()

        for j in range(1, self.bits + 1):

            @pl.when(phase(j))
            def _(j=j, t=t - j):
                u = self.unit(t)
                first_index = sum(1 << (self.bits - 1 - i) for i in range(j - 1))
                for c, s in enumerate(self.spread(self.rep, t, range(j, self.bits))):
                    part = self.came.at[u, first_index + c]
                    arrived(part, self.down_recv.at[u, first_index + c])
                    self.held[u, s] = (self.held[u, s].astype(F32) + part[...].astype(F32)).astype(
                        BF16
                    )
                if j < self.bits:
                    for copy in self.downs(t, j):
                        copy.start()
                else:
                    self.deliver(t, lambda c: c.start(), lambda c: c.start())

        for j in range(self.bits + 1):

            @pl.when(phase(self.bits + 1 + j))
            def _(j=j, t=t - self.bits - 1 - j):
                e = self.source(t)
                if j == 0:
                    arrived(self.result.at[e, self.rep], self.own_recv.at[e])
                else:
                    bit = self.bits - j
                    held = self.spread(self.rep, t, range(self.bits - 1, bit, -1))
                    for s in held:
                        s = self.flip(s, self.weight(t, bit))
                        arrived(self.result.at[e, s], self.up_recv.at[e, s])
                if j < self.bits:
                    for copy in self.ups(t, j):
                        copy.start()

    def ticks(self):
        return self.units + 2 * self.bits + 1

    def finish(self):
        def one(t, _):
            for j in range(self.bits):
                for copy in self.downs(t, j) + self.ups(t, j):
                    copy.wait_send()
            self.deliver(t, lambda c: None, lambda c: c.wait_send())
            return 0

        lax.fori_loop(0, self.units, one, 0)

    @staticmethod
    def scratch(reps, units, share, cols):
        dma = pltpu.SemaphoreType.DMA
        return [
            pltpu.VMEM((units, reps, share, cols), BF16),
            pltpu.VMEM((units, reps - 1, share, cols), BF16),
            dma((units, reps - 1)),
            dma((units, reps - 1)),
            dma((units,)),
            dma((units,)),
            dma((units, reps - 1)),
            dma((units, reps)),
        ]


def interleave(gather, scatter, term, ready=None, then=None):
    chips = gather.chips
    middle = (gather.place > 0) & (gather.place < chips - 1)

    def stage(k, _):
        if ready is not None:
            ready(k)
        scatter.prepare(k, term)

        @pl.when(middle & (2 * k + 1 < chips))
        def _():
            gather.step(2 * k + 1)

        @pl.when(middle & (2 * k + 2 < chips))
        def _():
            gather.step(2 * k + 2)

        scatter.combine(k)

        @pl.when((~middle) & (k + 1 < chips))
        def _():
            gather.step(k + 1)

        then(k)
        return 0

    lax.fori_loop(0, chips, stage, 0)


def attention_kernel(
    owners,
    reps,
    heads,
    kv_heads,
    tokens_ref,
    query_ref,
    key_ref,
    value_ref,
    gate_ref,
    position_col_ref,
    position_row_ref,
    out_ref,
    gain_ref,
    cotangent_ref,
    in_pieces_ref,
    attn_out,
    hidden_out,
    entry_out,
    cotangent_out,
    columns_out,
    local_sem,
    *rest,
):
    me, rep = lax.axis_index("grp"), lax.axis_index("rep")
    scatter = Scatter(owners, rest[:4], rest[4:8], by_distance, PARTS)
    gather = Gather(owners, cotangent_out, *rest[8:10])
    reshard = Reshard(owners, reps, columns_out, rest[10:14])
    share = in_pieces_ref.shape[1] // reps
    cols = in_pieces_ref.shape[2]
    my_rows = pl.ds(pl.multiple_of(rep * share, share), share)

    def pieces(owner):
        return [(in_pieces_ref.at[owner, my_rows], pl.ds(0, cols))]

    own = pltpu.make_async_copy(cotangent_ref, cotangent_out.at[me], local_sem)
    own.start()
    meet(owners, reps)
    gather.forward(me, cotangent_ref)
    reshard.start(pieces)
    per_kv = heads // kv_heads
    block_rows = 2 * BLOCK_TOKENS

    def attend(at):
        for s in range(GROUP_SEQUENCES):
            rows = slice(s * block_rows, (s + 1) * block_rows)
            allowed = position_row_ref[s] <= position_col_ref[at, rows]
            allowed = jnp.concatenate([allowed] * per_kv, axis=0)
            for kv in range(kv_heads):
                span = slice(kv * HEAD_SIZE, (kv + 1) * HEAD_SIZE)
                spans = [
                    slice(h * HEAD_SIZE, (h + 1) * HEAD_SIZE)
                    for h in range(kv * per_kv, (kv + 1) * per_kv)
                ]
                query = jnp.concatenate([query_ref[at, rows, h] for h in spans], axis=0)
                keys = key_ref[:, rows, span].reshape(-1, HEAD_SIZE)
                values = value_ref[:, rows, span].reshape(-1, HEAD_SIZE)
                scores = dot_nt(query, keys) * HEAD_SIZE ** (-0.5)
                scores = jnp.where(allowed, scores, masked_value)
                exps = jnp.exp(scores - jnp.max(scores, axis=-1, keepdims=True))
                probability = exps / jnp.sum(exps, axis=-1, keepdims=True)
                attended = dot(probability.astype(BF16), values)
                for i, h in enumerate(spans):
                    gated = attended[i * block_rows : (i + 1) * block_rows] * jax.nn.sigmoid(
                        gate_ref[at, rows, h]
                    )
                    attn_out[at, rows, h] = gated.astype(BF16)

    def ready(k):
        at = scatter.at(k)

        def one(core, _):
            attend(2 * at + core)
            return 0

        lax.fori_loop(0, 2, one, 0)

    def term(at):
        both = attn_out[pl.ds(2 * at, 2)]
        return dot(both.reshape(-1, both.shape[-1]), out_ref[...])

    def then(k):
        pl.when(k == 0)(reshard.relay)
        gather.sibling(k)

    interleave(gather, scatter, term, ready, then)
    hidden = tokens_ref[...].astype(F32) + scatter.acc[...]
    hidden_out[...] = hidden
    entry_out[...] = (head_norm(hidden)[0] * gain_ref[...]).astype(BF16)
    own.wait()
    reshard.wait()
    gather.finish()
    scatter.finish()
    reshard.finish()


def attention(
    owners,
    reps,
    heads,
    kv_heads,
    tokens,
    query_rot,
    key_rot,
    value_rows,
    gate_raw,
    position_col,
    position_row,
    w_out,
    gain_mlp,
    cotangent,
    in_pieces,
):
    rows, width = tokens.shape
    shape = jax.ShapeDtypeStruct
    share = in_pieces.shape[1] // reps
    outs = (
        shape(query_rot.shape, BF16),
        shape((rows, width), F32),
        shape((rows, width), BF16),
        shape((owners, rows, width), BF16),
        shape((owners, reps, share, in_pieces.shape[2]), BF16),
    )
    return pl.pallas_call(
        functools.partial(attention_kernel, owners, reps, heads, kv_heads),
        out_shape=outs,
        in_specs=[vmem()] * 9 + [anywhere()] * 2,
        out_specs=(vmem(),) * 3 + (anywhere(),) * 2,
        scratch_shapes=[pltpu.SemaphoreType.DMA]
        + Scatter.scratch(owners, rows, width, PARTS)
        + Gather.scratch(owners)
        + Reshard.scratch(owners, reps),
        compiler_params=pltpu.CompilerParams(
            collective_id=1, has_side_effects=True, vmem_limit_bytes=60 * 2**20
        ),
        cost_estimate=pl.CostEstimate(
            flops=4 * owners * rows * width * query_rot.shape[2],
            bytes_accessed=40 * 2**20,
            transcendentals=0,
        ),
        name="attention",
    )(
        tokens,
        query_rot,
        key_rot,
        value_rows,
        gate_raw,
        position_col,
        position_row,
        w_out,
        gain_mlp,
        cotangent,
        in_pieces,
    )


def mlp_kernel(
    owners,
    reps,
    entry_ref,
    cotangent_all_ref,
    in_ref,
    down_ref,
    hidden_ref,
    cotangent_ref,
    gain_ref,
    entry_all,
    activated_out,
    grads_out,
    grad_hidden_out,
    grad_branch_out,
    gain_out,
    entry_buf,
    cotangent_buf,
    activated_buf,
    grad_entry_buf,
    local_sem,
    load_sem,
    store_sem,
    *rest,
):
    me = lax.axis_index("grp")
    chips = owners // 2
    halves = GROUP_SEQUENCES
    gathers = [Gather(owners, entry_all, *rest[8:10], half) for half in range(halves)]
    scatters = [
        Scatter(owners, rest[:4], rest[4:8], by_distance, HALF_PARTS, half)
        for half in range(halves)
    ]
    units = down_ref.shape[0]
    place = gathers[0].place
    own = pltpu.make_async_copy(entry_ref, entry_all.at[me], local_sem)
    own.start()
    meet(owners, reps)
    gathers[0].forward(me, entry_ref.at[0])
    own.wait()

    def compute(k, half, first):
        gather = gathers[half]
        pair = pl.ds(2 * nearest(place, k, chips), 2)
        cotangent_load = pltpu.make_async_copy(
            cotangent_all_ref.at[pair, half], cotangent_buf, load_sem.at[1]
        )
        cotangent_load.start()
        gather.sibling(k)
        entry_load = pltpu.make_async_copy(entry_all.at[pair, half], entry_buf, load_sem.at[0])
        entry_load.start()
        cotangent_load.wait()
        both = cotangent_buf.shape[0] * cotangent_buf.shape[1]
        grad_activated = dot_nt(cotangent_buf[...].reshape(both, -1), down_ref[...])
        entry_load.wait()
        gate_up = dot(entry_buf[...].reshape(both, -1), in_ref[...])
        gate, up = gate_up[:, :units], gate_up[:, units:]
        sig = jax.nn.sigmoid(gate)
        silu = gate * sig
        store = pltpu.make_async_copy(activated_buf, activated_out.at[pair, half], store_sem)

        @pl.when(jnp.logical_not(first))
        def _():
            store.wait()

        activated_buf[...] = (silu * up).astype(BF16).reshape(activated_buf.shape)
        store.start()
        shape = activated_buf.shape
        grads_out[pair, half, :, :units] = (
            (grad_activated * up * sig * (1.0 + gate * (1.0 - sig))).astype(BF16).reshape(shape)
        )
        grads_out[pair, half, :, units:] = (grad_activated * silu).astype(BF16).reshape(shape)

    def term_of(half):
        def term(at):
            both = grads_out[pl.ds(2 * at, 2), half]
            return dot_nt(both.reshape(-1, both.shape[-1]), in_ref[...])

        return term

    def front(k, _):
        @pl.when(k > 0)
        def _():
            gathers[0].step(k)

        compute(k, 0, k == 0)
        return 0

    lax.fori_loop(0, chips, front, 0)
    for half in range(1, halves):
        gathers[half].forward(me, entry_ref.at[half])
        interleave(
            gathers[half],
            scatters[half - 1],
            term_of(half - 1),
            then=lambda k, half=half: compute(k, half, k < 0),
        )
        grad_entry_buf[half - 1] = scatters[half - 1].acc[...]

    def back(k, _):
        scatters[-1].prepare(k, term_of(halves - 1))
        scatters[-1].combine(k)
        return 0

    lax.fori_loop(0, chips, back, 0)
    grad_entry_buf[halves - 1] = scatters[-1].acc[...]
    hidden = hidden_ref[...]
    normed, scale = head_norm(hidden)
    grad_entry = grad_entry_buf[...].reshape(hidden.shape)
    gain_out[...] = jnp.sum(grad_entry * normed, axis=0, keepdims=True)
    weighted = grad_entry * gain_ref[...]
    grad_hidden = cotangent_ref[...].astype(F32) + scale * (
        weighted - normed * jnp.mean(weighted * normed, axis=-1, keepdims=True)
    )
    grad_hidden_out[...] = grad_hidden
    grad_branch_out[...] = grad_hidden.astype(BF16)
    pltpu.make_async_copy(
        activated_buf, activated_out.at[pl.ds(0, 2), 0], store_sem
    ).wait()
    for half in range(halves):
        gathers[half].finish()
        scatters[half].finish()


HALF_PARTS = 2


def mlp(owners, reps, entry, cotangent_all, in_cols, w_down, hidden, cotangent, gain_mlp):
    rows, width = entry.shape
    units = w_down.shape[0]
    halves = GROUP_SEQUENCES
    half_rows = rows // halves
    shape = jax.ShapeDtypeStruct
    outs = (
        shape((owners, halves, half_rows, width), BF16),
        shape((owners, halves, half_rows, units), BF16),
        shape((owners, halves, half_rows, 2 * units), BF16),
        shape((rows, width), F32),
        shape((rows, width), BF16),
        shape((1, width), F32),
    )
    return pl.pallas_call(
        functools.partial(mlp_kernel, owners, reps),
        out_shape=outs,
        in_specs=[anywhere()] * 2 + [vmem()] * 5,
        out_specs=(anywhere(),) * 2 + (vmem(),) * 4,
        scratch_shapes=[
            pltpu.VMEM((2, half_rows, width), BF16),
            pltpu.VMEM((2, half_rows, width), BF16),
            pltpu.VMEM((2, half_rows, units), BF16),
            pltpu.VMEM((halves, half_rows, width), F32),
            pltpu.SemaphoreType.DMA,
            pltpu.SemaphoreType.DMA((2,)),
            pltpu.SemaphoreType.DMA,
        ]
        + Scatter.scratch(owners, rows, width, HALF_PARTS, halves)
        + Gather.scratch(owners, halves),
        compiler_params=pltpu.CompilerParams(
            collective_id=2, has_side_effects=True, vmem_limit_bytes=60 * 2**20
        ),
        cost_estimate=pl.CostEstimate(
            flops=10 * owners * rows * width * units,
            bytes_accessed=40 * 2**20,
            transcendentals=0,
        ),
        name="mlp",
    )(
        entry.reshape(halves, half_rows, width),
        cotangent_all.reshape(owners, halves, half_rows, width),
        in_cols,
        w_down,
        hidden,
        cotangent,
        gain_mlp,
    )


def unturned_norm_back(grad, raw, gain, cosine, sine):
    back = turn_back(grad, cosine, sine)
    normed, scale = head_norm(raw)
    weighted = back * gain
    grad_raw = scale * (weighted - normed * jnp.mean(weighted * normed, axis=-1, keepdims=True))
    return grad_raw, jnp.sum(back * normed, axis=0, keepdims=True)


def backward_kernel(
    owners,
    reps,
    heads,
    kv_heads,
    branch_ref,
    activated_ref,
    down_ref,
    out_ref,
    hidden_ref,
    query_ref,
    query_rot_ref,
    gate_ref,
    key_ref,
    key_rot_ref,
    value_ref,
    position_col_ref,
    position_row_ref,
    cosine_ref,
    sine_ref,
    heads_gain_ref,
    attn_out_ref,
    branch_all,
    output_out,
    grads_out,
    gain_out,
    out_term,
    branch_buf,
    key_sum,
    value_sum,
    local_sem,
    load_sem,
    *rest,
):
    me = lax.axis_index("grp")
    chips = owners // 2
    scatter = Scatter(owners, rest[:4], rest[4:8], by_distance, PARTS)
    gather = Gather(owners, branch_all, *rest[8:10])
    own = pltpu.make_async_copy(branch_ref, branch_all.at[me], local_sem)
    own.start()
    meet(owners, reps)
    gather.forward(me, branch_ref)
    own.wait()
    key_sum[...] = jnp.zeros_like(key_sum)
    value_sum[...] = jnp.zeros_like(value_sum)
    gain_out[...] = jnp.zeros_like(gain_out)
    out_term[...] = jnp.zeros_like(out_term)
    per_kv = heads // kv_heads
    q_cols, kv_cols = heads * HEAD_SIZE, kv_heads * HEAD_SIZE
    block_rows = 2 * BLOCK_TOKENS
    root = HEAD_SIZE ** (-0.5)
    gain_query = heads_gain_ref[:, :HEAD_SIZE]
    gain_key = heads_gain_ref[:, HEAD_SIZE:]

    def block(at):
        load = pltpu.make_async_copy(branch_all.at[at], branch_buf, load_sem)
        load.start()
        load.wait()
        grad_attn_out = dot_nt(branch_buf[...], out_ref[...])
        out_term[...] += dot_tn(attn_out_ref[at], branch_buf[...])
        for s in range(GROUP_SEQUENCES):
            rows = slice(s * block_rows, (s + 1) * block_rows)
            cosine, sine = cosine_ref[at, rows], sine_ref[at, rows]
            allowed = position_row_ref[s] <= position_col_ref[at, rows]
            allowed = jnp.concatenate([allowed] * per_kv, axis=0)
            for kv in range(kv_heads):
                span = slice(kv * HEAD_SIZE, (kv + 1) * HEAD_SIZE)
                spans = [
                    slice(h * HEAD_SIZE, (h + 1) * HEAD_SIZE)
                    for h in range(kv * per_kv, (kv + 1) * per_kv)
                ]
                query = jnp.concatenate([query_rot_ref[at, rows, h] for h in spans], axis=0)
                keys = key_rot_ref[:, rows, span].reshape(-1, HEAD_SIZE)
                values = value_ref[:, rows, span].reshape(-1, HEAD_SIZE)
                scores = dot_nt(query, keys) * root
                scores = jnp.where(allowed, scores, masked_value)
                exps = jnp.exp(scores - jnp.max(scores, axis=-1, keepdims=True))
                exact = exps / jnp.sum(exps, axis=-1, keepdims=True)
                low = exact.astype(BF16)
                attended = dot(low, values)
                inputs = []
                for i, h in enumerate(spans):
                    grad = grad_attn_out[rows, h]
                    sig = jax.nn.sigmoid(gate_ref[at, rows, h])
                    inputs.append((grad * sig).astype(BF16))
                    gated = slice(q_cols + h.start, q_cols + h.stop)
                    grads_out[at, rows, gated] = (
                        grad
                        * attended[i * block_rows : (i + 1) * block_rows]
                        * sig
                        * (1.0 - sig)
                    ).astype(BF16)
                grad_attended = jnp.concatenate(inputs, axis=0)
                grad_probs = dot_nt(grad_attended, values)
                inner = jnp.sum(exact * grad_probs, axis=-1, keepdims=True)
                grad_scores = (exact * (grad_probs - inner)).astype(BF16)
                grad_query = dot(grad_scores, keys) * root
                key_sum[s, kv] += dot_tn(grad_scores, query)
                value_sum[s, kv] += dot_tn(low, grad_attended)
                for i, h in enumerate(spans):
                    grad_raw, gain_sum = unturned_norm_back(
                        grad_query[i * block_rows : (i + 1) * block_rows],
                        query_ref[at, rows, h],
                        gain_query,
                        cosine,
                        sine,
                    )
                    grads_out[at, rows, h] = grad_raw.astype(BF16)
                    gain_out[:, :HEAD_SIZE] += gain_sum

    def term(at):
        both = activated_ref[pl.ds(2 * at, 2)]
        return dot(both.reshape(-1, both.shape[-1]), down_ref[...])

    def then(k):
        def one(which, _):
            @pl.when(which == 1)
            def _():
                gather.sibling(k)

            block(
                2 * nearest(gather.place, k, chips)
                + jnp.where(which == 0, gather.core, 1 - gather.core)
            )
            return 0

        lax.fori_loop(0, 2, one, 0)

    interleave(gather, scatter, term, then=then)
    output_out[...] = (hidden_ref[...] + scatter.acc[...]).astype(BF16)

    def keys(at, _):
        for s in range(GROUP_SEQUENCES):
            rows = slice(s * block_rows, (s + 1) * block_rows)
            for kv in range(kv_heads):
                span = slice(kv * HEAD_SIZE, (kv + 1) * HEAD_SIZE)
                place = pl.ds(pl.multiple_of(at * block_rows, block_rows), block_rows)
                grad_raw, gain_sum = unturned_norm_back(
                    key_sum[s, kv, place] * root,
                    key_ref[at, rows, span],
                    gain_key,
                    cosine_ref[at, rows],
                    sine_ref[at, rows],
                )
                first_col = 2 * q_cols + kv * HEAD_SIZE
                grads_out[at, rows, first_col : first_col + HEAD_SIZE] = grad_raw.astype(BF16)
                first_col += kv_cols
                grads_out[at, rows, first_col : first_col + HEAD_SIZE] = value_sum[
                    s, kv, place
                ].astype(BF16)
                gain_out[:, HEAD_SIZE:] += gain_sum
        return 0

    lax.fori_loop(0, owners, keys, 0)
    gather.finish()
    scatter.finish()


def backward(
    owners,
    reps,
    heads,
    kv_heads,
    branch,
    activated,
    w_down,
    w_out,
    hidden,
    query_raw,
    query_rot,
    gate_raw,
    key_raw,
    key_rot,
    value_rows,
    position_col,
    position_row,
    cosine,
    sine,
    heads_gain,
    attn_out,
):
    rows, width = branch.shape
    cols = 2 * (heads + kv_heads) * HEAD_SIZE
    seq_len = position_row.shape[-1]
    shape = jax.ShapeDtypeStruct
    outs = (
        shape((owners, rows, width), BF16),
        shape((rows, width), BF16),
        shape((owners, rows, cols), BF16),
        shape((1, 2 * HEAD_SIZE), F32),
        shape(w_out.shape, F32),
    )
    return pl.pallas_call(
        functools.partial(backward_kernel, owners, reps, heads, kv_heads),
        out_shape=outs,
        in_specs=[anywhere()] + [vmem()] * 16,
        out_specs=(anywhere(),) + (vmem(),) * 4,
        scratch_shapes=[
            pltpu.VMEM((rows, width), BF16),
            pltpu.VMEM((GROUP_SEQUENCES, kv_heads, seq_len, HEAD_SIZE), F32),
            pltpu.VMEM((GROUP_SEQUENCES, kv_heads, seq_len, HEAD_SIZE), F32),
            pltpu.SemaphoreType.DMA,
            pltpu.SemaphoreType.DMA,
        ]
        + Scatter.scratch(owners, rows, width, PARTS)
        + Gather.scratch(owners),
        compiler_params=pltpu.CompilerParams(
            collective_id=3, has_side_effects=True, vmem_limit_bytes=60 * 2**20
        ),
        cost_estimate=pl.CostEstimate(
            flops=4 * owners * rows * width * cols,
            bytes_accessed=40 * 2**20,
            transcendentals=0,
        ),
        name="backward",
    )(
        branch,
        activated,
        w_down,
        w_out,
        hidden,
        query_raw,
        query_rot,
        gate_raw,
        key_raw,
        key_rot,
        value_rows,
        position_col,
        position_row,
        cosine,
        sine,
        heads_gain,
        attn_out,
    )


def column_loads(source_ref, buf, sem, shard):
    def load(slot, u):
        columns = pl.ds(pl.multiple_of(u * shard, shard), shard)
        return pltpu.make_async_copy(source_ref.at[:, :, columns], buf.at[slot], sem.at[slot])

    return load


def columns_term(total, load, buf, grads):
    def term(t, u):
        @pl.when(t + 1 < total.units)
        def _():
            load((t + 1) % 2, total.unit(t + 1)).start()

        load(t % 2, u).wait()
        entry = buf[t % 2]
        return dot_tn(entry.reshape(-1, entry.shape[-1]), grads())

    return term


def last_kernel(
    owners,
    reps,
    grads_ref,
    weight_ref,
    tokens_ref,
    grad_hidden_ref,
    gain_ref,
    out_term_ref,
    gain_mlp_ref,
    gain_heads_ref,
    entry_ref,
    grad_out,
    gains_out,
    weight_out,
    out_weight_out,
    entry_buf,
    gains_send,
    gains_came,
    gains_all,
    load_sem,
    g_send,
    g_recv,
    r_send,
    r_recv,
    *rest,
):
    me, rep = lax.axis_index("grp"), lax.axis_index("rep")
    chips = owners // 2
    scatter = Scatter(owners, rest[:4], rest[4:8], by_distance, PARTS)
    columns = RepSum(owners, reps, owners, True, rest[8], rest[9], weight_out, rest[10:16])
    rows = RepSum(owners, reps, 1, False, rest[16], rest[17], out_weight_out, rest[18:24])
    shard = entry_buf.shape[-1]
    load = column_loads(entry_ref, entry_buf, load_sem, shard)
    load(0, me).start()
    meet(owners, reps)

    def flat(ref):
        return ref[...].reshape(-1, ref.shape[-1])

    columns_of = columns_term(columns, load, entry_buf, lambda: flat(grads_ref))

    def rows_of(t, u):
        return out_term_ref[...]

    def tick(t):
        rows.tick(t, rows_of)
        columns.tick(t, columns_of)

    def term(at):
        both = grads_ref[pl.ds(2 * at, 2)]
        return dot_nt(both.reshape(-1, both.shape[-1]), weight_ref[...])

    def stage(k, _):
        scatter.prepare(k, term)
        tick(TICKS * k)
        scatter.combine(k)

        def one(t, _):
            tick(t)
            return 0

        lax.fori_loop(TICKS * k + 1, TICKS * (k + 1), one, 0)
        return 0

    lax.fori_loop(0, chips, stage, 0)
    grad = scatter.acc[...]
    normed, scale = head_norm(tokens_ref[...].astype(F32))
    gain_attn = jnp.sum(grad * normed, axis=0, keepdims=True)
    gain_mlp = gain_mlp_ref[...]
    for e in range(owners):
        span = slice(e * shard, (e + 1) * shard)
        gains_send[e] = jnp.concatenate(
            [gain_attn[:, span], gain_mlp[:, span], gain_heads_ref[...]], axis=1
        )

    def gains_copy(ahead):
        device = lax.rem(me + ahead, owners)
        return to_grp(
            gains_send.at[device],
            gains_came.at[me],
            g_send.at[ahead],
            g_recv.at[me],
            device,
        )

    def gains_up(ahead):
        return to_rep(
            gains_all.at[rep],
            gains_all.at[rep],
            r_send.at[ahead],
            r_recv.at[rep],
            lax.rem(rep + ahead, reps),
        )

    for ahead in range(1, owners):
        gains_copy(ahead).start()
    gains_came[me] = gains_send[me]
    weighted = grad * gain_ref[...]
    grad_out[...] = (
        grad_hidden_ref[...]
        + scale * (weighted - normed * jnp.mean(weighted * normed, axis=-1, keepdims=True))
    ).astype(BF16)
    for ahead in range(1, owners):
        source = lax.rem(me + ahead, owners)
        arrived(gains_came.at[source], g_recv.at[source])
    gains_all[rep] = jnp.sum(gains_came[...], axis=0)
    for ahead in range(1, reps):
        gains_up(ahead).start()

    def one(t, _):
        tick(t)
        return 0

    lax.fori_loop(TICKS * chips, max(columns.ticks(), rows.ticks()), one, 0)
    for ahead in range(1, reps):
        source = lax.rem(rep + ahead, reps)
        arrived(gains_all.at[source], r_recv.at[source])
    gains_out[...] = jnp.sum(gains_all[...], axis=0)
    for ahead in range(1, owners):
        gains_copy(ahead).wait_send()
    for ahead in range(1, reps):
        gains_up(ahead).wait_send()
    scatter.finish()
    columns.finish()
    rows.finish()


TICKS = 3


def last(
    owners,
    reps,
    grads,
    weight,
    tokens,
    grad_hidden,
    gain,
    out_term,
    gain_mlp,
    gain_heads,
    entry_all,
):
    rows, width = tokens.shape
    cols = grads.shape[2]
    shard = width // owners
    share = shard // reps
    small = 2 * shard + gain_heads.shape[1]
    shape = jax.ShapeDtypeStruct
    dma = pltpu.SemaphoreType.DMA
    return pl.pallas_call(
        functools.partial(last_kernel, owners, reps),
        out_shape=(
            shape((rows, width), BF16),
            shape((1, small), F32),
            shape((owners, reps, share, cols), BF16),
            shape((1, reps, share, width), BF16),
        ),
        in_specs=[vmem()] * 8 + [anywhere()],
        out_specs=(vmem(),) * 2 + (anywhere(),) * 2,
        scratch_shapes=[
            pltpu.VMEM((2, owners, rows, shard), BF16),
            pltpu.VMEM((owners, 1, small), F32),
            pltpu.VMEM((owners, 1, small), F32),
            pltpu.VMEM((reps, 1, small), F32),
            dma((2,)),
            dma((owners,)),
            dma((owners,)),
            dma((reps,)),
            dma((reps,)),
        ]
        + Scatter.scratch(owners, rows, width, PARTS)
        + RepSum.scratch(reps, owners, share, cols)
        + RepSum.scratch(reps, 1, share, width),
        compiler_params=pltpu.CompilerParams(
            collective_id=4, has_side_effects=True, vmem_limit_bytes=60 * 2**20
        ),
        cost_estimate=pl.CostEstimate(
            flops=4 * owners * rows * width * cols,
            bytes_accessed=40 * 2**20,
            transcendentals=0,
        ),
        name="last",
    )(
        grads,
        weight,
        tokens,
        grad_hidden,
        gain,
        out_term,
        gain_mlp,
        gain_heads,
        entry_all,
    )


def positions_of(block_ids):
    offsets = jnp.arange(BLOCK_TOKENS, dtype=jnp.int32)
    return (block_ids[:, :, None] * BLOCK_TOKENS + offsets[None, None, :]).reshape(
        block_ids.shape[0], -1
    )


def to_rows(gradient):
    reps = lax.axis_size("rep")
    owners = lax.axis_size("grp")
    rows = gradient.shape[0] // owners
    shaped = gradient.reshape(owners, reps, rows // reps, -1)
    shaped = jnp.swapaxes(shaped, 0, 1).reshape(gradient.shape)
    share = lax.psum_scatter(shaped, "rep", scatter_dimension=0, tiled=True)
    share = share.reshape(owners, rows // reps, -1)
    swapped = lax.all_to_all(share, "grp", 0, 0, tiled=True)
    return lax.all_gather(jnp.swapaxes(swapped, 0, 1), "rep", axis=0, tiled=True)


def sum_rep(gradient):
    share = lax.psum_scatter(gradient, "rep", scatter_dimension=0, tiled=True)
    return lax.all_gather(share, "rep", axis=0, tiled=True)


def body(
    tokens,
    block_map,
    w_qkvg,
    w_out,
    w_in,
    w_down,
    norm_attn,
    norm_query,
    norm_key,
    norm_mlp,
    cotangent,
):
    owners = lax.axis_size("grp")
    me = lax.axis_index("grp")
    heads = QUERY_HEADS // owners
    sharers = max(1, owners // KEY_VALUE_HEADS)
    kv_heads = KEY_VALUE_HEADS * sharers // owners
    per_kv = heads // kv_heads
    q_cols = heads * HEAD_SIZE
    kv_cols = kv_heads * HEAD_SIZE
    rows_here, width = tokens.shape
    shard = w_qkvg.shape[0]
    block_rows = 2 * BLOCK_TOKENS
    seq_len = owners * block_rows
    all_q = QUERY_HEADS * HEAD_SIZE
    all_kv = KEY_VALUE_HEADS * HEAD_SIZE
    hidden_units = w_down.shape[0]

    in_pieces = w_in.reshape(shard, 2, owners, hidden_units).transpose(2, 0, 1, 3)
    in_pieces = in_pieces.reshape(owners, shard, 2 * hidden_units)
    reps = lax.axis_size("rep")
    head_part = norm_query.shape[0]
    spread = jnp.zeros((2, HEAD_SIZE), jnp.float32)
    spread = lax.dynamic_update_slice(
        spread, jnp.stack([norm_query, norm_key]).astype(jnp.float32), (0, me * head_part)
    )
    small = jnp.concatenate(
        [norm_attn.astype(jnp.float32), norm_mlp.astype(jnp.float32), spread.reshape(-1)]
    )[None]

    positions = positions_of(block_map)
    cosine, sine = rotary_tables(positions)
    sine = sine * jnp.where(jnp.arange(HEAD_SIZE) < HEAD_SIZE // 2, -1.0, 1.0)

    def by_block(table):
        shaped = table.reshape(GROUP_SEQUENCES, owners, block_rows, HEAD_SIZE)
        return jnp.swapaxes(shaped, 0, 1).reshape(owners, rows_here, HEAD_SIZE)

    cosine = by_block(cosine)
    sine = by_block(sine)
    (
        attn_input,
        query_raw,
        gate_raw,
        key_raw,
        value_rows,
        query_rot,
        key_rot,
        qkvg_cols,
        small_all,
    ) = first(
        owners,
        reps,
        heads,
        kv_heads,
        sharers,
        tokens,
        w_qkvg,
        small,
        cosine,
        sine,
    )
    small_all = small_all[:, 0]
    gain_attn = small_all[:, :shard].reshape(-1)
    gain_mlp = small_all[:, shard : 2 * shard].reshape(-1)
    spread = jnp.sum(small_all[:, 2 * shard :], axis=0)
    position_blocks = jnp.swapaxes(
        positions.reshape(GROUP_SEQUENCES, owners, block_rows), 0, 1
    ).reshape(owners, rows_here, 1)
    attn_out, hidden, mlp_own, cotangent_all, in_cols = attention(
        owners,
        reps,
        heads,
        kv_heads,
        tokens,
        query_rot,
        key_rot,
        value_rows,
        gate_raw,
        position_blocks,
        positions[:, None, :],
        w_out,
        gain_mlp[None],
        cotangent,
        in_pieces,
    )
    in_cols = in_cols.reshape(width, -1)
    mlp_input, activated, grad_gate_up, grad_hidden, branch_own, gain_mlp_sum = mlp(
        owners, reps, mlp_own, cotangent_all, in_cols, w_down, hidden, cotangent, gain_mlp[None]
    )
    mlp_input = mlp_input.reshape(-1, width)
    grad_gate_up = grad_gate_up.reshape(-1, 2 * hidden_units)
    cotangent_all = cotangent_all.reshape(-1, width)
    _, output, grad_projected, gain_heads_sum, out_term = backward(
        owners,
        reps,
        heads,
        kv_heads,
        branch_own,
        activated.reshape(owners, rows_here, hidden_units),
        w_down,
        w_out,
        hidden,
        query_raw,
        query_rot,
        gate_raw,
        key_raw,
        key_rot,
        value_rows,
        position_blocks,
        positions[:, None, :],
        cosine,
        sine,
        spread[None],
        attn_out,
    )
    grad_tokens, gains, rows_qkvg, rows_out = last(
        owners,
        reps,
        grad_projected,
        qkvg_cols.reshape(width, -1),
        tokens,
        grad_hidden,
        gain_attn[None],
        out_term,
        gain_mlp_sum,
        gain_heads_sum,
        attn_input,
    )
    activated = activated.reshape(-1, hidden_units)
    term_in = jnp.dot(mlp_input.T, grad_gate_up, preferred_element_type=jnp.float32)
    term_down = jnp.dot(activated.T, cotangent_all, preferred_element_type=jnp.float32)
    shard_down = sum_rep(term_down.astype(jnp.bfloat16)).astype(jnp.float32)
    rows_in = to_rows(term_in.astype(jnp.bfloat16)).astype(jnp.float32)
    shard_in = jnp.swapaxes(rows_in.reshape(shard, owners, 2, hidden_units), 1, 2).reshape(
        w_in.shape
    )
    shard_out = rows_out.reshape(w_out.shape).astype(jnp.float32)
    rows_qkvg = rows_qkvg.reshape(owners, shard, -1).swapaxes(0, 1).astype(jnp.float32)

    def joined(part, repeat):
        if repeat > 1:
            part = part.reshape(shard, owners // repeat, repeat, -1).sum(2)
        return part.reshape(shard, -1)

    shard_qkvg = jnp.concatenate(
        [
            joined(rows_qkvg[:, :, :q_cols], 1),
            joined(rows_qkvg[:, :, q_cols : 2 * q_cols], 1),
            joined(rows_qkvg[:, :, 2 * q_cols : 2 * q_cols + kv_cols], sharers),
            joined(rows_qkvg[:, :, 2 * q_cols + kv_cols :], sharers),
        ],
        axis=1,
    )
    return (
        output,
        grad_tokens,
        shard_qkvg,
        shard_out,
        shard_in,
        shard_down,
        gains[0, :shard],
        lax.dynamic_slice_in_dim(gains[0], 2 * shard + me * head_part, head_part),
        lax.dynamic_slice_in_dim(gains[0], 2 * shard + HEAD_SIZE + me * head_part, head_part),
        gains[0, shard : 2 * shard],
    )


def solution(mesh):
    placed = (
        P(("rep", "grp"), None),
        P("rep", None),
        P("grp", None),
        P("grp", None),
        P("grp", None, None),
        P("grp", None),
        P("grp"),
        P("grp"),
        P("grp"),
        P("grp"),
        P(("rep", "grp"), None),
    )
    return jax.shard_map(
        body,
        mesh=mesh,
        in_specs=placed,
        out_specs=(
            P(("rep", "grp"), None),
            P(("rep", "grp"), None),
            P("grp", None),
            P("grp", None),
            P("grp", None, None),
            P("grp", None),
            P("grp"),
            P("grp"),
            P("grp"),
            P("grp"),
        ),
        check_vma=False,
    )
```

```python
import functools

import jax
import jax.numpy as jnp
from jax import lax
from jax.experimental import pallas as pl
from jax.experimental.pallas import tpu as pltpu
from jax.sharding import PartitionSpec as P

QUERY_HEADS = 16
KEY_VALUE_HEADS = 8
HEAD_SIZE = 128
BLOCK_TOKENS = 64
GROUP_SEQUENCES = 2


norm_epsilon = 1e-06
rotary_base = 1000000.0
masked_value = -1e30


def rotary_table(positions):
    exponent = jnp.arange(HEAD_SIZE // 2, dtype=jnp.float32) * (2.0 / HEAD_SIZE)
    inverse = jnp.power(jnp.float32(rotary_base), -exponent)
    angle = positions.astype(jnp.float32)[..., None] * inverse
    return jnp.concatenate([jnp.cos(angle), jnp.sin(angle)], axis=-1)


MESH = pl.DeviceIdType.MESH
F32 = jnp.float32
BF16 = jnp.bfloat16


def nearest(place, step, chips):
    low = jnp.minimum(place, chips - 1 - place)
    near = (step + 1) // 2
    both = jnp.where(step % 2 == 1, place - near, place + near)
    past = step - low
    rest = jnp.where(place > chips - 1 - place, place - past, place + past)
    return jnp.where(step <= 2 * low, both, rest)


def meet(owners, reps):
    barrier = pltpu.get_barrier_semaphore()
    me, rep = lax.axis_index("grp"), lax.axis_index("rep")
    for ahead in range(1, owners):
        pl.semaphore_signal(
            barrier, 1, device_id={"grp": lax.rem(me + ahead, owners)}, device_id_type=MESH
        )
    for ahead in range(1, reps):
        pl.semaphore_signal(
            barrier, 1, device_id={"rep": lax.rem(rep + ahead, reps)}, device_id_type=MESH
        )
    pl.semaphore_wait(barrier, owners + reps - 2)


def to_grp(source, target, send, recv, device):
    return pltpu.make_async_remote_copy(
        src_ref=source,
        dst_ref=target,
        send_sem=send,
        recv_sem=recv,
        device_id={"grp": device},
        device_id_type=MESH,
    )


def to_rep(source, target, send, recv, device):
    return pltpu.make_async_remote_copy(
        src_ref=source,
        dst_ref=target,
        send_sem=send,
        recv_sem=recv,
        device_id={"rep": device},
        device_id_type=MESH,
    )


def arrived(ref, sem):
    pltpu.make_async_copy(ref, ref, sem).wait()


def dot(a, b):
    return jnp.dot(a, b, preferred_element_type=F32)


def dot_nt(a, b):
    return lax.dot_general(a, b, (((1,), (1,)), ((), ())), preferred_element_type=F32)


def dot_tn(a, b):
    return lax.dot_general(a, b, (((0,), (0,)), ((), ())), preferred_element_type=F32)


class Gather:
    def __init__(self, owners, buf, send, recv, half=0):
        self.owners, self.chips = owners, owners // 2
        self.me = lax.axis_index("grp")
        self.place, self.core = self.me // 2, self.me % 2
        self.buf, self.send, self.recv, self.half = buf, send, recv, half

    def of(self, block):
        return self.buf.at[block, self.half] if len(self.buf.shape) == 4 else self.buf.at[block]

    def sent(self, way, at):
        return self.send.at[self.half, way, at]

    def got(self, block):
        return self.recv.at[self.half, block]

    def copies(self, block, source=None):
        src = self.of(block) if source is None else source
        at = block // 2
        ways = (
            ((at <= self.place) & (self.place < self.chips - 1), self.me + 2),
            ((at >= self.place) & (self.place > 0), self.me - 2),
            (None, self.me + 1 - 2 * self.core),
        )
        return [
            (
                when,
                to_grp(src, self.of(block), self.sent(way, at), self.got(block), device),
            )
            for way, (when, device) in enumerate(ways)
        ]

    def forward(self, block, source=None):
        for when, copy in self.copies(block, source):
            if when is None:
                copy.start()
            else:
                pl.when(when)(copy.start)

    def step(self, k):
        block = 2 * nearest(self.place, k, self.chips) + self.core
        arrived(self.of(block), self.got(block))
        self.forward(block)

    def sibling(self, k):
        block = 2 * nearest(self.place, k, self.chips) + 1 - self.core
        arrived(self.of(block), self.got(block))

    def finish(self):
        def one(at, _):
            for when, copy in self.copies(2 * at + self.core):
                if when is None:
                    copy.wait_send()
                else:
                    pl.when(when)(copy.wait_send)
            return 0

        lax.fori_loop(0, self.chips, one, 0)

    @staticmethod
    def scratch(owners, halves=1):
        return [
            pltpu.SemaphoreType.DMA((halves, 3, owners // 2)),
            pltpu.SemaphoreType.DMA((halves, owners)),
        ]


class Reshard:
    def __init__(self, owners, reps, buf, sems):
        self.owners, self.reps = owners, reps
        self.me, self.rep = lax.axis_index("grp"), lax.axis_index("rep")
        self.buf = buf
        self.send1, self.recv1, self.send2, self.recv2 = sems

    def start(self, pieces):
        for source, columns in pieces(self.me):
            pltpu.make_async_copy(
                source, self.buf.at[self.me, self.rep, :, columns], self.recv1.at[self.me]
            ).start()

        def one(ahead, _):
            device = lax.rem(self.me + ahead, self.owners)
            for source, columns in pieces(device):
                to_grp(
                    source,
                    self.buf.at[self.me, self.rep, :, columns],
                    self.send1.at[device],
                    self.recv1.at[self.me],
                    device,
                ).start()
            return 0

        lax.fori_loop(1, self.owners, one, 0)

    def relay(self):
        def one(ahead, _):
            owner = lax.rem(self.me + ahead, self.owners)
            part = self.buf.at[owner, self.rep]
            arrived(part, self.recv1.at[owner])
            for other in range(1, self.reps):
                to_rep(
                    part,
                    part,
                    self.send2.at[other],
                    self.recv2.at[other],
                    lax.rem(self.rep + other, self.reps),
                ).start()
            return 0

        lax.fori_loop(0, self.owners, one, 0)

    def wait(self):
        for other in range(1, self.reps):
            source = lax.rem(self.rep + self.reps - other, self.reps)
            arrived(self.buf.at[:, source], self.recv2.at[other])

    def finish(self):
        def one(ahead, _):
            device = lax.rem(self.me + ahead, self.owners)
            arrived(self.buf.at[device, self.rep], self.send1.at[device])
            return 0

        lax.fori_loop(1, self.owners, one, 0)
        for other in range(1, self.reps):
            arrived(self.buf.at[:, self.rep], self.send2.at[other])

    @staticmethod
    def scratch(owners, reps):
        return [
            pltpu.SemaphoreType.DMA((owners,)),
            pltpu.SemaphoreType.DMA((owners,)),
            pltpu.SemaphoreType.DMA((reps,)),
            pltpu.SemaphoreType.DMA((reps,)),
        ]


def query_positions(map_ref, s, at):
    row = lax.broadcasted_iota(jnp.int32, (2 * BLOCK_TOKENS, 1), 0)
    return row + jnp.where(
        row < BLOCK_TOKENS,
        map_ref[s, 2 * at] * BLOCK_TOKENS,
        (map_ref[s, 2 * at + 1] - 1) * BLOCK_TOKENS,
    )


def angles(table):
    turned = pltpu.roll(table, HEAD_SIZE // 2, 1)
    low = lax.broadcasted_iota(jnp.int32, table.shape, 1) < HEAD_SIZE // 2
    return jnp.where(low, table, turned), jnp.where(low, -turned, table)


def head_norm(values):
    scale = lax.rsqrt(jnp.mean(values * values, axis=-1, keepdims=True) + norm_epsilon)
    return values * scale, scale


def turn(values, cosine, sine):
    return values * cosine + pltpu.roll(values, HEAD_SIZE // 2, 1) * sine


def turn_back(values, cosine, sine):
    return values * cosine - pltpu.roll(values, HEAD_SIZE // 2, 1) * sine


def first_kernel(
    owners,
    reps,
    heads,
    kv_heads,
    sharers,
    tokens_ref,
    weight_ref,
    small_ref,
    table_ref,
    input_out,
    query_out,
    gate_out,
    key_out,
    value_out,
    query_rot_out,
    key_rot_out,
    columns_out,
    small_out,
    buf,
    weight_buf,
    small_send,
    small_recv,
    local_sem,
    out_sem,
    g_send,
    g_recv,
    *r_sems,
):
    me, rep = lax.axis_index("grp"), lax.axis_index("rep")
    rows, width = tokens_ref.shape
    shard = weight_ref.shape[0]
    share = shard // reps
    q_cols, kv_cols = heads * HEAD_SIZE, kv_heads * HEAD_SIZE
    all_q = QUERY_HEADS * HEAD_SIZE
    all_kv = KEY_VALUE_HEADS * HEAD_SIZE
    gather = Gather(owners, buf, g_send, g_recv)
    reshard = Reshard(owners, reps, weight_buf, r_sems)
    my_rows = pl.ds(pl.multiple_of(rep * share, share), share)

    def pieces(owner):
        out = []
        at = 0
        for base, cols, step in (
            (0, q_cols, owner),
            (all_q, q_cols, owner),
            (2 * all_q, kv_cols, owner // sharers),
            (2 * all_q + all_kv, kv_cols, owner // sharers),
        ):
            first = pl.multiple_of(base + step * cols, HEAD_SIZE)
            out.append((weight_ref.at[my_rows, pl.ds(first, cols)], pl.ds(at, cols)))
            at += cols
        return out

    own = pltpu.make_async_copy(tokens_ref, buf.at[me], local_sem)
    own.start()
    small_out[me] = small_ref[...]
    meet(owners, reps)
    reshard.start(pieces)

    def small_copy(device, index):
        return to_grp(
            small_ref, small_out.at[me], small_send.at[index], small_recv.at[index], device
        )

    for ahead in range(1, owners):
        small_copy(lax.rem(me + ahead, owners), ahead).start()
    gather.forward(me, tokens_ref)
    reshard.relay()
    for ahead in range(1, owners):
        source = lax.rem(me + owners - ahead, owners)
        arrived(small_out.at[source], small_recv.at[ahead])
    own.wait()
    middle = (gather.place > 0) & (gather.place < gather.chips - 1)
    early = jnp.where(middle, gather.chips, gather.chips - 1)

    def step(k, _):
        gather.step(k)
        return 0

    lax.fori_loop(1, early, step, 0)
    reshard.wait()
    columns_copy = pltpu.make_async_copy(weight_buf, columns_out, out_sem)
    columns_copy.start()

    gain = jnp.concatenate([small_out[e][:, :shard] for e in range(owners)], axis=1)
    heads_gain = small_out[0][:, 2 * shard :]
    for e in range(1, owners):
        heads_gain = heads_gain + small_out[e][:, 2 * shard :]
    gain_query = heads_gain[:, :HEAD_SIZE]
    gain_key = heads_gain[:, HEAD_SIZE:]
    total_cols = 2 * q_cols + 2 * kv_cols
    weight = weight_buf.reshape(width, total_cols)

    def block(k, _):
        @pl.when(k >= early)
        def _():
            gather.step(k)

        def core(which, _):
            mine = which == 0

            @pl.when(which == 1)
            def _():
                gather.sibling(k)

            at = 2 * nearest(gather.place, k, gather.chips) + jnp.where(
                mine, gather.core, 1 - gather.core
            )
            values = buf[at].astype(F32)
            normed, _unused = head_norm(values)
            entry = (normed * gain).astype(BF16)
            input_out[at] = entry
            projected = dot(entry, weight[...])
            cosine, sine = angles(table_ref[at])
            for h in range(heads):
                span = slice(h * HEAD_SIZE, (h + 1) * HEAD_SIZE)
                raw = projected[:, span]
                query_out[at, :, span] = raw
                query_rot_out[at, :, span] = turn(
                    head_norm(raw)[0] * gain_query, cosine, sine
                ).astype(BF16)
            gate_out[at] = projected[:, q_cols : 2 * q_cols]
            for h in range(kv_heads):
                span = slice(h * HEAD_SIZE, (h + 1) * HEAD_SIZE)
                raw = projected[:, 2 * q_cols + h * HEAD_SIZE : 2 * q_cols + (h + 1) * HEAD_SIZE]
                key_out[at, :, span] = raw
                key_rot_out[at, :, span] = turn(
                    head_norm(raw)[0] * gain_key, cosine, sine
                ).astype(BF16)
            value_out[at] = projected[:, 2 * q_cols + kv_cols :].astype(BF16)
            return 0

        lax.fori_loop(0, 2, core, 0)
        return 0

    lax.fori_loop(0, gather.chips, block, 0)
    columns_copy.wait()
    gather.finish()
    reshard.finish()
    for ahead in range(1, owners):
        small_copy(lax.rem(me + ahead, owners), ahead).wait_send()


def vmem():
    return pl.BlockSpec(memory_space=pltpu.VMEM)


def smem():
    return pl.BlockSpec(memory_space=pltpu.SMEM)


def anywhere():
    return pl.BlockSpec(memory_space=pl.ANY)


def first(owners, reps, heads, kv_heads, sharers, tokens, w_qkvg, small, table):
    rows, width = tokens.shape
    shard = w_qkvg.shape[0]
    q_cols, kv_cols = heads * HEAD_SIZE, kv_heads * HEAD_SIZE
    cols = 2 * q_cols + 2 * kv_cols
    shape = jax.ShapeDtypeStruct
    outs = (
        shape((owners, rows, width), BF16),
        shape((owners, rows, q_cols), F32),
        shape((owners, rows, q_cols), F32),
        shape((owners, rows, kv_cols), F32),
        shape((owners, rows, kv_cols), BF16),
        shape((owners, rows, q_cols), BF16),
        shape((owners, rows, kv_cols), BF16),
        shape((owners, reps, shard // reps, cols), BF16),
        shape((owners,) + small.shape, F32),
    )
    flops = 2 * owners * rows * width * cols
    return pl.pallas_call(
        functools.partial(first_kernel, owners, reps, heads, kv_heads, sharers),
        out_shape=outs,
        in_specs=[anywhere(), anywhere(), vmem(), vmem()],
        out_specs=(vmem(),) * 7 + (anywhere(), vmem()),
        scratch_shapes=[
            pltpu.VMEM((owners, rows, width), BF16),
            pltpu.VMEM((owners, reps, shard // reps, cols), BF16),
            pltpu.SemaphoreType.DMA((owners,)),
            pltpu.SemaphoreType.DMA((owners,)),
            pltpu.SemaphoreType.DMA,
            pltpu.SemaphoreType.DMA,
        ]
        + Gather.scratch(owners)
        + Reshard.scratch(owners, reps),
        compiler_params=pltpu.CompilerParams(
            collective_id=0, has_side_effects=True, vmem_limit_bytes=60 * 2**20
        ),
        cost_estimate=pl.CostEstimate(
            flops=flops, bytes_accessed=40 * 2**20, transcendentals=0
        ),
        name="first",
    )(tokens, w_qkvg, small, table)


def by_distance(place, step, chips):
    return nearest(place, chips - 1 - step, chips)


class Scatter:
    def __init__(self, owners, bufs, sems, order, parts, half=0):
        self.owners, self.chips = owners, owners // 2
        self.me = lax.axis_index("grp")
        self.place, self.core = self.me // 2, self.me % 2
        self.stage, self.near, self.line, self.both = bufs
        self.acc = self.both.at[self.core]
        self.near_send, self.near_recv, self.line_send, self.line_recv = sems
        self.order, self.parts, self.half = order, parts, half
        self.part = self.both.shape[1] // parts

    def at(self, k):
        return self.order(self.place, k, self.chips)

    def near_copy(self, k):
        at = self.at(k)
        return to_grp(
            self.stage.at[self.half, k % 2],
            self.near.at[self.half, at],
            self.near_send.at[self.half, k % 2],
            self.near_recv.at[self.half, at],
            self.me + 1 - 2 * self.core,
        )

    def rows(self, s):
        return pl.ds(s * self.part, self.part)

    def line_copy(self, at, s):
        target = self.place + jnp.where(at > self.place, 1, -1)
        slot = jnp.where((target == at) & (at < self.place), self.chips, at)
        return to_grp(
            self.near.at[self.half, at, self.rows(s)],
            self.line.at[self.half, slot, self.rows(s)],
            self.line_send.at[self.half, at, s],
            self.line_recv.at[self.half, slot, s],
            2 * target + self.core,
        )

    def prepare(self, k, term):
        @pl.when(k >= 2)
        def _():
            self.near_copy(k - 2).wait_send()

        self.both[...] = term(self.at(k)).reshape(self.both.shape)
        self.stage[self.half, k % 2] = self.both[1 - self.core].astype(BF16)
        self.near_copy(k).start()

    def add(self, slot, s):
        part = self.line.at[self.half, slot, self.rows(s)]
        arrived(part, self.line_recv.at[self.half, slot, s])
        self.acc[self.rows(s)] += part[...].astype(F32)

    def combine(self, k):
        at = self.at(k)
        arrived(self.near.at[self.half, at], self.near_recv.at[self.half, at])
        self.acc[...] += self.near[self.half, at].astype(F32)
        below = self.place > 0
        above = self.place < self.chips - 1

        def one(s, _):
            @pl.when(((at >= self.place) & below) | ((at < self.place) & above))
            def _():
                self.add(at, s)

            @pl.when((at == self.place) & above)
            def _():
                self.add(self.chips, s)

            @pl.when(at != self.place)
            def _():
                self.near[self.half, at, self.rows(s)] = self.acc[self.rows(s)].astype(BF16)
                self.line_copy(at, s).start()

            return 0

        lax.fori_loop(0, self.parts, one, 0)

    def finish(self):
        self.near_copy(self.chips - 2).wait_send()
        self.near_copy(self.chips - 1).wait_send()

        def one(at, _):
            @pl.when(at != self.place)
            def _():
                for s in range(self.parts):
                    self.line_copy(at, s).wait_send()

            return 0

        lax.fori_loop(0, self.chips, one, 0)

    @staticmethod
    def scratch(owners, rows, width, parts, halves=1):
        chips = owners // 2
        rows //= halves
        return [
            pltpu.VMEM((halves, 2, rows, width), BF16),
            pltpu.VMEM((halves, chips, rows, width), BF16),
            pltpu.VMEM((halves, chips + 1, rows, width), BF16),
            pltpu.VMEM((2, rows, width), F32),
            pltpu.SemaphoreType.DMA((halves, 2)),
            pltpu.SemaphoreType.DMA((halves, chips)),
            pltpu.SemaphoreType.DMA((halves, chips, parts)),
            pltpu.SemaphoreType.DMA((halves, chips + 1, parts)),
        ]


PARTS = 4


class RepSum:
    def __init__(self, owners, reps, units, along, held, came, result, sems):
        self.owners, self.reps, self.units, self.along = owners, reps, units, along
        self.me, self.rep = lax.axis_index("grp"), lax.axis_index("rep")
        self.bits = reps.bit_length() - 1
        self.held, self.came, self.result = held, came, result
        self.down_send, self.down_recv, self.own_send, self.own_recv, self.up_send, self.up_recv = sems

    def weight(self, t, j):
        which = (t + j) % self.bits
        return sum(jnp.where(which == b, 1 << b, 0) for b in range(self.bits))

    @staticmethod
    def flip(index, weight):
        return index + weight * (1 - 2 * ((index // weight) % 2))

    def spread(self, index, t, bits):
        out = [index]
        for j in bits:
            out += [self.flip(i, self.weight(t, j)) for i in out]
        return out

    def unit(self, t):
        return lax.rem(self.me + t, self.owners) if self.along else t

    def source(self, t):
        return lax.rem(self.me + self.owners - t, self.owners) if self.along else t

    def downs(self, t, j):
        u = self.unit(t)
        first_index = sum(1 << (self.bits - 1 - i) for i in range(j))
        partner = self.flip(self.rep, self.weight(t, j))
        return [
            to_rep(
                self.held.at[u, s],
                self.came.at[u, first_index + c],
                self.down_send.at[u, first_index + c],
                self.down_recv.at[u, first_index + c],
                partner,
            )
            for c, s in enumerate(self.spread(partner, t, range(j + 1, self.bits)))
        ]

    def ups(self, t, j):
        e = self.source(t)
        held = self.spread(self.rep, t, range(self.bits - 1, self.bits - 1 - j, -1))
        partner = self.flip(self.rep, self.weight(t, self.bits - 1 - j))
        return [
            to_rep(
                self.result.at[e, s],
                self.result.at[e, s],
                self.up_send.at[e, (1 << j) - 1 + c],
                self.up_recv.at[e, s],
                partner,
            )
            for c, s in enumerate(held)
        ]

    def deliver(self, t, do_local, do_remote):
        u = self.unit(t)
        source = self.held.at[u, self.rep]
        slot = self.me if self.along else u
        local = pltpu.make_async_copy(source, self.result.at[slot, self.rep], self.own_recv.at[slot])
        if not self.along:
            do_local(local)
            return
        remote = to_grp(
            source,
            self.result.at[slot, self.rep],
            self.own_send.at[u],
            self.own_recv.at[slot],
            u,
        )
        pl.when(u == self.me)(lambda: do_local(local))
        pl.when(u != self.me)(lambda: do_remote(remote))

    def tick(self, t, term):
        def phase(lag):
            return (t >= lag) & (t < self.units + lag)

        @pl.when(phase(0))
        def _():
            u = self.unit(t)
            self.held[u] = term(t, u).astype(BF16).reshape(self.held.shape[1:])
            for copy in self.downs(t, 0):
                copy.start()

        for j in range(1, self.bits + 1):

            @pl.when(phase(j))
            def _(j=j, t=t - j):
                u = self.unit(t)
                first_index = sum(1 << (self.bits - 1 - i) for i in range(j - 1))
                for c, s in enumerate(self.spread(self.rep, t, range(j, self.bits))):
                    part = self.came.at[u, first_index + c]
                    arrived(part, self.down_recv.at[u, first_index + c])
                    self.held[u, s] = (self.held[u, s].astype(F32) + part[...].astype(F32)).astype(
                        BF16
                    )
                if j < self.bits:
                    for copy in self.downs(t, j):
                        copy.start()
                else:
                    self.deliver(t, lambda c: c.start(), lambda c: c.start())

        for j in range(self.bits + 1):

            @pl.when(phase(self.bits + 1 + j))
            def _(j=j, t=t - self.bits - 1 - j):
                e = self.source(t)
                if j == 0:
                    arrived(self.result.at[e, self.rep], self.own_recv.at[e])
                else:
                    bit = self.bits - j
                    held = self.spread(self.rep, t, range(self.bits - 1, bit, -1))
                    for s in held:
                        s = self.flip(s, self.weight(t, bit))
                        arrived(self.result.at[e, s], self.up_recv.at[e, s])
                if j < self.bits:
                    for copy in self.ups(t, j):
                        copy.start()

    def ticks(self):
        return self.units + 2 * self.bits + 1

    def finish(self):
        def one(t, _):
            for j in range(self.bits):
                for copy in self.downs(t, j) + self.ups(t, j):
                    copy.wait_send()
            self.deliver(t, lambda c: None, lambda c: c.wait_send())
            return 0

        lax.fori_loop(0, self.units, one, 0)

    @staticmethod
    def scratch(reps, units, share, cols):
        dma = pltpu.SemaphoreType.DMA
        return [
            pltpu.VMEM((units, reps, share, cols), BF16),
            pltpu.VMEM((units, reps - 1, share, cols), BF16),
            dma((units, reps - 1)),
            dma((units, reps - 1)),
            dma((units,)),
            dma((units,)),
            dma((units, reps - 1)),
            dma((units, reps)),
        ]


def interleave(gather, scatter, term, ready=None, then=None, fill=None):
    chips = gather.chips
    middle = (gather.place > 0) & (gather.place < chips - 1)

    def stage(k, _):
        if ready is not None:
            ready(k)
        scatter.prepare(k, term)
        if fill is not None:
            fill(k)

        @pl.when(middle & (2 * k + 1 < chips))
        def _():
            gather.step(2 * k + 1)

        @pl.when(middle & (2 * k + 2 < chips))
        def _():
            gather.step(2 * k + 2)

        scatter.combine(k)

        @pl.when((~middle) & (k + 1 < chips))
        def _():
            gather.step(k + 1)

        then(k)
        return 0

    lax.fori_loop(0, chips, stage, 0)


def attention_kernel(
    owners,
    reps,
    heads,
    kv_heads,
    tokens_ref,
    query_ref,
    key_ref,
    value_ref,
    gate_ref,
    map_ref,
    position_row_ref,
    out_ref,
    gain_ref,
    cotangent_ref,
    in_pieces_ref,
    attn_out,
    hidden_out,
    entry_out,
    cotangent_out,
    columns_out,
    local_sem,
    *rest,
):
    me, rep = lax.axis_index("grp"), lax.axis_index("rep")
    scatter = Scatter(owners, rest[:4], rest[4:8], by_distance, PARTS)
    gather = Gather(owners, cotangent_out, *rest[8:10])
    reshard = Reshard(owners, reps, columns_out, rest[10:14])
    cols = in_pieces_ref.shape[2]

    def pieces(owner):
        return [(in_pieces_ref.at[owner], pl.ds(0, cols))]

    own = pltpu.make_async_copy(cotangent_ref, cotangent_out.at[me], local_sem)
    own.start()
    meet(owners, reps)
    gather.forward(me, cotangent_ref)
    reshard.start(pieces)
    per_kv = heads // kv_heads
    block_rows = 2 * BLOCK_TOKENS

    def attend(at):
        for s in range(GROUP_SEQUENCES):
            rows = slice(s * block_rows, (s + 1) * block_rows)
            allowed = position_row_ref[s] <= query_positions(map_ref, s, at)
            allowed = jnp.concatenate([allowed] * per_kv, axis=0)
            for kv in range(kv_heads):
                span = slice(kv * HEAD_SIZE, (kv + 1) * HEAD_SIZE)
                spans = [
                    slice(h * HEAD_SIZE, (h + 1) * HEAD_SIZE)
                    for h in range(kv * per_kv, (kv + 1) * per_kv)
                ]
                query = jnp.concatenate([query_ref[at, rows, h] for h in spans], axis=0)
                keys = key_ref[:, rows, span].reshape(-1, HEAD_SIZE)
                values = value_ref[:, rows, span].reshape(-1, HEAD_SIZE)
                scores = dot_nt(query, keys) * HEAD_SIZE ** (-0.5)
                scores = jnp.where(allowed, scores, masked_value)
                exps = jnp.exp(scores - jnp.max(scores, axis=-1, keepdims=True))
                probability = exps / jnp.sum(exps, axis=-1, keepdims=True)
                attended = dot(probability.astype(BF16), values)
                for i, h in enumerate(spans):
                    gated = attended[i * block_rows : (i + 1) * block_rows] * jax.nn.sigmoid(
                        gate_ref[at, rows, h]
                    )
                    attn_out[at, rows, h] = gated.astype(BF16)

    def ready(k):
        at = scatter.at(k)

        def one(core, _):
            attend(2 * at + core)
            return 0

        lax.fori_loop(0, 2, one, 0)

    def term(at):
        both = attn_out[pl.ds(2 * at, 2)]
        return dot(both.reshape(-1, both.shape[-1]), out_ref[...])

    def then(k):
        pl.when(k == 0)(reshard.relay)
        gather.sibling(k)

    interleave(gather, scatter, term, ready, then)
    hidden = tokens_ref[...].astype(F32) + scatter.acc[...]
    hidden_out[...] = hidden
    entry_out[...] = (head_norm(hidden)[0] * gain_ref[...]).astype(BF16)
    own.wait()
    reshard.wait()
    gather.finish()
    scatter.finish()
    reshard.finish()


def attention(
    owners,
    reps,
    heads,
    kv_heads,
    tokens,
    query_rot,
    key_rot,
    value_rows,
    gate_raw,
    block_map,
    position_row,
    w_out,
    gain_mlp,
    cotangent,
    in_pieces,
):
    rows, width = tokens.shape
    shape = jax.ShapeDtypeStruct
    share = in_pieces.shape[1]
    outs = (
        shape(query_rot.shape, BF16),
        shape((rows, width), F32),
        shape((rows, width), BF16),
        shape((owners, rows, width), BF16),
        shape((owners, reps, share, in_pieces.shape[2]), BF16),
    )
    return pl.pallas_call(
        functools.partial(attention_kernel, owners, reps, heads, kv_heads),
        out_shape=outs,
        in_specs=[vmem()] * 5 + [smem()] + [vmem()] * 3 + [anywhere()] * 2,
        out_specs=(vmem(),) * 3 + (anywhere(),) * 2,
        scratch_shapes=[pltpu.SemaphoreType.DMA]
        + Scatter.scratch(owners, rows, width, PARTS)
        + Gather.scratch(owners)
        + Reshard.scratch(owners, reps),
        compiler_params=pltpu.CompilerParams(
            collective_id=1, has_side_effects=True, vmem_limit_bytes=60 * 2**20
        ),
        cost_estimate=pl.CostEstimate(
            flops=4 * owners * rows * width * query_rot.shape[2],
            bytes_accessed=40 * 2**20,
            transcendentals=0,
        ),
        name="attention",
    )(
        tokens,
        query_rot,
        key_rot,
        value_rows,
        gate_raw,
        block_map,
        position_row,
        w_out,
        gain_mlp,
        cotangent,
        in_pieces,
    )


def mlp_kernel(
    owners,
    reps,
    entry_ref,
    cotangent_all_ref,
    in_ref,
    down_ref,
    hidden_ref,
    cotangent_ref,
    gain_ref,
    entry_all,
    activated_out,
    grads_out,
    grad_hidden_out,
    grad_branch_out,
    gain_out,
    weight_out,
    entry_buf,
    cotangent_buf,
    activated_buf,
    down_sum,
    local_sem,
    load_sem,
    store_sem,
    *rest,
):
    me = lax.axis_index("grp")
    chips = owners // 2
    gather = Gather(owners, entry_all, *rest[8:10])
    scatter = Scatter(owners, rest[:4], rest[4:8], by_distance, PARTS)
    shard = weight_out.shape[1] * weight_out.shape[2]
    rows = RepSum(
        owners, reps, down_ref.shape[0] // shard, False, rest[10], rest[11], weight_out, rest[12:18]
    )
    units = down_ref.shape[0]
    own = pltpu.make_async_copy(entry_ref, entry_all.at[me], local_sem)
    own.start()
    meet(owners, reps)
    gather.forward(me, entry_ref)
    down_sum[...] = jnp.zeros_like(down_sum)
    own.wait()

    def block_of(k, which):
        return 2 * nearest(gather.place, k, chips) + jnp.where(
            which == 0, gather.core, 1 - gather.core
        )

    def store(which, at):
        return pltpu.make_async_copy(
            activated_buf.at[which], activated_out.at[at], store_sem.at[which]
        )

    def compute(k):
        def one(which, _):
            at = block_of(k, which)
            cotangent_load = pltpu.make_async_copy(
                cotangent_all_ref.at[at], cotangent_buf.at[which], load_sem.at[1, which]
            )
            cotangent_load.start()

            @pl.when(which == 1)
            def _():
                gather.sibling(k)

            entry_load = pltpu.make_async_copy(
                entry_all.at[at], entry_buf.at[which], load_sem.at[0, which]
            )
            entry_load.start()
            cotangent_load.wait()
            grad_activated = dot_nt(cotangent_buf[which], down_ref[...])
            entry_load.wait()
            gate_up = dot(entry_buf[which], in_ref[...])
            gate, up = gate_up[:, :units], gate_up[:, units:]
            sig = jax.nn.sigmoid(gate)
            silu = gate * sig

            @pl.when(k > 0)
            def _():
                store(which, at).wait()

            activated_buf[which] = (silu * up).astype(BF16)
            store(which, at).start()
            grads_out[at, :, :units] = (
                grad_activated * up * sig * (1.0 + gate * (1.0 - sig))
            ).astype(BF16)
            grads_out[at, :, units:] = (grad_activated * silu).astype(BF16)
            down_sum[...] += dot_tn(activated_buf[which], cotangent_buf[which])
            return 0

        lax.fori_loop(0, 2, one, 0)

    def term(at):
        both = grads_out[pl.ds(2 * at, 2)]
        return dot_nt(both.reshape(-1, both.shape[-1]), in_ref[...])

    def rows_of(t, u):
        return down_sum[pl.ds(pl.multiple_of(u * shard, shard), shard)]

    middle = (gather.place > 0) & (gather.place < chips - 1)
    early = jnp.where(middle, chips, 1)

    def step(k, _):
        gather.step(k)
        return 0

    def front(k, _):
        @pl.when(k >= early)
        def _():
            gather.step(k)

        compute(k)
        return 0

    lax.fori_loop(1, early, step, 0)
    lax.fori_loop(0, chips, front, 0)

    def back(k, _):
        scatter.prepare(k, term)
        rows.tick(TICKS * k, rows_of)
        scatter.combine(k)

        def one(t, _):
            rows.tick(t, rows_of)
            return 0

        lax.fori_loop(TICKS * k + 1, TICKS * (k + 1), one, 0)
        return 0

    lax.fori_loop(0, chips, back, 0)
    hidden = hidden_ref[...]
    normed, scale = head_norm(hidden)
    grad_entry = scatter.acc[...]
    gain_out[...] = jnp.sum(grad_entry * normed, axis=0, keepdims=True)
    weighted = grad_entry * gain_ref[...]
    grad_hidden = cotangent_ref[...].astype(F32) + scale * (
        weighted - normed * jnp.mean(weighted * normed, axis=-1, keepdims=True)
    )
    grad_hidden_out[...] = grad_hidden
    grad_branch_out[...] = grad_hidden.astype(BF16)

    def late(t, _):
        rows.tick(t, rows_of)
        return 0

    lax.fori_loop(TICKS * chips, rows.ticks(), late, 0)
    for which in range(2):
        store(which, block_of(chips - 1, which)).wait()
    gather.finish()
    scatter.finish()
    rows.finish()


def mlp(owners, reps, entry, cotangent_all, in_cols, w_down, hidden, cotangent, gain_mlp):
    rows, width = entry.shape
    units = w_down.shape[0]
    shard = width // owners
    share = shard // reps
    shape = jax.ShapeDtypeStruct
    outs = (
        shape((owners, rows, width), BF16),
        shape((owners, rows, units), BF16),
        shape((owners, rows, 2 * units), BF16),
        shape((rows, width), F32),
        shape((rows, width), BF16),
        shape((1, width), F32),
        shape((units // shard, reps, share, width), BF16),
    )
    return pl.pallas_call(
        functools.partial(mlp_kernel, owners, reps),
        out_shape=outs,
        in_specs=[anywhere()] * 2 + [vmem()] * 5,
        out_specs=(anywhere(),) * 2 + (vmem(),) * 4 + (anywhere(),),
        scratch_shapes=[
            pltpu.VMEM((2, rows, width), BF16),
            pltpu.VMEM((2, rows, width), BF16),
            pltpu.VMEM((2, rows, units), BF16),
            pltpu.VMEM((units, width), F32),
            pltpu.SemaphoreType.DMA,
            pltpu.SemaphoreType.DMA((2, 2)),
            pltpu.SemaphoreType.DMA((2,)),
        ]
        + Scatter.scratch(owners, rows, width, PARTS)
        + Gather.scratch(owners)
        + RepSum.scratch(reps, units // shard, share, width),
        compiler_params=pltpu.CompilerParams(
            collective_id=2, has_side_effects=True, vmem_limit_bytes=63 * 2**20
        ),
        cost_estimate=pl.CostEstimate(
            flops=12 * owners * rows * width * units,
            bytes_accessed=40 * 2**20,
            transcendentals=0,
        ),
        name="mlp",
    )(entry, cotangent_all, in_cols, w_down, hidden, cotangent, gain_mlp)


def unturned_norm_back(grad, raw, gain, cosine, sine):
    back = turn_back(grad, cosine, sine)
    normed, scale = head_norm(raw)
    weighted = back * gain
    grad_raw = scale * (weighted - normed * jnp.mean(weighted * normed, axis=-1, keepdims=True))
    return grad_raw, jnp.sum(back * normed, axis=0, keepdims=True)


def backward_kernel(
    owners,
    reps,
    heads,
    kv_heads,
    branch_ref,
    activated_ref,
    down_ref,
    out_ref,
    hidden_ref,
    query_ref,
    query_rot_ref,
    gate_ref,
    key_ref,
    key_rot_ref,
    value_ref,
    map_ref,
    position_row_ref,
    table_ref,
    heads_gain_ref,
    attn_out_ref,
    grad_gate_up_ref,
    entry_ref,
    branch_all,
    output_out,
    grads_out,
    gain_out,
    out_term,
    weight_out,
    branch_buf,
    key_sum,
    value_sum,
    entry_buf,
    activated_buf,
    attn_buf,
    local_sem,
    load_sem,
    entry_sem,
    *rest,
):
    me = lax.axis_index("grp")
    chips = owners // 2
    scatter = Scatter(owners, rest[:4], rest[4:8], by_distance, PARTS)
    gather = Gather(owners, branch_all, *rest[8:10])
    columns = RepSum(owners, reps, owners, True, rest[10], rest[11], weight_out, rest[12:18])
    load_columns = column_loads(entry_ref, entry_buf, entry_sem, entry_buf.shape[-1])
    load_columns(0, me).start()
    columns_of = columns_term(
        columns,
        load_columns,
        entry_buf,
        lambda: grad_gate_up_ref[...].reshape(-1, grad_gate_up_ref.shape[-1]),
    )

    def tick(t):
        columns.tick(t, columns_of)
    own = pltpu.make_async_copy(branch_ref, branch_all.at[me], local_sem)
    own.start()
    meet(owners, reps)
    gather.forward(me, branch_ref)
    own.wait()
    key_sum[...] = jnp.zeros_like(key_sum)
    value_sum[...] = jnp.zeros_like(value_sum)
    gain_out[...] = jnp.zeros_like(gain_out)
    out_term[...] = jnp.zeros_like(out_term)
    per_kv = heads // kv_heads
    q_cols, kv_cols = heads * HEAD_SIZE, kv_heads * HEAD_SIZE
    block_rows = 2 * BLOCK_TOKENS
    root = HEAD_SIZE ** (-0.5)
    gain_query = heads_gain_ref[:, :HEAD_SIZE]
    gain_key = heads_gain_ref[:, HEAD_SIZE:]

    def block(at):
        load = pltpu.make_async_copy(branch_all.at[at], branch_buf, load_sem)
        load_attn = pltpu.make_async_copy(attn_out_ref.at[at], attn_buf, local_sem)
        load.start()
        load_attn.start()
        load.wait()
        grad_attn_out = dot_nt(branch_buf[...], out_ref[...])
        load_attn.wait()
        out_term[...] += dot_tn(attn_buf[...], branch_buf[...])
        for s in range(GROUP_SEQUENCES):
            rows = slice(s * block_rows, (s + 1) * block_rows)
            cosine, sine = angles(table_ref[at, rows])
            allowed = position_row_ref[s] <= query_positions(map_ref, s, at)
            allowed = jnp.concatenate([allowed] * per_kv, axis=0)
            for kv in range(kv_heads):
                span = slice(kv * HEAD_SIZE, (kv + 1) * HEAD_SIZE)
                spans = [
                    slice(h * HEAD_SIZE, (h + 1) * HEAD_SIZE)
                    for h in range(kv * per_kv, (kv + 1) * per_kv)
                ]
                query = jnp.concatenate([query_rot_ref[at, rows, h] for h in spans], axis=0)
                keys = key_rot_ref[:, rows, span].reshape(-1, HEAD_SIZE)
                values = value_ref[:, rows, span].reshape(-1, HEAD_SIZE)
                scores = dot_nt(query, keys) * root
                scores = jnp.where(allowed, scores, masked_value)
                exps = jnp.exp(scores - jnp.max(scores, axis=-1, keepdims=True))
                exact = exps / jnp.sum(exps, axis=-1, keepdims=True)
                low = exact.astype(BF16)
                attended = dot(low, values)
                inputs = []
                for i, h in enumerate(spans):
                    grad = grad_attn_out[rows, h]
                    sig = jax.nn.sigmoid(gate_ref[at, rows, h])
                    inputs.append((grad * sig).astype(BF16))
                    gated = slice(q_cols + h.start, q_cols + h.stop)
                    grads_out[at, rows, gated] = (
                        grad
                        * attended[i * block_rows : (i + 1) * block_rows]
                        * sig
                        * (1.0 - sig)
                    ).astype(BF16)
                grad_attended = jnp.concatenate(inputs, axis=0)
                grad_probs = dot_nt(grad_attended, values)
                inner = jnp.sum(exact * grad_probs, axis=-1, keepdims=True)
                grad_scores = (exact * (grad_probs - inner)).astype(BF16)
                grad_query = dot(grad_scores, keys) * root
                key_sum[s, kv] += dot_tn(grad_scores, query)
                value_sum[s, kv] += dot_tn(low, grad_attended)
                for i, h in enumerate(spans):
                    grad_raw, gain_sum = unturned_norm_back(
                        grad_query[i * block_rows : (i + 1) * block_rows],
                        query_ref[at, rows, h],
                        gain_query,
                        cosine,
                        sine,
                    )
                    grads_out[at, rows, h] = grad_raw.astype(BF16)
                    gain_out[:, :HEAD_SIZE] += gain_sum

    def term(at):
        load = pltpu.make_async_copy(activated_ref.at[pl.ds(2 * at, 2)], activated_buf, load_sem)
        load.start()
        load.wait()
        both = activated_buf[...]
        return dot(both.reshape(-1, both.shape[-1]), down_ref[...])

    def then(k):
        def one(which, _):
            @pl.when(which == 1)
            def _():
                gather.sibling(k)

            block(
                2 * nearest(gather.place, k, chips)
                + jnp.where(which == 0, gather.core, 1 - gather.core)
            )
            tick(TICKS * k + 1 + which)
            return 0

        lax.fori_loop(0, 2, one, 0)

    interleave(gather, scatter, term, then=then, fill=lambda k: tick(TICKS * k))
    hidden = scatter.both.at[1 - scatter.core]
    load_hidden = pltpu.make_async_copy(hidden_ref, hidden, local_sem)
    load_hidden.start()
    load_hidden.wait()
    output_out[...] = (hidden[...] + scatter.acc[...]).astype(BF16)

    key_raw = scatter.both.at[0]

    def key_columns(at):
        return pl.ds(pl.multiple_of(at * kv_cols, HEAD_SIZE), kv_cols)

    def load_keys(at, _):
        pltpu.make_async_copy(key_ref.at[at], key_raw.at[:, key_columns(at)], load_sem).start()
        return 0

    lax.fori_loop(0, owners, load_keys, 0)
    arrived(key_raw.at[:, pl.ds(0, owners * kv_cols)], load_sem)

    def keys(at, _):
        for s in range(GROUP_SEQUENCES):
            rows = slice(s * block_rows, (s + 1) * block_rows)
            for kv in range(kv_heads):
                span = slice(kv * HEAD_SIZE, (kv + 1) * HEAD_SIZE)
                place = pl.ds(pl.multiple_of(at * block_rows, block_rows), block_rows)
                grad_raw, gain_sum = unturned_norm_back(
                    key_sum[s, kv, place] * root,
                    key_raw[
                        rows, pl.ds(pl.multiple_of(at * kv_cols, HEAD_SIZE) + span.start, HEAD_SIZE)
                    ],
                    gain_key,
                    *angles(table_ref[at, rows]),
                )
                first_col = 2 * q_cols + kv * HEAD_SIZE
                grads_out[at, rows, first_col : first_col + HEAD_SIZE] = grad_raw.astype(BF16)
                first_col += kv_cols
                grads_out[at, rows, first_col : first_col + HEAD_SIZE] = value_sum[
                    s, kv, place
                ].astype(BF16)
                gain_out[:, HEAD_SIZE:] += gain_sum
        return 0

    lax.fori_loop(0, owners, keys, 0)

    def late(t, _):
        tick(t)
        return 0

    lax.fori_loop(TICKS * chips, columns.ticks(), late, 0)
    gather.finish()
    scatter.finish()
    columns.finish()


def backward(
    owners,
    reps,
    heads,
    kv_heads,
    branch,
    activated,
    w_down,
    w_out,
    hidden,
    query_raw,
    query_rot,
    gate_raw,
    key_raw,
    key_rot,
    value_rows,
    block_map,
    position_row,
    table,
    heads_gain,
    attn_out,
    grad_gate_up,
    entry_all,
):
    rows, width = branch.shape
    cols = 2 * (heads + kv_heads) * HEAD_SIZE
    seq_len = position_row.shape[-1]
    shard = width // owners
    shape = jax.ShapeDtypeStruct
    outs = (
        shape((owners, rows, width), BF16),
        shape((rows, width), BF16),
        shape((owners, rows, cols), BF16),
        shape((1, 2 * HEAD_SIZE), F32),
        shape(w_out.shape, F32),
        shape((owners, reps, shard // reps, grad_gate_up.shape[2]), BF16),
    )
    return pl.pallas_call(
        functools.partial(backward_kernel, owners, reps, heads, kv_heads),
        out_shape=outs,
        in_specs=[anywhere()] * 2
        + [vmem()] * 2
        + [anywhere()]
        + [vmem()] * 3
        + [anywhere()]
        + [vmem()] * 2
        + [smem()]
        + [vmem()] * 3
        + [anywhere()]
        + [vmem()]
        + [anywhere()],
        out_specs=(anywhere(),) + (vmem(),) * 4 + (anywhere(),),
        scratch_shapes=[
            pltpu.VMEM((rows, width), BF16),
            pltpu.VMEM((GROUP_SEQUENCES, kv_heads, seq_len, HEAD_SIZE), F32),
            pltpu.VMEM((GROUP_SEQUENCES, kv_heads, seq_len, HEAD_SIZE), F32),
            pltpu.VMEM((2, owners, rows, shard), BF16),
            pltpu.VMEM((2,) + activated.shape[1:], BF16),
            pltpu.VMEM(attn_out.shape[1:], BF16),
            pltpu.SemaphoreType.DMA,
            pltpu.SemaphoreType.DMA,
            pltpu.SemaphoreType.DMA((2,)),
        ]
        + Scatter.scratch(owners, rows, width, PARTS)
        + Gather.scratch(owners)
        + RepSum.scratch(reps, owners, shard // reps, grad_gate_up.shape[2]),
        compiler_params=pltpu.CompilerParams(
            collective_id=3, has_side_effects=True, vmem_limit_bytes=63 * 2**20
        ),
        cost_estimate=pl.CostEstimate(
            flops=4 * owners * rows * width * cols,
            bytes_accessed=40 * 2**20,
            transcendentals=0,
        ),
        name="backward",
    )(
        branch,
        activated,
        w_down,
        w_out,
        hidden,
        query_raw,
        query_rot,
        gate_raw,
        key_raw,
        key_rot,
        value_rows,
        block_map,
        position_row,
        table,
        heads_gain,
        attn_out,
        grad_gate_up,
        entry_all,
    )


def column_loads(source_ref, buf, sem, shard):
    def load(slot, u):
        columns = pl.ds(pl.multiple_of(u * shard, shard), shard)
        return pltpu.make_async_copy(source_ref.at[:, :, columns], buf.at[slot], sem.at[slot])

    return load


def columns_term(total, load, buf, grads):
    def term(t, u):
        @pl.when(t + 1 < total.units)
        def _():
            load((t + 1) % 2, total.unit(t + 1)).start()

        load(t % 2, u).wait()
        entry = buf[t % 2]
        return dot_tn(entry.reshape(-1, entry.shape[-1]), grads())

    return term


def last_kernel(
    owners,
    reps,
    grads_ref,
    weight_ref,
    tokens_ref,
    grad_hidden_ref,
    gain_ref,
    out_term_ref,
    gain_mlp_ref,
    gain_heads_ref,
    entry_ref,
    grad_out,
    gains_out,
    weight_out,
    out_weight_out,
    entry_buf,
    gains_send,
    gains_came,
    gains_all,
    load_sem,
    g_send,
    g_recv,
    r_send,
    r_recv,
    *rest,
):
    me, rep = lax.axis_index("grp"), lax.axis_index("rep")
    chips = owners // 2
    scatter = Scatter(owners, rest[:4], rest[4:8], by_distance, PARTS)
    columns = RepSum(owners, reps, owners, True, rest[8], rest[9], weight_out, rest[10:16])
    rows = RepSum(owners, reps, 1, False, rest[16], rest[17], out_weight_out, rest[18:24])
    shard = entry_buf.shape[-1]
    load = column_loads(entry_ref, entry_buf, load_sem, shard)
    load(0, me).start()
    meet(owners, reps)

    def flat(ref):
        return ref[...].reshape(-1, ref.shape[-1])

    columns_of = columns_term(columns, load, entry_buf, lambda: flat(grads_ref))

    def rows_of(t, u):
        return out_term_ref[...]

    def tick(t):
        rows.tick(t, rows_of)
        columns.tick(t, columns_of)

    def term(at):
        both = grads_ref[pl.ds(2 * at, 2)]
        return dot_nt(both.reshape(-1, both.shape[-1]), weight_ref[...])

    def stage(k, _):
        scatter.prepare(k, term)
        tick(TICKS * k)
        scatter.combine(k)

        def one(t, _):
            tick(t)
            return 0

        lax.fori_loop(TICKS * k + 1, TICKS * (k + 1), one, 0)
        return 0

    lax.fori_loop(0, chips, stage, 0)
    grad = scatter.acc[...]
    normed, scale = head_norm(tokens_ref[...].astype(F32))
    gain_attn = jnp.sum(grad * normed, axis=0, keepdims=True)
    gain_mlp = gain_mlp_ref[...]
    for e in range(owners):
        span = slice(e * shard, (e + 1) * shard)
        gains_send[e] = jnp.concatenate(
            [gain_attn[:, span], gain_mlp[:, span], gain_heads_ref[...]], axis=1
        )

    def gains_copy(ahead):
        device = lax.rem(me + ahead, owners)
        return to_grp(
            gains_send.at[device],
            gains_came.at[me],
            g_send.at[ahead],
            g_recv.at[me],
            device,
        )

    def gains_up(ahead):
        return to_rep(
            gains_all.at[rep],
            gains_all.at[rep],
            r_send.at[ahead],
            r_recv.at[rep],
            lax.rem(rep + ahead, reps),
        )

    for ahead in range(1, owners):
        gains_copy(ahead).start()
    gains_came[me] = gains_send[me]
    weighted = grad * gain_ref[...]
    grad_out[...] = (
        grad_hidden_ref[...]
        + scale * (weighted - normed * jnp.mean(weighted * normed, axis=-1, keepdims=True))
    ).astype(BF16)
    for ahead in range(1, owners):
        source = lax.rem(me + ahead, owners)
        arrived(gains_came.at[source], g_recv.at[source])
    gains_all[rep] = jnp.sum(gains_came[...], axis=0)
    for ahead in range(1, reps):
        gains_up(ahead).start()

    def one(t, _):
        tick(t)
        return 0

    lax.fori_loop(TICKS * chips, max(columns.ticks(), rows.ticks()), one, 0)
    for ahead in range(1, reps):
        source = lax.rem(rep + ahead, reps)
        arrived(gains_all.at[source], r_recv.at[source])
    gains_out[...] = jnp.sum(gains_all[...], axis=0)
    for ahead in range(1, owners):
        gains_copy(ahead).wait_send()
    for ahead in range(1, reps):
        gains_up(ahead).wait_send()
    scatter.finish()
    columns.finish()
    rows.finish()


TICKS = 3


def last(
    owners,
    reps,
    grads,
    weight,
    tokens,
    grad_hidden,
    gain,
    out_term,
    gain_mlp,
    gain_heads,
    entry_all,
):
    rows, width = tokens.shape
    cols = grads.shape[2]
    shard = width // owners
    share = shard // reps
    small = 2 * shard + gain_heads.shape[1]
    shape = jax.ShapeDtypeStruct
    dma = pltpu.SemaphoreType.DMA
    return pl.pallas_call(
        functools.partial(last_kernel, owners, reps),
        out_shape=(
            shape((rows, width), BF16),
            shape((1, small), F32),
            shape((owners, reps, share, cols), BF16),
            shape((1, reps, share, width), BF16),
        ),
        in_specs=[vmem()] * 8 + [anywhere()],
        out_specs=(vmem(),) * 2 + (anywhere(),) * 2,
        scratch_shapes=[
            pltpu.VMEM((2, owners, rows, shard), BF16),
            pltpu.VMEM((owners, 1, small), F32),
            pltpu.VMEM((owners, 1, small), F32),
            pltpu.VMEM((reps, 1, small), F32),
            dma((2,)),
            dma((owners,)),
            dma((owners,)),
            dma((reps,)),
            dma((reps,)),
        ]
        + Scatter.scratch(owners, rows, width, PARTS)
        + RepSum.scratch(reps, owners, share, cols)
        + RepSum.scratch(reps, 1, share, width),
        compiler_params=pltpu.CompilerParams(
            collective_id=4, has_side_effects=True, vmem_limit_bytes=60 * 2**20
        ),
        cost_estimate=pl.CostEstimate(
            flops=4 * owners * rows * width * cols,
            bytes_accessed=40 * 2**20,
            transcendentals=0,
        ),
        name="last",
    )(
        grads,
        weight,
        tokens,
        grad_hidden,
        gain,
        out_term,
        gain_mlp,
        gain_heads,
        entry_all,
    )


def in_rows_kernel(grads_ref, out_ref):
    units = out_ref.shape[2]
    grads = grads_ref[0].reshape(-1, 2 * units).astype(F32)
    out_ref[:, 0, :] = grads[:, :units]
    out_ref[:, 1, :] = grads[:, units:]


def in_rows(grads):
    owners, reps, share, cols = grads.shape
    units = cols // 2
    return pl.pallas_call(
        in_rows_kernel,
        grid=(owners,),
        out_shape=jax.ShapeDtypeStruct((reps * share, 2, owners * units), F32),
        in_specs=[pl.BlockSpec((1, reps, share, cols), lambda e: (e, 0, 0, 0))],
        out_specs=pl.BlockSpec((reps * share, 2, units), lambda e: (0, 0, e)),
        compiler_params=pltpu.CompilerParams(vmem_limit_bytes=40 * 2**20),
        name="in_rows",
    )(grads)


def qkvg_rows_kernel(groups, grads_ref, out_ref, buf, sem):
    e = pl.program_id(0)
    owners = pl.num_programs(0)

    def copies(e):
        slot = e % 2
        for i, (base, at, cols) in enumerate(groups):
            yield pltpu.make_async_copy(
                buf.at[slot, :, pl.ds(at, cols)],
                out_ref.at[:, pl.ds(pl.multiple_of(base + e * cols, HEAD_SIZE), cols)],
                sem.at[slot, i],
            )

    @pl.when(e >= 2)
    def _():
        for copy in copies(e - 2):
            copy.wait()

    buf[e % 2] = grads_ref[0].reshape(buf.shape[1:]).astype(F32)
    for copy in copies(e):
        copy.start()

    @pl.when(e == owners - 1)
    def _():
        for late in (e - 1, e):
            for copy in copies(late):
                copy.wait()


def qkvg_rows(grads, heads, kv_heads):
    owners, reps, share, cols = grads.shape
    q_cols, kv_cols = heads * HEAD_SIZE, kv_heads * HEAD_SIZE
    groups, base, at = [], 0, 0
    for width in (q_cols, q_cols, kv_cols, kv_cols):
        groups.append((base, at, width))
        base += width * owners
        at += width
    return pl.pallas_call(
        functools.partial(qkvg_rows_kernel, tuple(groups)),
        grid=(owners,),
        out_shape=jax.ShapeDtypeStruct((reps * share, owners * cols), F32),
        in_specs=[pl.BlockSpec((1, reps, share, cols), lambda e: (e, 0, 0, 0))],
        out_specs=anywhere(),
        scratch_shapes=[
            pltpu.VMEM((2, reps * share, cols), F32),
            pltpu.SemaphoreType.DMA((2, len(groups))),
        ],
        compiler_params=pltpu.CompilerParams(vmem_limit_bytes=40 * 2**20),
        name="qkvg_rows",
    )(grads)


def positions_of(block_ids):
    offsets = jnp.arange(BLOCK_TOKENS, dtype=jnp.int32)
    return (block_ids[:, :, None] * BLOCK_TOKENS + offsets[None, None, :]).reshape(
        block_ids.shape[0], -1
    )


def body(
    tokens,
    block_map,
    w_qkvg,
    w_out,
    w_in,
    w_down,
    norm_attn,
    norm_query,
    norm_key,
    norm_mlp,
    cotangent,
):
    owners = lax.axis_size("grp")
    me = lax.axis_index("grp")
    heads = QUERY_HEADS // owners
    sharers = max(1, owners // KEY_VALUE_HEADS)
    kv_heads = KEY_VALUE_HEADS * sharers // owners
    per_kv = heads // kv_heads
    q_cols = heads * HEAD_SIZE
    kv_cols = kv_heads * HEAD_SIZE
    rows_here, width = tokens.shape
    shard = w_qkvg.shape[0]
    block_rows = 2 * BLOCK_TOKENS
    seq_len = owners * block_rows
    all_q = QUERY_HEADS * HEAD_SIZE
    all_kv = KEY_VALUE_HEADS * HEAD_SIZE
    hidden_units = w_down.shape[0]

    reps = lax.axis_size("rep")
    share = shard // reps
    in_pieces = lax.dynamic_slice_in_dim(w_in, lax.axis_index("rep") * share, share, 0)
    in_pieces = in_pieces.reshape(share, 2, owners, hidden_units).transpose(2, 0, 1, 3)
    in_pieces = in_pieces.reshape(owners, share, 2 * hidden_units)
    head_part = norm_query.shape[0]
    spread = jnp.zeros((2, HEAD_SIZE), jnp.float32)
    spread = lax.dynamic_update_slice(
        spread, jnp.stack([norm_query, norm_key]).astype(jnp.float32), (0, me * head_part)
    )
    small = jnp.concatenate(
        [norm_attn.astype(jnp.float32), norm_mlp.astype(jnp.float32), spread.reshape(-1)]
    )[None]

    positions = positions_of(block_map)
    table = rotary_table(positions)
    table = table.reshape(GROUP_SEQUENCES, owners, block_rows, HEAD_SIZE)
    table = jnp.swapaxes(table, 0, 1).reshape(owners, rows_here, HEAD_SIZE)
    (
        attn_input,
        query_raw,
        gate_raw,
        key_raw,
        value_rows,
        query_rot,
        key_rot,
        qkvg_cols,
        small_all,
    ) = first(
        owners,
        reps,
        heads,
        kv_heads,
        sharers,
        tokens,
        w_qkvg,
        small,
        table,
    )
    small_all = small_all[:, 0]
    gain_attn = small_all[:, :shard].reshape(-1)
    gain_mlp = small_all[:, shard : 2 * shard].reshape(-1)
    spread = jnp.sum(small_all[:, 2 * shard :], axis=0)
    attn_out, hidden, mlp_own, cotangent_all, in_cols = attention(
        owners,
        reps,
        heads,
        kv_heads,
        tokens,
        query_rot,
        key_rot,
        value_rows,
        gate_raw,
        block_map,
        positions[:, None, :],
        w_out,
        gain_mlp[None],
        cotangent,
        in_pieces,
    )
    in_cols = in_cols.reshape(width, -1)
    (
        mlp_input,
        activated,
        grad_gate_up,
        grad_hidden,
        branch_own,
        gain_mlp_sum,
        rows_down,
    ) = mlp(
        owners, reps, mlp_own, cotangent_all, in_cols, w_down, hidden, cotangent, gain_mlp[None]
    )
    _, output, grad_projected, gain_heads_sum, out_term, rows_in = backward(
        owners,
        reps,
        heads,
        kv_heads,
        branch_own,
        activated.reshape(owners, rows_here, hidden_units),
        w_down,
        w_out,
        hidden,
        query_raw,
        query_rot,
        gate_raw,
        key_raw,
        key_rot,
        value_rows,
        block_map,
        positions[:, None, :],
        table,
        spread[None],
        attn_out,
        grad_gate_up.reshape(owners, rows_here, 2 * hidden_units),
        mlp_input.reshape(owners, rows_here, width),
    )
    grad_tokens, gains, rows_qkvg, rows_out = last(
        owners,
        reps,
        grad_projected,
        qkvg_cols.reshape(width, -1),
        tokens,
        grad_hidden,
        gain_attn[None],
        out_term,
        gain_mlp_sum,
        gain_heads_sum,
        attn_input,
    )
    shard_in = in_rows(rows_in)
    shard_down = rows_down.reshape(w_down.shape).astype(jnp.float32)
    shard_out = rows_out.reshape(w_out.shape).astype(jnp.float32)
    if sharers == 1:
        shard_qkvg = qkvg_rows(rows_qkvg, heads, kv_heads)
    else:
        rows_qkvg = rows_qkvg.reshape(owners, shard, -1).swapaxes(0, 1).astype(jnp.float32)
        queries = [rows_qkvg[:, :, i * q_cols : (i + 1) * q_cols] for i in range(2)]
        others = [
            rows_qkvg[:, :, 2 * q_cols + i * kv_cols : 2 * q_cols + (i + 1) * kv_cols]
            .reshape(shard, owners // sharers, sharers, kv_cols)
            .sum(2)
            for i in range(2)
        ]
        shard_qkvg = jnp.concatenate(
            [part.reshape(shard, -1) for part in queries + others], axis=1
        )
    return (
        output,
        grad_tokens,
        shard_qkvg,
        shard_out,
        shard_in,
        shard_down,
        gains[0, :shard],
        lax.dynamic_slice_in_dim(gains[0], 2 * shard + me * head_part, head_part),
        lax.dynamic_slice_in_dim(gains[0], 2 * shard + HEAD_SIZE + me * head_part, head_part),
        gains[0, shard : 2 * shard],
    )


def solution(mesh):
    placed = (
        P(("rep", "grp"), None),
        P("rep", None),
        P("grp", None),
        P("grp", None),
        P("grp", None, None),
        P("grp", None),
        P("grp"),
        P("grp"),
        P("grp"),
        P("grp"),
        P(("rep", "grp"), None),
    )
    return jax.shard_map(
        body,
        mesh=mesh,
        in_specs=placed,
        out_specs=(
            P(("rep", "grp"), None),
            P(("rep", "grp"), None),
            P("grp", None),
            P("grp", None),
            P("grp", None, None),
            P("grp", None),
            P("grp"),
            P("grp"),
            P("grp"),
            P("grp"),
        ),
        check_vma=False,
    )
```

```python
import functools

import jax
import jax.numpy as jnp
from jax import lax
from jax.experimental import pallas as pl
from jax.experimental.pallas import tpu as pltpu
from jax.sharding import PartitionSpec as P

QUERY_HEADS = 16
KEY_VALUE_HEADS = 8
HEAD_SIZE = 128
BLOCK_TOKENS = 64
GROUP_SEQUENCES = 2


norm_epsilon = 1e-06
rotary_base = 1000000.0
masked_value = -1e30


def rotary_table(positions):
    exponent = jnp.arange(HEAD_SIZE // 2, dtype=jnp.float32) * (2.0 / HEAD_SIZE)
    inverse = jnp.power(jnp.float32(rotary_base), -exponent)
    angle = positions.astype(jnp.float32)[..., None] * inverse
    return jnp.concatenate([jnp.cos(angle), jnp.sin(angle)], axis=-1)


MESH = pl.DeviceIdType.MESH
F32 = jnp.float32
BF16 = jnp.bfloat16


def nearest(place, step, chips):
    low = jnp.minimum(place, chips - 1 - place)
    near = (step + 1) // 2
    side = jnp.where(2 * place < chips, near, -near)
    both = jnp.where(step % 2 == 1, place + side, place - side)
    past = step - low
    rest = jnp.where(place > chips - 1 - place, place - past, place + past)
    return jnp.where(step <= 2 * low, both, rest)


def meet(owners, reps):
    barrier = pltpu.get_barrier_semaphore()
    me, rep = lax.axis_index("grp"), lax.axis_index("rep")
    for ahead in range(1, owners):
        pl.semaphore_signal(
            barrier, 1, device_id={"grp": lax.rem(me + ahead, owners)}, device_id_type=MESH
        )
    for ahead in range(1, reps):
        pl.semaphore_signal(
            barrier, 1, device_id={"rep": lax.rem(rep + ahead, reps)}, device_id_type=MESH
        )
    pl.semaphore_wait(barrier, owners + reps - 2)


def to_grp(source, target, send, recv, device):
    return pltpu.make_async_remote_copy(
        src_ref=source,
        dst_ref=target,
        send_sem=send,
        recv_sem=recv,
        device_id={"grp": device},
        device_id_type=MESH,
    )


def to_rep(source, target, send, recv, device):
    return pltpu.make_async_remote_copy(
        src_ref=source,
        dst_ref=target,
        send_sem=send,
        recv_sem=recv,
        device_id={"rep": device},
        device_id_type=MESH,
    )


def arrived(ref, sem):
    pltpu.make_async_copy(ref, ref, sem).wait()


def dot(a, b):
    return jnp.dot(a, b, preferred_element_type=F32)


def dot_nt(a, b):
    return lax.dot_general(a, b, (((1,), (1,)), ((), ())), preferred_element_type=F32)


def dot_tn(a, b):
    return lax.dot_general(a, b, (((0,), (0,)), ((), ())), preferred_element_type=F32)


class Gather:
    def __init__(self, owners, buf, send, recv, half=0):
        self.owners, self.chips = owners, owners // 2
        self.me = lax.axis_index("grp")
        self.place, self.core = self.me // 2, self.me % 2
        self.buf, self.send, self.recv, self.half = buf, send, recv, half

    def of(self, block):
        return self.buf.at[block, self.half] if len(self.buf.shape) == 4 else self.buf.at[block]

    def sent(self, way, at):
        return self.send.at[self.half, way, at]

    def got(self, block):
        return self.recv.at[self.half, block]

    def copies(self, block, source=None):
        src = self.of(block) if source is None else source
        at = block // 2
        ways = (
            ((at <= self.place) & (self.place < self.chips - 1), self.me + 2),
            ((at >= self.place) & (self.place > 0), self.me - 2),
            (None, self.me + 1 - 2 * self.core),
        )
        return [
            (
                when,
                to_grp(src, self.of(block), self.sent(way, at), self.got(block), device),
            )
            for way, (when, device) in enumerate(ways)
        ]

    def forward(self, block, source=None):
        for when, copy in self.copies(block, source):
            if when is None:
                copy.start()
            else:
                pl.when(when)(copy.start)

    def step(self, k):
        block = 2 * nearest(self.place, k, self.chips) + self.core
        arrived(self.of(block), self.got(block))
        self.forward(block)

    def sibling(self, k):
        block = 2 * nearest(self.place, k, self.chips) + 1 - self.core
        arrived(self.of(block), self.got(block))

    def finish(self):
        def one(at, _):
            for when, copy in self.copies(2 * at + self.core):
                if when is None:
                    copy.wait_send()
                else:
                    pl.when(when)(copy.wait_send)
            return 0

        lax.fori_loop(0, self.chips, one, 0)

    @staticmethod
    def scratch(owners, halves=1):
        return [
            pltpu.SemaphoreType.DMA((halves, 3, owners // 2)),
            pltpu.SemaphoreType.DMA((halves, owners)),
        ]


class FarGather:
    def __init__(self, owners, buf, send, recv, parts):
        self.owners, self.chips, self.parts = owners, owners // 2, parts
        self.me = lax.axis_index("grp")
        self.place, self.core = self.me // 2, self.me % 2
        self.buf, self.send, self.recv = buf, send, recv
        self.part = buf.shape[1] // parts
        self.devices = (self.me + 2, self.me - 2, self.me + 1 - 2 * self.core)

    def rows(self, part):
        return pl.ds(part * self.part, self.part)

    def copy(self, way, block, part):
        ref = self.buf.at[block, self.rows(part)]
        return to_grp(
            ref,
            ref,
            self.send.at[way, block // 2, part],
            self.recv.at[block, part],
            self.devices[way],
        )

    def own(self, way):
        for part in range(self.parts):
            self.copy(way, self.me, part).start()

    def begin(self):
        self.own(2)
        pl.when(self.place == 0)(lambda: self.own(0))
        pl.when(self.place == self.chips - 1)(lambda: self.own(1))

    def pass_on(self, way, at, part, onward):
        block = 2 * at + self.core
        arrived(self.buf.at[block, self.rows(part)], self.recv.at[block, part])
        pl.when(onward)(lambda: self.copy(way, block, part).start())
        self.copy(2, block, part).start()

    def up(self, r, part):
        pl.when(r < self.place)(
            lambda: self.pass_on(0, r, part, self.place < self.chips - 1)
        )

    def down(self, r, part):
        at = self.chips - 1 - r
        pl.when(at > self.place)(lambda: self.pass_on(1, at, part, self.place > 0))

    def round(self, r):
        def flows(ahead, behind):
            ahead(r, 0)
            for part in range(1, self.parts):
                ahead(r, part)
                behind(r, part - 1)
            behind(r, self.parts - 1)

        lower = 2 * self.place < self.chips
        pl.when(lower)(lambda: flows(self.up, self.down))
        pl.when(jnp.logical_not(lower))(lambda: flows(self.down, self.up))
        last = self.chips - 1
        pl.when((r == self.place - 1) & (self.place < last))(lambda: self.own(0))
        pl.when((last - r == self.place + 1) & (self.place > 0))(lambda: self.own(1))

    def sibling(self, at):
        block = 2 * at + 1 - self.core
        for part in range(self.parts):
            arrived(self.buf.at[block, self.rows(part)], self.recv.at[block, part])

    def finish(self):
        last = self.chips - 1

        def one(at, _):
            block = 2 * at + self.core
            for part in range(self.parts):
                for way, when in (
                    (0, (at <= self.place) & (self.place < last)),
                    (1, (at >= self.place) & (self.place > 0)),
                ):
                    pl.when(when)(
                        lambda way=way, part=part: self.copy(way, block, part).wait_send()
                    )
                self.copy(2, block, part).wait_send()
            return 0

        lax.fori_loop(0, self.chips, one, 0)

    @staticmethod
    def scratch(owners, parts):
        return [
            pltpu.SemaphoreType.DMA((3, owners // 2, parts)),
            pltpu.SemaphoreType.DMA((owners, parts)),
        ]


class Reshard:
    def __init__(self, owners, reps, buf, sems):
        self.owners, self.reps = owners, reps
        self.me, self.rep = lax.axis_index("grp"), lax.axis_index("rep")
        self.buf = buf
        self.send1, self.recv1, self.send2, self.recv2 = sems

    def start(self, pieces):
        for source, columns in pieces(self.me):
            pltpu.make_async_copy(
                source, self.buf.at[self.me, self.rep, :, columns], self.recv1.at[self.me]
            ).start()

        def one(ahead, _):
            device = lax.rem(self.me + ahead, self.owners)
            for source, columns in pieces(device):
                to_grp(
                    source,
                    self.buf.at[self.me, self.rep, :, columns],
                    self.send1.at[device],
                    self.recv1.at[self.me],
                    device,
                ).start()
            return 0

        lax.fori_loop(1, self.owners, one, 0)

    def relay(self):
        def one(ahead, _):
            owner = lax.rem(self.me + ahead, self.owners)
            part = self.buf.at[owner, self.rep]
            arrived(part, self.recv1.at[owner])
            for other in range(1, self.reps):
                to_rep(
                    part,
                    part,
                    self.send2.at[other],
                    self.recv2.at[other],
                    lax.rem(self.rep + other, self.reps),
                ).start()
            return 0

        lax.fori_loop(0, self.owners, one, 0)

    def wait(self):
        for other in range(1, self.reps):
            source = lax.rem(self.rep + self.reps - other, self.reps)
            arrived(self.buf.at[:, source], self.recv2.at[other])

    def finish(self):
        def one(ahead, _):
            device = lax.rem(self.me + ahead, self.owners)
            arrived(self.buf.at[device, self.rep], self.send1.at[device])
            return 0

        lax.fori_loop(1, self.owners, one, 0)
        for other in range(1, self.reps):
            arrived(self.buf.at[:, self.rep], self.send2.at[other])

    @staticmethod
    def scratch(owners, reps):
        return [
            pltpu.SemaphoreType.DMA((owners,)),
            pltpu.SemaphoreType.DMA((owners,)),
            pltpu.SemaphoreType.DMA((reps,)),
            pltpu.SemaphoreType.DMA((reps,)),
        ]


def query_positions(map_ref, s, at):
    row = lax.broadcasted_iota(jnp.int32, (2 * BLOCK_TOKENS, 1), 0)
    return row + jnp.where(
        row < BLOCK_TOKENS,
        map_ref[s, 2 * at] * BLOCK_TOKENS,
        (map_ref[s, 2 * at + 1] - 1) * BLOCK_TOKENS,
    )


def angles(table):
    turned = pltpu.roll(table, HEAD_SIZE // 2, 1)
    low = lax.broadcasted_iota(jnp.int32, table.shape, 1) < HEAD_SIZE // 2
    return jnp.where(low, table, turned), jnp.where(low, -turned, table)


def head_norm(values):
    scale = lax.rsqrt(jnp.mean(values * values, axis=-1, keepdims=True) + norm_epsilon)
    return values * scale, scale


def turn(values, cosine, sine):
    return values * cosine + pltpu.roll(values, HEAD_SIZE // 2, 1) * sine


def turn_back(values, cosine, sine):
    return values * cosine - pltpu.roll(values, HEAD_SIZE // 2, 1) * sine


def first_kernel(
    owners,
    reps,
    heads,
    kv_heads,
    sharers,
    tokens_ref,
    weight_ref,
    small_ref,
    table_ref,
    input_out,
    query_out,
    gate_out,
    key_out,
    value_out,
    query_rot_out,
    key_rot_out,
    columns_out,
    small_out,
    buf,
    weight_buf,
    small_send,
    small_recv,
    local_sem,
    out_sem,
    g_send,
    g_recv,
    *r_sems,
):
    me, rep = lax.axis_index("grp"), lax.axis_index("rep")
    rows, width = tokens_ref.shape
    shard = weight_ref.shape[0]
    share = shard // reps
    q_cols, kv_cols = heads * HEAD_SIZE, kv_heads * HEAD_SIZE
    all_q = QUERY_HEADS * HEAD_SIZE
    all_kv = KEY_VALUE_HEADS * HEAD_SIZE
    gather = Gather(owners, buf, g_send, g_recv)
    reshard = Reshard(owners, reps, weight_buf, r_sems)
    my_rows = pl.ds(pl.multiple_of(rep * share, share), share)

    def pieces(owner):
        out = []
        at = 0
        for base, cols, step in (
            (0, q_cols, owner),
            (all_q, q_cols, owner),
            (2 * all_q, kv_cols, owner // sharers),
            (2 * all_q + all_kv, kv_cols, owner // sharers),
        ):
            first = pl.multiple_of(base + step * cols, HEAD_SIZE)
            out.append((weight_ref.at[my_rows, pl.ds(first, cols)], pl.ds(at, cols)))
            at += cols
        return out

    own = pltpu.make_async_copy(tokens_ref, buf.at[me], local_sem)
    own.start()
    small_out[me] = small_ref[...]
    meet(owners, reps)
    reshard.start(pieces)

    def small_copy(device, index):
        return to_grp(
            small_ref, small_out.at[me], small_send.at[index], small_recv.at[index], device
        )

    for ahead in range(1, owners):
        small_copy(lax.rem(me + ahead, owners), ahead).start()
    gather.forward(me, tokens_ref)
    reshard.relay()
    for ahead in range(1, owners):
        source = lax.rem(me + owners - ahead, owners)
        arrived(small_out.at[source], small_recv.at[ahead])
    own.wait()
    middle = (gather.place > 0) & (gather.place < gather.chips - 1)
    early = jnp.where(middle, gather.chips, gather.chips - 1)

    def step(k, _):
        gather.step(k)
        return 0

    lax.fori_loop(1, early, step, 0)
    reshard.wait()
    columns_copy = pltpu.make_async_copy(weight_buf, columns_out, out_sem)
    columns_copy.start()

    gain = jnp.concatenate([small_out[e][:, :shard] for e in range(owners)], axis=1)
    heads_gain = small_out[0][:, 2 * shard :]
    for e in range(1, owners):
        heads_gain = heads_gain + small_out[e][:, 2 * shard :]
    gain_query = heads_gain[:, :HEAD_SIZE]
    gain_key = heads_gain[:, HEAD_SIZE:]
    total_cols = 2 * q_cols + 2 * kv_cols
    weight = weight_buf.reshape(width, total_cols)

    def block(k, _):
        @pl.when(k >= early)
        def _():
            gather.step(k)

        def core(which, _):
            mine = which == 0

            @pl.when(which == 1)
            def _():
                gather.sibling(k)

            at = 2 * nearest(gather.place, k, gather.chips) + jnp.where(
                mine, gather.core, 1 - gather.core
            )
            values = buf[at].astype(F32)
            normed, _unused = head_norm(values)
            entry = (normed * gain).astype(BF16)
            input_out[at] = entry
            projected = dot(entry, weight[...])
            cosine, sine = angles(table_ref[at])
            for h in range(heads):
                span = slice(h * HEAD_SIZE, (h + 1) * HEAD_SIZE)
                raw = projected[:, span]
                query_out[at, :, span] = raw
                query_rot_out[at, :, span] = turn(
                    head_norm(raw)[0] * gain_query, cosine, sine
                ).astype(BF16)
            gate_out[at] = projected[:, q_cols : 2 * q_cols]
            for h in range(kv_heads):
                span = slice(h * HEAD_SIZE, (h + 1) * HEAD_SIZE)
                raw = projected[:, 2 * q_cols + h * HEAD_SIZE : 2 * q_cols + (h + 1) * HEAD_SIZE]
                key_out[at, :, span] = raw
                key_rot_out[at, :, span] = turn(
                    head_norm(raw)[0] * gain_key, cosine, sine
                ).astype(BF16)
            value_out[at] = projected[:, 2 * q_cols + kv_cols :].astype(BF16)
            return 0

        lax.fori_loop(0, 2, core, 0)
        return 0

    lax.fori_loop(0, gather.chips, block, 0)
    columns_copy.wait()
    gather.finish()
    reshard.finish()
    for ahead in range(1, owners):
        small_copy(lax.rem(me + ahead, owners), ahead).wait_send()


def vmem():
    return pl.BlockSpec(memory_space=pltpu.VMEM)


def smem():
    return pl.BlockSpec(memory_space=pltpu.SMEM)


def anywhere():
    return pl.BlockSpec(memory_space=pl.ANY)


def first(owners, reps, heads, kv_heads, sharers, tokens, w_qkvg, small, table):
    rows, width = tokens.shape
    shard = w_qkvg.shape[0]
    q_cols, kv_cols = heads * HEAD_SIZE, kv_heads * HEAD_SIZE
    cols = 2 * q_cols + 2 * kv_cols
    shape = jax.ShapeDtypeStruct
    outs = (
        shape((owners, rows, width), BF16),
        shape((owners, rows, q_cols), F32),
        shape((owners, rows, q_cols), F32),
        shape((owners, rows, kv_cols), F32),
        shape((owners, rows, kv_cols), BF16),
        shape((owners, rows, q_cols), BF16),
        shape((owners, rows, kv_cols), BF16),
        shape((owners, reps, shard // reps, cols), BF16),
        shape((owners,) + small.shape, F32),
    )
    flops = 2 * owners * rows * width * cols
    return pl.pallas_call(
        functools.partial(first_kernel, owners, reps, heads, kv_heads, sharers),
        out_shape=outs,
        in_specs=[anywhere(), anywhere(), vmem(), vmem()],
        out_specs=(vmem(),) * 7 + (anywhere(), vmem()),
        scratch_shapes=[
            pltpu.VMEM((owners, rows, width), BF16),
            pltpu.VMEM((owners, reps, shard // reps, cols), BF16),
            pltpu.SemaphoreType.DMA((owners,)),
            pltpu.SemaphoreType.DMA((owners,)),
            pltpu.SemaphoreType.DMA,
            pltpu.SemaphoreType.DMA,
        ]
        + Gather.scratch(owners)
        + Reshard.scratch(owners, reps),
        compiler_params=pltpu.CompilerParams(
            collective_id=0, has_side_effects=True, vmem_limit_bytes=60 * 2**20
        ),
        cost_estimate=pl.CostEstimate(
            flops=flops, bytes_accessed=40 * 2**20, transcendentals=0
        ),
        name="first",
    )(tokens, w_qkvg, small, table)


def by_distance(place, step, chips):
    return nearest(place, chips - 1 - step, chips)


class Scatter:
    def __init__(self, owners, bufs, sems, order, parts, half=0):
        self.owners, self.chips = owners, owners // 2
        self.me = lax.axis_index("grp")
        self.place, self.core = self.me // 2, self.me % 2
        self.stage, self.near, self.line, self.both = bufs
        self.acc = self.both.at[self.core]
        self.near_send, self.near_recv, self.line_send, self.line_recv = sems
        self.order, self.parts, self.half = order, parts, half
        self.part = self.both.shape[1] // parts

    def at(self, k):
        return self.order(self.place, k, self.chips)

    def near_copy(self, k):
        at = self.at(k)
        return to_grp(
            self.stage.at[self.half, k % 2],
            self.near.at[self.half, at],
            self.near_send.at[self.half, k % 2],
            self.near_recv.at[self.half, at],
            self.me + 1 - 2 * self.core,
        )

    def rows(self, s):
        return pl.ds(s * self.part, self.part)

    def line_copy(self, at, s):
        target = self.place + jnp.where(at > self.place, 1, -1)
        slot = jnp.where((target == at) & (at < self.place), self.chips, at)
        return to_grp(
            self.near.at[self.half, at, self.rows(s)],
            self.line.at[self.half, slot, self.rows(s)],
            self.line_send.at[self.half, at, s],
            self.line_recv.at[self.half, slot, s],
            2 * target + self.core,
        )

    def prepare(self, k, term):
        @pl.when(k >= 2)
        def _():
            self.near_copy(k - 2).wait_send()

        self.both[...] = term(self.at(k)).reshape(self.both.shape)
        self.stage[self.half, k % 2] = self.both[1 - self.core].astype(BF16)
        self.near_copy(k).start()

    def add(self, slot, s):
        part = self.line.at[self.half, slot, self.rows(s)]
        arrived(part, self.line_recv.at[self.half, slot, s])
        self.acc[self.rows(s)] += part[...].astype(F32)

    def combine(self, k):
        at = self.at(k)
        arrived(self.near.at[self.half, at], self.near_recv.at[self.half, at])
        self.acc[...] += self.near[self.half, at].astype(F32)
        below = self.place > 0
        above = self.place < self.chips - 1

        def one(s, _):
            @pl.when(((at >= self.place) & below) | ((at < self.place) & above))
            def _():
                self.add(at, s)

            @pl.when((at == self.place) & above)
            def _():
                self.add(self.chips, s)

            @pl.when(at != self.place)
            def _():
                self.near[self.half, at, self.rows(s)] = self.acc[self.rows(s)].astype(BF16)
                self.line_copy(at, s).start()

            return 0

        lax.fori_loop(0, self.parts, one, 0)

    def finish(self):
        self.near_copy(self.chips - 2).wait_send()
        self.near_copy(self.chips - 1).wait_send()

        def one(at, _):
            @pl.when(at != self.place)
            def _():
                for s in range(self.parts):
                    self.line_copy(at, s).wait_send()

            return 0

        lax.fori_loop(0, self.chips, one, 0)

    @staticmethod
    def scratch(owners, rows, width, parts, halves=1):
        chips = owners // 2
        rows //= halves
        return [
            pltpu.VMEM((halves, 2, rows, width), BF16),
            pltpu.VMEM((halves, chips, rows, width), BF16),
            pltpu.VMEM((halves, chips + 1, rows, width), BF16),
            pltpu.VMEM((2, rows, width), F32),
            pltpu.SemaphoreType.DMA((halves, 2)),
            pltpu.SemaphoreType.DMA((halves, chips)),
            pltpu.SemaphoreType.DMA((halves, chips, parts)),
            pltpu.SemaphoreType.DMA((halves, chips + 1, parts)),
        ]


PARTS = 4


class RepSum:
    def __init__(self, owners, reps, units, along, held, came, result, sems):
        self.owners, self.reps, self.units, self.along = owners, reps, units, along
        self.me, self.rep = lax.axis_index("grp"), lax.axis_index("rep")
        self.bits = reps.bit_length() - 1
        self.held, self.came, self.result = held, came, result
        self.down_send, self.down_recv, self.own_send, self.own_recv, self.up_send, self.up_recv = sems

    def weight(self, t, j):
        which = (t + j) % self.bits
        return sum(jnp.where(which == b, 1 << b, 0) for b in range(self.bits))

    @staticmethod
    def flip(index, weight):
        return index + weight * (1 - 2 * ((index // weight) % 2))

    def spread(self, index, t, bits):
        out = [index]
        for j in bits:
            out += [self.flip(i, self.weight(t, j)) for i in out]
        return out

    def unit(self, t):
        return lax.rem(self.me + t, self.owners) if self.along else t

    def source(self, t):
        return lax.rem(self.me + self.owners - t, self.owners) if self.along else t

    def downs(self, t, j):
        u = self.unit(t)
        first_index = sum(1 << (self.bits - 1 - i) for i in range(j))
        partner = self.flip(self.rep, self.weight(t, j))
        return [
            to_rep(
                self.held.at[u, s],
                self.came.at[u, first_index + c],
                self.down_send.at[u, first_index + c],
                self.down_recv.at[u, first_index + c],
                partner,
            )
            for c, s in enumerate(self.spread(partner, t, range(j + 1, self.bits)))
        ]

    def ups(self, t, j):
        e = self.source(t)
        held = self.spread(self.rep, t, range(self.bits - 1, self.bits - 1 - j, -1))
        partner = self.flip(self.rep, self.weight(t, self.bits - 1 - j))
        return [
            to_rep(
                self.result.at[e, s],
                self.result.at[e, s],
                self.up_send.at[e, (1 << j) - 1 + c],
                self.up_recv.at[e, s],
                partner,
            )
            for c, s in enumerate(held)
        ]

    def deliver(self, t, sent=False):
        u = self.unit(t)
        source = self.held.at[u, self.rep]
        slot = self.me if self.along else u
        target = self.result.at[slot, self.rep]

        def local():
            if not sent:
                pltpu.make_async_copy(source, target, self.own_recv.at[slot]).start()

        def remote():
            copy = to_grp(source, target, self.own_send.at[u], self.own_recv.at[slot], u)
            copy.wait_send() if sent else copy.start()

        if self.along:
            pl.when(u == self.me)(local)
            pl.when(u != self.me)(remote)
        else:
            local()

    def tick(self, t, term):
        def phase(step, more=0):
            return (t >= LAG * step + more) & (t < self.units + LAG * step + more)

        @pl.when(phase(0))
        def _():
            u = self.unit(t)
            self.held[u] = term(t, u).astype(BF16).reshape(self.held.shape[1:])
            for copy in self.downs(t, 0):
                copy.start()

        for j in range(1, self.bits + 1):

            @pl.when(phase(j))
            def _(j=j, t=t - LAG * j):
                u = self.unit(t)
                first_index = sum(1 << (self.bits - 1 - i) for i in range(j - 1))
                for c, s in enumerate(self.spread(self.rep, t, range(j, self.bits))):
                    part = self.came.at[u, first_index + c]
                    arrived(part, self.down_recv.at[u, first_index + c])
                    self.held[u, s] = (self.held[u, s].astype(F32) + part[...].astype(F32)).astype(
                        BF16
                    )
                if j < self.bits:
                    for copy in self.downs(t, j):
                        copy.start()
                else:
                    self.deliver(t)

        for j in range(self.bits + 1):

            @pl.when(phase(self.bits + 1 + j, FAR_LAG))
            def _(j=j, t=t - LAG * (self.bits + 1 + j) - FAR_LAG):
                e = self.source(t)
                if j == 0:
                    arrived(self.result.at[e, self.rep], self.own_recv.at[e])
                else:
                    bit = self.bits - j
                    held = self.spread(self.rep, t, range(self.bits - 1, bit, -1))
                    for s in held:
                        s = self.flip(s, self.weight(t, bit))
                        arrived(self.result.at[e, s], self.up_recv.at[e, s])
                if j < self.bits:
                    for copy in self.ups(t, j):
                        copy.start()

    def ticks(self):
        return self.units + LAG * (2 * self.bits + 1) + FAR_LAG

    def finish(self):
        def one(t, _):
            for j in range(self.bits):
                for copy in self.downs(t, j) + self.ups(t, j):
                    copy.wait_send()
            self.deliver(t, True)
            return 0

        lax.fori_loop(0, self.units, one, 0)

    @staticmethod
    def scratch(reps, units, share, cols):
        dma = pltpu.SemaphoreType.DMA
        return [
            pltpu.VMEM((units, reps, share, cols), BF16),
            pltpu.VMEM((units, reps - 1, share, cols), BF16),
            dma((units, reps - 1)),
            dma((units, reps - 1)),
            dma((units,)),
            dma((units,)),
            dma((units, reps - 1)),
            dma((units, reps)),
        ]


def staged(scatter, chips, k, term, work):
    middle = (scatter.place > 0) & (scatter.place < chips - 1)
    scatter.prepare(k, term)

    @pl.when(~middle)
    def _():
        scatter.combine(k)

    work()

    @pl.when(middle)
    def _():
        scatter.combine(k)


LAG = 2
FAR_LAG = 0


def interleave(gather, scatter, term, ready=None, then=None):
    chips = gather.chips
    middle = (gather.place > 0) & (gather.place < chips - 1)

    def stage(k, _):
        if ready is not None:
            ready(k)

        def work():
            then(k)

            @pl.when((~middle) & (k + 1 < chips))
            def _():
                gather.step(k + 1)

            @pl.when(middle & (2 * k + 1 < chips))
            def _():
                gather.step(2 * k + 1)

            @pl.when(middle & (2 * k + 2 < chips))
            def _():
                gather.step(2 * k + 2)

        staged(scatter, chips, k, term, work)
        return 0

    lax.fori_loop(0, chips, stage, 0)


def attention_kernel(
    owners,
    reps,
    heads,
    kv_heads,
    tokens_ref,
    query_ref,
    key_ref,
    value_ref,
    gate_ref,
    map_ref,
    position_row_ref,
    out_ref,
    gain_ref,
    cotangent_ref,
    in_pieces_ref,
    attn_out,
    hidden_out,
    entry_out,
    cotangent_out,
    columns_out,
    local_sem,
    *rest,
):
    me, rep = lax.axis_index("grp"), lax.axis_index("rep")
    scatter = Scatter(owners, rest[:4], rest[4:8], by_distance, PARTS)
    gather = Gather(owners, cotangent_out, *rest[8:10])
    reshard = Reshard(owners, reps, columns_out, rest[10:14])
    cols = in_pieces_ref.shape[2]

    def pieces(owner):
        return [(in_pieces_ref.at[owner], pl.ds(0, cols))]

    own = pltpu.make_async_copy(cotangent_ref, cotangent_out.at[me], local_sem)
    own.start()
    meet(owners, reps)
    gather.forward(me, cotangent_ref)
    reshard.start(pieces)
    per_kv = heads // kv_heads
    block_rows = 2 * BLOCK_TOKENS

    def attend(at):
        for s in range(GROUP_SEQUENCES):
            rows = slice(s * block_rows, (s + 1) * block_rows)
            allowed = position_row_ref[s] <= query_positions(map_ref, s, at)
            allowed = jnp.concatenate([allowed] * per_kv, axis=0)
            for kv in range(kv_heads):
                span = slice(kv * HEAD_SIZE, (kv + 1) * HEAD_SIZE)
                spans = [
                    slice(h * HEAD_SIZE, (h + 1) * HEAD_SIZE)
                    for h in range(kv * per_kv, (kv + 1) * per_kv)
                ]
                query = jnp.concatenate([query_ref[at, rows, h] for h in spans], axis=0)
                keys = key_ref[:, rows, span].reshape(-1, HEAD_SIZE)
                values = value_ref[:, rows, span].reshape(-1, HEAD_SIZE)
                scores = dot_nt(query, keys) * HEAD_SIZE ** (-0.5)
                scores = jnp.where(allowed, scores, masked_value)
                exps = jnp.exp(scores - jnp.max(scores, axis=-1, keepdims=True))
                probability = exps / jnp.sum(exps, axis=-1, keepdims=True)
                attended = dot(probability.astype(BF16), values)
                for i, h in enumerate(spans):
                    gated = attended[i * block_rows : (i + 1) * block_rows] * jax.nn.sigmoid(
                        gate_ref[at, rows, h]
                    )
                    attn_out[at, rows, h] = gated.astype(BF16)

    def ready(k):
        at = scatter.at(k)

        def one(core, _):
            attend(2 * at + core)
            return 0

        lax.fori_loop(0, 2, one, 0)

    def term(at):
        both = attn_out[pl.ds(2 * at, 2)]
        return dot(both.reshape(-1, both.shape[-1]), out_ref[...])

    def then(k):
        pl.when(k == 0)(reshard.relay)
        gather.sibling(k)

    interleave(gather, scatter, term, ready, then)
    hidden = tokens_ref[...].astype(F32) + scatter.acc[...]
    hidden_out[...] = hidden
    entry_out[...] = (head_norm(hidden)[0] * gain_ref[...]).astype(BF16)
    own.wait()
    reshard.wait()
    gather.finish()
    scatter.finish()
    reshard.finish()


def attention(
    owners,
    reps,
    heads,
    kv_heads,
    tokens,
    query_rot,
    key_rot,
    value_rows,
    gate_raw,
    block_map,
    position_row,
    w_out,
    gain_mlp,
    cotangent,
    in_pieces,
):
    rows, width = tokens.shape
    shape = jax.ShapeDtypeStruct
    share = in_pieces.shape[1]
    outs = (
        shape(query_rot.shape, BF16),
        shape((rows, width), F32),
        shape((rows, width), BF16),
        shape((owners, rows, width), BF16),
        shape((owners, reps, share, in_pieces.shape[2]), BF16),
    )
    return pl.pallas_call(
        functools.partial(attention_kernel, owners, reps, heads, kv_heads),
        out_shape=outs,
        in_specs=[vmem()] * 5 + [smem()] + [vmem()] * 3 + [anywhere()] * 2,
        out_specs=(vmem(),) * 3 + (anywhere(),) * 2,
        scratch_shapes=[pltpu.SemaphoreType.DMA]
        + Scatter.scratch(owners, rows, width, PARTS)
        + Gather.scratch(owners)
        + Reshard.scratch(owners, reps),
        compiler_params=pltpu.CompilerParams(
            collective_id=1, has_side_effects=True, vmem_limit_bytes=60 * 2**20
        ),
        cost_estimate=pl.CostEstimate(
            flops=4 * owners * rows * width * query_rot.shape[2],
            bytes_accessed=40 * 2**20,
            transcendentals=0,
        ),
        name="attention",
    )(
        tokens,
        query_rot,
        key_rot,
        value_rows,
        gate_raw,
        block_map,
        position_row,
        w_out,
        gain_mlp,
        cotangent,
        in_pieces,
    )


def mlp_kernel(
    owners,
    reps,
    entry_ref,
    cotangent_all_ref,
    in_ref,
    down_ref,
    hidden_ref,
    cotangent_ref,
    gain_ref,
    entry_all,
    activated_out,
    grads_out,
    grad_hidden_out,
    grad_branch_out,
    gain_out,
    down_sum,
    entry_buf,
    cotangent_buf,
    activated_buf,
    local_sem,
    load_sem,
    store_sem,
    *rest,
):
    me = lax.axis_index("grp")
    chips = owners // 2
    gather = FarGather(owners, entry_all, *rest[8:10], PARTS)
    scatter = Scatter(owners, rest[:4], rest[4:8], by_distance, PARTS)
    units = down_ref.shape[0]
    middle = (gather.place > 0) & (gather.place < chips - 1)
    own = pltpu.make_async_copy(entry_ref, entry_all.at[me], local_sem)
    own.start()
    meet(owners, reps)
    own.wait()
    gather.begin()
    down_sum[...] = jnp.zeros_like(down_sum)

    def stores(at):
        return pltpu.make_async_copy(
            activated_buf, activated_out.at[pl.ds(2 * at, 2)], store_sem
        )

    def compute(at, first=False):
        pair = pl.ds(2 * at, 2)
        cotangent_load = pltpu.make_async_copy(
            cotangent_all_ref.at[pair], cotangent_buf, load_sem.at[1]
        )
        cotangent_load.start()
        gather.sibling(at)
        entry_load = pltpu.make_async_copy(entry_all.at[pair], entry_buf, load_sem.at[0])
        entry_load.start()
        cotangent_load.wait()
        cotangent = cotangent_buf[...].reshape(-1, cotangent_buf.shape[-1])
        grad_activated = dot_nt(cotangent, down_ref[...])
        entry_load.wait()
        gate_up = dot(entry_buf[...].reshape(-1, entry_buf.shape[-1]), in_ref[...])
        gate, up = gate_up[:, :units], gate_up[:, units:]
        sig = jax.nn.sigmoid(gate)
        silu = gate * sig
        if not first:
            stores(at).wait()
        activated = (silu * up).astype(BF16)
        shape = activated_buf.shape
        activated_buf[...] = activated.reshape(shape)
        stores(at).start()
        grads_out[pair, :, :units] = (
            (grad_activated * up * sig * (1.0 + gate * (1.0 - sig))).astype(BF16).reshape(shape)
        )
        grads_out[pair, :, units:] = (grad_activated * silu).astype(BF16).reshape(shape)
        down_sum[...] += dot_tn(activated, cotangent)

    def term(at):
        both = grads_out[pl.ds(2 * at, 2)]
        return dot_nt(both.reshape(-1, both.shape[-1]), in_ref[...])

    def step(r, _):
        gather.round(r)
        return 0

    lax.fori_loop(0, jnp.where(middle, chips - 1, 1), step, 0)
    stores(0).start()

    def compute_step(k, _):
        compute(jnp.where(k < 0, gather.place, scatter.at(jnp.maximum(k, 0))))
        return 0

    lax.fori_loop(jnp.where(middle, 0, -1), 1, compute_step, 0)

    def back(k, _):
        more = jnp.where(middle, k + 1 < chips, k + 1 < chips - 1)

        def work():
            @pl.when(more & (~middle))
            def _():
                gather.round(k + 1)

            @pl.when(more)
            def _():
                compute(scatter.at(k + 1))

        staged(scatter, chips, k, term, work)
        return 0

    lax.fori_loop(0, chips, back, 0)
    hidden_buf = scatter.both.at[1 - scatter.core]
    load_hidden = pltpu.make_async_copy(hidden_ref, hidden_buf, local_sem)
    load_hidden.start()
    load_hidden.wait()
    hidden = hidden_buf[...]
    normed, scale = head_norm(hidden)
    grad_entry = scatter.acc[...]
    gain_out[...] = jnp.sum(grad_entry * normed, axis=0, keepdims=True)
    weighted = grad_entry * gain_ref[...]
    grad_hidden = cotangent_ref[...].astype(F32) + scale * (
        weighted - normed * jnp.mean(weighted * normed, axis=-1, keepdims=True)
    )
    grad_hidden_out[...] = grad_hidden
    grad_branch_out[...] = grad_hidden.astype(BF16)
    stores(0).wait()
    gather.finish()
    scatter.finish()


def mlp(owners, reps, entry, cotangent_all, in_cols, w_down, hidden, cotangent, gain_mlp):
    rows, width = entry.shape
    units = w_down.shape[0]
    shape = jax.ShapeDtypeStruct
    outs = (
        shape((owners, rows, width), BF16),
        shape((owners, rows, units), BF16),
        shape((owners, rows, 2 * units), BF16),
        shape((rows, width), F32),
        shape((rows, width), BF16),
        shape((1, width), F32),
        shape((units, width), F32),
    )
    return pl.pallas_call(
        functools.partial(mlp_kernel, owners, reps),
        out_shape=outs,
        in_specs=[anywhere()] * 2 + [vmem()] * 2 + [anywhere()] + [vmem()] * 2,
        out_specs=(anywhere(),) * 2 + (vmem(),) * 5,
        scratch_shapes=[
            pltpu.VMEM((2, rows, width), BF16),
            pltpu.VMEM((2, rows, width), BF16),
            pltpu.VMEM((2, rows, units), BF16),
            pltpu.SemaphoreType.DMA,
            pltpu.SemaphoreType.DMA((2,)),
            pltpu.SemaphoreType.DMA,
        ]
        + Scatter.scratch(owners, rows, width, PARTS)
        + FarGather.scratch(owners, PARTS),
        compiler_params=pltpu.CompilerParams(
            collective_id=2, has_side_effects=True, vmem_limit_bytes=63 * 2**20
        ),
        cost_estimate=pl.CostEstimate(
            flops=12 * owners * rows * width * units,
            bytes_accessed=40 * 2**20,
            transcendentals=0,
        ),
        name="mlp",
    )(entry, cotangent_all, in_cols, w_down, hidden, cotangent, gain_mlp)


def unturned_norm_back(grad, raw, gain, cosine, sine):
    back = turn_back(grad, cosine, sine)
    normed, scale = head_norm(raw)
    weighted = back * gain
    grad_raw = scale * (weighted - normed * jnp.mean(weighted * normed, axis=-1, keepdims=True))
    return grad_raw, jnp.sum(back * normed, axis=0, keepdims=True)


def backward_kernel(
    owners,
    reps,
    heads,
    kv_heads,
    branch_ref,
    activated_ref,
    down_ref,
    out_ref,
    hidden_ref,
    query_ref,
    query_rot_ref,
    gate_ref,
    key_ref,
    key_rot_ref,
    value_ref,
    map_ref,
    position_row_ref,
    table_ref,
    heads_gain_ref,
    attn_out_ref,
    grad_gate_up_ref,
    entry_ref,
    branch_all,
    output_out,
    grads_out,
    gain_out,
    out_term,
    weight_out,
    branch_buf,
    key_sum,
    value_sum,
    entry_buf,
    activated_buf,
    attn_buf,
    grad_attn_buf,
    gate_buf,
    local_sem,
    load_sem,
    activated_sem,
    gate_sem,
    entry_sem,
    *rest,
):
    me = lax.axis_index("grp")
    chips = owners // 2
    scatter = Scatter(owners, rest[:4], rest[4:8], by_distance, PARTS)
    gather = Gather(owners, branch_all, *rest[8:10])
    columns = RepSum(owners, reps, owners, True, rest[10], rest[11], weight_out, rest[12:18])
    load_columns = column_loads(entry_ref, entry_buf, entry_sem, entry_buf.shape[-1])
    load_columns(0, me).start()
    columns_of = columns_term(
        columns,
        load_columns,
        entry_buf,
        lambda: grad_gate_up_ref[...].reshape(-1, grad_gate_up_ref.shape[-1]),
    )

    def tick(t):
        columns.tick(t, columns_of)
    own = pltpu.make_async_copy(branch_ref, branch_all.at[me], local_sem)
    own.start()
    meet(owners, reps)
    gather.forward(me, branch_ref)
    own.wait()
    key_sum[...] = jnp.zeros_like(key_sum)
    value_sum[...] = jnp.zeros_like(value_sum)
    gain_out[...] = jnp.zeros_like(gain_out)
    out_term[...] = jnp.zeros_like(out_term)
    per_kv = heads // kv_heads
    q_cols, kv_cols = heads * HEAD_SIZE, kv_heads * HEAD_SIZE
    block_rows = 2 * BLOCK_TOKENS
    root = HEAD_SIZE ** (-0.5)
    gain_query = heads_gain_ref[:, :HEAD_SIZE]
    gain_key = heads_gain_ref[:, HEAD_SIZE:]

    def block(at, which):
        grad_attn_out = grad_attn_buf[which]
        for s in range(GROUP_SEQUENCES):
            rows = slice(s * block_rows, (s + 1) * block_rows)
            cosine, sine = angles(table_ref[at, rows])
            allowed = position_row_ref[s] <= query_positions(map_ref, s, at)
            allowed = jnp.concatenate([allowed] * per_kv, axis=0)
            for kv in range(kv_heads):
                span = slice(kv * HEAD_SIZE, (kv + 1) * HEAD_SIZE)
                spans = [
                    slice(h * HEAD_SIZE, (h + 1) * HEAD_SIZE)
                    for h in range(kv * per_kv, (kv + 1) * per_kv)
                ]
                query = jnp.concatenate([query_rot_ref[at, rows, h] for h in spans], axis=0)
                keys = key_rot_ref[:, rows, span].reshape(-1, HEAD_SIZE)
                values = value_ref[:, rows, span].reshape(-1, HEAD_SIZE)
                scores = dot_nt(query, keys) * root
                scores = jnp.where(allowed, scores, masked_value)
                exps = jnp.exp(scores - jnp.max(scores, axis=-1, keepdims=True))
                exact = exps / jnp.sum(exps, axis=-1, keepdims=True)
                low = exact.astype(BF16)
                attended = dot(low, values)
                inputs = []
                for i, h in enumerate(spans):
                    grad = grad_attn_out[rows, h]
                    sig = jax.nn.sigmoid(gate_buf[which, rows, h])
                    inputs.append((grad * sig).astype(BF16))
                    gated = slice(q_cols + h.start, q_cols + h.stop)
                    grads_out[at, rows, gated] = (
                        grad
                        * attended[i * block_rows : (i + 1) * block_rows]
                        * sig
                        * (1.0 - sig)
                    ).astype(BF16)
                grad_attended = jnp.concatenate(inputs, axis=0)
                grad_probs = dot_nt(grad_attended, values)
                inner = jnp.sum(exact * grad_probs, axis=-1, keepdims=True)
                grad_scores = (exact * (grad_probs - inner)).astype(BF16)
                grad_query = dot(grad_scores, keys) * root
                key_sum[s, kv] += dot_tn(grad_scores, query)
                value_sum[s, kv] += dot_tn(low, grad_attended)
                for i, h in enumerate(spans):
                    grad_raw, gain_sum = unturned_norm_back(
                        grad_query[i * block_rows : (i + 1) * block_rows],
                        query_ref[at, rows, h],
                        gain_query,
                        cosine,
                        sine,
                    )
                    grads_out[at, rows, h] = grad_raw.astype(BF16)
                    gain_out[:, :HEAD_SIZE] += gain_sum

    def load_activated(k):
        pair = pl.ds(2 * scatter.at(k), 2)
        return pltpu.make_async_copy(activated_ref.at[pair], activated_buf, activated_sem)

    load_activated(0).start()

    def term(at):
        load_activated(0).wait()
        both = activated_buf[...]
        return dot(both.reshape(-1, both.shape[-1]), down_ref[...])

    def then(k):
        @pl.when(k + 1 < chips)
        def _():
            load_activated(k + 1).start()

        at = nearest(gather.place, k, chips)
        pair = pl.ds(2 * at, 2)
        gather.sibling(k)
        load = pltpu.make_async_copy(branch_all.at[pair], branch_buf, load_sem)
        load_attn = pltpu.make_async_copy(attn_out_ref.at[pair], attn_buf, local_sem)
        load_gate = pltpu.make_async_copy(gate_ref.at[pair], gate_buf, gate_sem)
        load.start()
        load_attn.start()
        load_gate.start()
        tick(TICKS * k)
        load.wait()
        load_attn.wait()
        load_gate.wait()
        branch = branch_buf[...].reshape(-1, branch_buf.shape[-1])
        grad_attn_buf[...] = dot_nt(branch, out_ref[...]).reshape(grad_attn_buf.shape)
        out_term[...] += dot_tn(attn_buf[...].reshape(-1, attn_buf.shape[-1]), branch)

        def one(which, _):
            block(2 * at + which, which)
            late_tick(TICKS * k + 1 + TICKS // 2 * which)
            return 0

        lax.fori_loop(0, 2, one, 0)

    def late_tick(t):
        def two(t, _):
            tick(t)
            return 0

        lax.fori_loop(t, t + TICKS // 2, two, 0)

    interleave(gather, scatter, term, then=then)
    hidden = scatter.both.at[1 - scatter.core]
    load_hidden = pltpu.make_async_copy(hidden_ref, hidden, local_sem)
    load_hidden.start()
    load_hidden.wait()
    output_out[...] = (hidden[...] + scatter.acc[...]).astype(BF16)

    key_raw = scatter.both.at[0]

    def key_columns(at):
        return pl.ds(pl.multiple_of(at * kv_cols, HEAD_SIZE), kv_cols)

    def load_keys(at, _):
        pltpu.make_async_copy(key_ref.at[at], key_raw.at[:, key_columns(at)], load_sem).start()
        return 0

    lax.fori_loop(0, owners, load_keys, 0)
    arrived(key_raw.at[:, pl.ds(0, owners * kv_cols)], load_sem)

    def keys(at, _):
        for s in range(GROUP_SEQUENCES):
            rows = slice(s * block_rows, (s + 1) * block_rows)
            for kv in range(kv_heads):
                span = slice(kv * HEAD_SIZE, (kv + 1) * HEAD_SIZE)
                place = pl.ds(pl.multiple_of(at * block_rows, block_rows), block_rows)
                grad_raw, gain_sum = unturned_norm_back(
                    key_sum[s, kv, place] * root,
                    key_raw[
                        rows, pl.ds(pl.multiple_of(at * kv_cols, HEAD_SIZE) + span.start, HEAD_SIZE)
                    ],
                    gain_key,
                    *angles(table_ref[at, rows]),
                )
                first_col = 2 * q_cols + kv * HEAD_SIZE
                grads_out[at, rows, first_col : first_col + HEAD_SIZE] = grad_raw.astype(BF16)
                first_col += kv_cols
                grads_out[at, rows, first_col : first_col + HEAD_SIZE] = value_sum[
                    s, kv, place
                ].astype(BF16)
                gain_out[:, HEAD_SIZE:] += gain_sum
        return 0

    lax.fori_loop(0, owners, keys, 0)

    def late(t, _):
        tick(t)
        return 0

    lax.fori_loop(TICKS * chips, columns.ticks(), late, 0)
    gather.finish()
    scatter.finish()
    columns.finish()


VMEM_LIMIT = 63 * 2**20 + 2**19


def backward(
    owners,
    reps,
    heads,
    kv_heads,
    branch,
    activated,
    w_down,
    w_out,
    hidden,
    query_raw,
    query_rot,
    gate_raw,
    key_raw,
    key_rot,
    value_rows,
    block_map,
    position_row,
    table,
    heads_gain,
    attn_out,
    grad_gate_up,
    entry_all,
):
    rows, width = branch.shape
    cols = 2 * (heads + kv_heads) * HEAD_SIZE
    seq_len = position_row.shape[-1]
    shard = width // owners
    shape = jax.ShapeDtypeStruct
    outs = (
        shape((owners, rows, width), BF16),
        shape((rows, width), BF16),
        shape((owners, rows, cols), BF16),
        shape((1, 2 * HEAD_SIZE), F32),
        shape(w_out.shape, F32),
        shape((owners, reps, shard // reps, grad_gate_up.shape[2]), BF16),
    )
    return pl.pallas_call(
        functools.partial(backward_kernel, owners, reps, heads, kv_heads),
        out_shape=outs,
        in_specs=[anywhere()] * 2
        + [vmem()] * 2
        + [anywhere()]
        + [vmem()] * 2
        + [anywhere()] * 2
        + [vmem()] * 2
        + [smem()]
        + [vmem()] * 3
        + [anywhere()]
        + [vmem()]
        + [anywhere()],
        out_specs=(anywhere(),) + (vmem(),) * 4 + (anywhere(),),
        scratch_shapes=[
            pltpu.VMEM((2, rows, width), BF16),
            pltpu.VMEM((GROUP_SEQUENCES, kv_heads, seq_len, HEAD_SIZE), F32),
            pltpu.VMEM((GROUP_SEQUENCES, kv_heads, seq_len, HEAD_SIZE), F32),
            pltpu.VMEM((2, owners, rows, shard), BF16),
            pltpu.VMEM((2,) + activated.shape[1:], BF16),
            pltpu.VMEM((2,) + attn_out.shape[1:], BF16),
            pltpu.VMEM((2,) + attn_out.shape[1:], F32),
            pltpu.VMEM((2,) + attn_out.shape[1:], F32),
            pltpu.SemaphoreType.DMA,
            pltpu.SemaphoreType.DMA,
            pltpu.SemaphoreType.DMA,
            pltpu.SemaphoreType.DMA,
            pltpu.SemaphoreType.DMA((2,)),
        ]
        + Scatter.scratch(owners, rows, width, PARTS)
        + Gather.scratch(owners)
        + RepSum.scratch(reps, owners, shard // reps, grad_gate_up.shape[2]),
        compiler_params=pltpu.CompilerParams(
            collective_id=3, has_side_effects=True, vmem_limit_bytes=VMEM_LIMIT
        ),
        cost_estimate=pl.CostEstimate(
            flops=4 * owners * rows * width * cols,
            bytes_accessed=40 * 2**20,
            transcendentals=0,
        ),
        name="backward",
    )(
        branch,
        activated,
        w_down,
        w_out,
        hidden,
        query_raw,
        query_rot,
        gate_raw,
        key_raw,
        key_rot,
        value_rows,
        block_map,
        position_row,
        table,
        heads_gain,
        attn_out,
        grad_gate_up,
        entry_all,
    )


def column_loads(source_ref, buf, sem, shard):
    def load(slot, u):
        columns = pl.ds(pl.multiple_of(u * shard, shard), shard)
        return pltpu.make_async_copy(source_ref.at[:, :, columns], buf.at[slot], sem.at[slot])

    return load


def columns_term(total, load, buf, grads):
    def term(t, u):
        @pl.when(t + 1 < total.units)
        def _():
            load((t + 1) % 2, total.unit(t + 1)).start()

        load(t % 2, u).wait()
        entry = buf[t % 2]
        return dot_tn(entry.reshape(-1, entry.shape[-1]), grads())

    return term


def last_kernel(
    owners,
    reps,
    grads_ref,
    weight_ref,
    tokens_ref,
    grad_hidden_ref,
    gain_ref,
    out_term_ref,
    down_term_ref,
    gain_mlp_ref,
    gain_heads_ref,
    entry_ref,
    grad_out,
    gains_out,
    weight_out,
    rows_out,
    entry_buf,
    gains_send,
    gains_came,
    gains_all,
    load_sem,
    g_send,
    g_recv,
    r_send,
    r_recv,
    *rest,
):
    me, rep = lax.axis_index("grp"), lax.axis_index("rep")
    chips = owners // 2
    scatter = Scatter(owners, rest[:4], rest[4:8], by_distance, PARTS)
    columns = RepSum(owners, reps, owners, True, rest[8], rest[9], weight_out, rest[10:16])
    rows = RepSum(
        owners, reps, rows_out.shape[0], False, rest[16], rest[17], rows_out, rest[18:24]
    )
    shard = entry_buf.shape[-1]
    load = column_loads(entry_ref, entry_buf, load_sem, shard)
    load(0, me).start()
    meet(owners, reps)

    def flat(ref):
        return ref[...].reshape(-1, ref.shape[-1])

    columns_of = columns_term(columns, load, entry_buf, lambda: flat(grads_ref))

    down_units = down_term_ref.shape[0] // shard

    def rows_of(t, u):
        at = jnp.minimum(u, down_units - 1) * shard
        down = down_term_ref[pl.ds(pl.multiple_of(at, shard), shard)]
        return jnp.where(u < down_units, down, out_term_ref[...])

    def tick(t):
        rows.tick(t, rows_of)
        columns.tick(t, columns_of)

    def term(at):
        both = grads_ref[pl.ds(2 * at, 2)]
        return dot_nt(both.reshape(-1, both.shape[-1]), weight_ref[...])

    def stage(k, _):
        def one(t, _):
            tick(t)
            return 0

        staged(
            scatter,
            chips,
            k,
            term,
            lambda: lax.fori_loop(TICKS * k, TICKS * (k + 1), one, 0),
        )
        return 0

    lax.fori_loop(0, chips, stage, 0)
    grad = scatter.acc[...]
    normed, scale = head_norm(tokens_ref[...].astype(F32))
    gain_attn = jnp.sum(grad * normed, axis=0, keepdims=True)
    gain_mlp = gain_mlp_ref[...]
    for e in range(owners):
        span = slice(e * shard, (e + 1) * shard)
        gains_send[e] = jnp.concatenate(
            [gain_attn[:, span], gain_mlp[:, span], gain_heads_ref[...]], axis=1
        )

    def gains_copy(ahead):
        device = lax.rem(me + ahead, owners)
        return to_grp(
            gains_send.at[device],
            gains_came.at[me],
            g_send.at[ahead],
            g_recv.at[me],
            device,
        )

    def gains_up(ahead):
        return to_rep(
            gains_all.at[rep],
            gains_all.at[rep],
            r_send.at[ahead],
            r_recv.at[rep],
            lax.rem(rep + ahead, reps),
        )

    for ahead in range(1, owners):
        gains_copy(ahead).start()
    gains_came[me] = gains_send[me]
    weighted = grad * gain_ref[...]
    grad_out[...] = (
        grad_hidden_ref[...]
        + scale * (weighted - normed * jnp.mean(weighted * normed, axis=-1, keepdims=True))
    ).astype(BF16)
    for ahead in range(1, owners):
        source = lax.rem(me + ahead, owners)
        arrived(gains_came.at[source], g_recv.at[source])
    gains_all[rep] = jnp.sum(gains_came[...], axis=0)
    for ahead in range(1, reps):
        gains_up(ahead).start()

    def one(t, _):
        tick(t)
        return 0

    lax.fori_loop(TICKS * chips, max(columns.ticks(), rows.ticks()), one, 0)
    for ahead in range(1, reps):
        source = lax.rem(rep + ahead, reps)
        arrived(gains_all.at[source], r_recv.at[source])
    gains_out[...] = jnp.sum(gains_all[...], axis=0)
    for ahead in range(1, owners):
        gains_copy(ahead).wait_send()
    for ahead in range(1, reps):
        gains_up(ahead).wait_send()
    scatter.finish()
    columns.finish()
    rows.finish()


TICKS = 5


def last(
    owners,
    reps,
    grads,
    weight,
    tokens,
    grad_hidden,
    gain,
    out_term,
    down_term,
    gain_mlp,
    gain_heads,
    entry_all,
):
    rows, width = tokens.shape
    cols = grads.shape[2]
    shard = width // owners
    share = shard // reps
    small = 2 * shard + gain_heads.shape[1]
    units = (out_term.shape[0] + down_term.shape[0]) // shard
    shape = jax.ShapeDtypeStruct
    dma = pltpu.SemaphoreType.DMA
    return pl.pallas_call(
        functools.partial(last_kernel, owners, reps),
        out_shape=(
            shape((rows, width), BF16),
            shape((1, small), F32),
            shape((owners, reps, share, cols), BF16),
            shape((units, reps, share, width), BF16),
        ),
        in_specs=[vmem()] * 9 + [anywhere()],
        out_specs=(vmem(),) * 2 + (anywhere(),) * 2,
        scratch_shapes=[
            pltpu.VMEM((2, owners, rows, shard), BF16),
            pltpu.VMEM((owners, 1, small), F32),
            pltpu.VMEM((owners, 1, small), F32),
            pltpu.VMEM((reps, 1, small), F32),
            dma((2,)),
            dma((owners,)),
            dma((owners,)),
            dma((reps,)),
            dma((reps,)),
        ]
        + Scatter.scratch(owners, rows, width, PARTS)
        + RepSum.scratch(reps, owners, share, cols)
        + RepSum.scratch(reps, units, share, width),
        compiler_params=pltpu.CompilerParams(
            collective_id=4, has_side_effects=True, vmem_limit_bytes=60 * 2**20
        ),
        cost_estimate=pl.CostEstimate(
            flops=4 * owners * rows * width * cols,
            bytes_accessed=40 * 2**20,
            transcendentals=0,
        ),
        name="last",
    )(
        grads,
        weight,
        tokens,
        grad_hidden,
        gain,
        out_term,
        down_term,
        gain_mlp,
        gain_heads,
        entry_all,
    )


def in_rows_kernel(grads_ref, out_ref):
    units = out_ref.shape[2]
    grads = grads_ref[0].reshape(-1, 2 * units).astype(F32)
    out_ref[:, 0, :] = grads[:, :units]
    out_ref[:, 1, :] = grads[:, units:]


def in_rows(grads):
    owners, reps, share, cols = grads.shape
    units = cols // 2
    return pl.pallas_call(
        in_rows_kernel,
        grid=(owners,),
        out_shape=jax.ShapeDtypeStruct((reps * share, 2, owners * units), F32),
        in_specs=[pl.BlockSpec((1, reps, share, cols), lambda e: (e, 0, 0, 0))],
        out_specs=pl.BlockSpec((reps * share, 2, units), lambda e: (0, 0, e)),
        compiler_params=pltpu.CompilerParams(vmem_limit_bytes=40 * 2**20),
        name="in_rows",
    )(grads)


def qkvg_rows_kernel(groups, grads_ref, out_ref, buf, sem):
    e = pl.program_id(0)
    owners = pl.num_programs(0)

    def copies(e):
        slot = e % 2
        for i, (base, at, cols) in enumerate(groups):
            yield pltpu.make_async_copy(
                buf.at[slot, :, pl.ds(at, cols)],
                out_ref.at[:, pl.ds(pl.multiple_of(base + e * cols, HEAD_SIZE), cols)],
                sem.at[slot, i],
            )

    @pl.when(e >= 2)
    def _():
        for copy in copies(e - 2):
            copy.wait()

    buf[e % 2] = grads_ref[0].reshape(buf.shape[1:]).astype(F32)
    for copy in copies(e):
        copy.start()

    @pl.when(e == owners - 1)
    def _():
        for late in (e - 1, e):
            for copy in copies(late):
                copy.wait()


def qkvg_rows(grads, heads, kv_heads):
    owners, reps, share, cols = grads.shape
    q_cols, kv_cols = heads * HEAD_SIZE, kv_heads * HEAD_SIZE
    groups, base, at = [], 0, 0
    for width in (q_cols, q_cols, kv_cols, kv_cols):
        groups.append((base, at, width))
        base += width * owners
        at += width
    return pl.pallas_call(
        functools.partial(qkvg_rows_kernel, tuple(groups)),
        grid=(owners,),
        out_shape=jax.ShapeDtypeStruct((reps * share, owners * cols), F32),
        in_specs=[pl.BlockSpec((1, reps, share, cols), lambda e: (e, 0, 0, 0))],
        out_specs=anywhere(),
        scratch_shapes=[
            pltpu.VMEM((2, reps * share, cols), F32),
            pltpu.SemaphoreType.DMA((2, len(groups))),
        ],
        compiler_params=pltpu.CompilerParams(vmem_limit_bytes=40 * 2**20),
        name="qkvg_rows",
    )(grads)


def positions_of(block_ids):
    offsets = jnp.arange(BLOCK_TOKENS, dtype=jnp.int32)
    return (block_ids[:, :, None] * BLOCK_TOKENS + offsets[None, None, :]).reshape(
        block_ids.shape[0], -1
    )


def body(
    tokens,
    block_map,
    w_qkvg,
    w_out,
    w_in,
    w_down,
    norm_attn,
    norm_query,
    norm_key,
    norm_mlp,
    cotangent,
):
    owners = lax.axis_size("grp")
    me = lax.axis_index("grp")
    heads = QUERY_HEADS // owners
    sharers = max(1, owners // KEY_VALUE_HEADS)
    kv_heads = KEY_VALUE_HEADS * sharers // owners
    per_kv = heads // kv_heads
    q_cols = heads * HEAD_SIZE
    kv_cols = kv_heads * HEAD_SIZE
    rows_here, width = tokens.shape
    shard = w_qkvg.shape[0]
    block_rows = 2 * BLOCK_TOKENS
    seq_len = owners * block_rows
    all_q = QUERY_HEADS * HEAD_SIZE
    all_kv = KEY_VALUE_HEADS * HEAD_SIZE
    hidden_units = w_down.shape[0]

    reps = lax.axis_size("rep")
    share = shard // reps
    in_pieces = lax.dynamic_slice_in_dim(w_in, lax.axis_index("rep") * share, share, 0)
    in_pieces = in_pieces.reshape(share, 2, owners, hidden_units).transpose(2, 0, 1, 3)
    in_pieces = in_pieces.reshape(owners, share, 2 * hidden_units)
    head_part = norm_query.shape[0]
    spread = jnp.zeros((2, HEAD_SIZE), jnp.float32)
    spread = lax.dynamic_update_slice(
        spread, jnp.stack([norm_query, norm_key]).astype(jnp.float32), (0, me * head_part)
    )
    small = jnp.concatenate(
        [norm_attn.astype(jnp.float32), norm_mlp.astype(jnp.float32), spread.reshape(-1)]
    )[None]

    positions = positions_of(block_map)
    table = rotary_table(positions)
    table = table.reshape(GROUP_SEQUENCES, owners, block_rows, HEAD_SIZE)
    table = jnp.swapaxes(table, 0, 1).reshape(owners, rows_here, HEAD_SIZE)
    (
        attn_input,
        query_raw,
        gate_raw,
        key_raw,
        value_rows,
        query_rot,
        key_rot,
        qkvg_cols,
        small_all,
    ) = first(
        owners,
        reps,
        heads,
        kv_heads,
        sharers,
        tokens,
        w_qkvg,
        small,
        table,
    )
    small_all = small_all[:, 0]
    gain_attn = small_all[:, :shard].reshape(-1)
    gain_mlp = small_all[:, shard : 2 * shard].reshape(-1)
    spread = jnp.sum(small_all[:, 2 * shard :], axis=0)
    attn_out, hidden, mlp_own, cotangent_all, in_cols = attention(
        owners,
        reps,
        heads,
        kv_heads,
        tokens,
        query_rot,
        key_rot,
        value_rows,
        gate_raw,
        block_map,
        positions[:, None, :],
        w_out,
        gain_mlp[None],
        cotangent,
        in_pieces,
    )
    in_cols = in_cols.reshape(width, -1)
    (
        mlp_input,
        activated,
        grad_gate_up,
        grad_hidden,
        branch_own,
        gain_mlp_sum,
        down_term,
    ) = mlp(
        owners, reps, mlp_own, cotangent_all, in_cols, w_down, hidden, cotangent, gain_mlp[None]
    )
    _, output, grad_projected, gain_heads_sum, out_term, rows_in = backward(
        owners,
        reps,
        heads,
        kv_heads,
        branch_own,
        activated.reshape(owners, rows_here, hidden_units),
        w_down,
        w_out,
        hidden,
        query_raw,
        query_rot,
        gate_raw,
        key_raw,
        key_rot,
        value_rows,
        block_map,
        positions[:, None, :],
        table,
        spread[None],
        attn_out,
        grad_gate_up.reshape(owners, rows_here, 2 * hidden_units),
        mlp_input.reshape(owners, rows_here, width),
    )
    grad_tokens, gains, rows_qkvg, rows_both = last(
        owners,
        reps,
        grad_projected,
        qkvg_cols.reshape(width, -1),
        tokens,
        grad_hidden,
        gain_attn[None],
        out_term,
        down_term,
        gain_mlp_sum,
        gain_heads_sum,
        attn_input,
    )
    shard_in = in_rows(rows_in)
    rows_both = rows_both.reshape(-1, width).astype(jnp.float32)
    shard_down = rows_both[: w_down.shape[0]]
    shard_out = rows_both[w_down.shape[0] :]
    if sharers == 1:
        shard_qkvg = qkvg_rows(rows_qkvg, heads, kv_heads)
    else:
        rows_qkvg = rows_qkvg.reshape(owners, shard, -1).swapaxes(0, 1).astype(jnp.float32)
        queries = [rows_qkvg[:, :, i * q_cols : (i + 1) * q_cols] for i in range(2)]
        others = [
            rows_qkvg[:, :, 2 * q_cols + i * kv_cols : 2 * q_cols + (i + 1) * kv_cols]
            .reshape(shard, owners // sharers, sharers, kv_cols)
            .sum(2)
            for i in range(2)
        ]
        shard_qkvg = jnp.concatenate(
            [part.reshape(shard, -1) for part in queries + others], axis=1
        )
    return (
        output,
        grad_tokens,
        shard_qkvg,
        shard_out,
        shard_in,
        shard_down,
        gains[0, :shard],
        lax.dynamic_slice_in_dim(gains[0], 2 * shard + me * head_part, head_part),
        lax.dynamic_slice_in_dim(gains[0], 2 * shard + HEAD_SIZE + me * head_part, head_part),
        gains[0, shard : 2 * shard],
    )


def solution(mesh):
    placed = (
        P(("rep", "grp"), None),
        P("rep", None),
        P("grp", None),
        P("grp", None),
        P("grp", None, None),
        P("grp", None),
        P("grp"),
        P("grp"),
        P("grp"),
        P("grp"),
        P(("rep", "grp"), None),
    )
    return jax.shard_map(
        body,
        mesh=mesh,
        in_specs=placed,
        out_specs=(
            P(("rep", "grp"), None),
            P(("rep", "grp"), None),
            P("grp", None),
            P("grp", None),
            P("grp", None, None),
            P("grp", None),
            P("grp"),
            P("grp"),
            P("grp"),
            P("grp"),
        ),
        check_vma=False,
    )
```

```python
import functools

import jax
import jax.numpy as jnp
from jax import lax
from jax.experimental import pallas as pl
from jax.experimental.pallas import tpu as pltpu
from jax.sharding import PartitionSpec as P

QUERY_HEADS = 16
KEY_VALUE_HEADS = 8
HEAD_SIZE = 128
BLOCK_TOKENS = 64
GROUP_SEQUENCES = 2


norm_epsilon = 1e-06
rotary_base = 1000000.0
masked_value = -1e30


def rotary_table(positions):
    exponent = jnp.arange(HEAD_SIZE // 2, dtype=jnp.float32) * (2.0 / HEAD_SIZE)
    inverse = jnp.power(jnp.float32(rotary_base), -exponent)
    angle = positions.astype(jnp.float32)[..., None] * inverse
    return jnp.concatenate([jnp.cos(angle), jnp.sin(angle)], axis=-1)


MESH = pl.DeviceIdType.MESH
F32 = jnp.float32
BF16 = jnp.bfloat16


def nearest(place, step, chips):
    low = jnp.minimum(place, chips - 1 - place)
    near = (step + 1) // 2
    side = jnp.where(2 * place < chips, near, -near)
    both = jnp.where(step % 2 == 1, place + side, place - side)
    past = step - low
    rest = jnp.where(place > chips - 1 - place, place - past, place + past)
    return jnp.where(step <= 2 * low, both, rest)


def meet(owners, reps):
    barrier = pltpu.get_barrier_semaphore()
    me, rep = lax.axis_index("grp"), lax.axis_index("rep")
    for ahead in range(1, owners):
        pl.semaphore_signal(
            barrier, 1, device_id={"grp": lax.rem(me + ahead, owners)}, device_id_type=MESH
        )
    for ahead in range(1, reps):
        pl.semaphore_signal(
            barrier, 1, device_id={"rep": lax.rem(rep + ahead, reps)}, device_id_type=MESH
        )
    pl.semaphore_wait(barrier, owners + reps - 2)


def to_grp(source, target, send, recv, device):
    return pltpu.make_async_remote_copy(
        src_ref=source,
        dst_ref=target,
        send_sem=send,
        recv_sem=recv,
        device_id={"grp": device},
        device_id_type=MESH,
    )


def to_rep(source, target, send, recv, device):
    return pltpu.make_async_remote_copy(
        src_ref=source,
        dst_ref=target,
        send_sem=send,
        recv_sem=recv,
        device_id={"rep": device},
        device_id_type=MESH,
    )


def arrived(ref, sem):
    pltpu.make_async_copy(ref, ref, sem).wait()


def dot(a, b):
    return jnp.dot(a, b, preferred_element_type=F32)


def dot_nt(a, b):
    return lax.dot_general(a, b, (((1,), (1,)), ((), ())), preferred_element_type=F32)


def dot_tn(a, b):
    return lax.dot_general(a, b, (((0,), (0,)), ((), ())), preferred_element_type=F32)


class Gather:
    def __init__(self, owners, buf, send, recv, half=0):
        self.owners, self.chips = owners, owners // 2
        self.me = lax.axis_index("grp")
        self.place, self.core = self.me // 2, self.me % 2
        self.buf, self.send, self.recv, self.half = buf, send, recv, half

    def of(self, block):
        return self.buf.at[block, self.half] if len(self.buf.shape) == 4 else self.buf.at[block]

    def sent(self, way, at):
        return self.send.at[self.half, way, at]

    def got(self, block):
        return self.recv.at[self.half, block]

    def copies(self, block, source=None):
        src = self.of(block) if source is None else source
        at = block // 2
        ways = (
            ((at <= self.place) & (self.place < self.chips - 1), self.me + 2),
            ((at >= self.place) & (self.place > 0), self.me - 2),
            (None, self.me + 1 - 2 * self.core),
        )
        return [
            (
                when,
                to_grp(src, self.of(block), self.sent(way, at), self.got(block), device),
            )
            for way, (when, device) in enumerate(ways)
        ]

    def forward(self, block, source=None):
        for when, copy in self.copies(block, source):
            if when is None:
                copy.start()
            else:
                pl.when(when)(copy.start)

    def step(self, k):
        block = 2 * nearest(self.place, k, self.chips) + self.core
        arrived(self.of(block), self.got(block))
        self.forward(block)

    def sibling(self, k):
        block = 2 * nearest(self.place, k, self.chips) + 1 - self.core
        arrived(self.of(block), self.got(block))

    def finish(self):
        def one(at, _):
            for when, copy in self.copies(2 * at + self.core):
                if when is None:
                    copy.wait_send()
                else:
                    pl.when(when)(copy.wait_send)
            return 0

        lax.fori_loop(0, self.chips, one, 0)

    @staticmethod
    def scratch(owners, halves=1):
        return [
            pltpu.SemaphoreType.DMA((halves, 3, owners // 2)),
            pltpu.SemaphoreType.DMA((halves, owners)),
        ]


class FarGather:
    def __init__(self, owners, buf, send, recv, parts):
        self.owners, self.chips, self.parts = owners, owners // 2, parts
        self.me = lax.axis_index("grp")
        self.place, self.core = self.me // 2, self.me % 2
        self.buf, self.send, self.recv = buf, send, recv
        self.part = buf.shape[1] // parts
        self.devices = (self.me + 2, self.me - 2, self.me + 1 - 2 * self.core)

    def rows(self, part):
        return pl.ds(part * self.part, self.part)

    def copy(self, way, block, part):
        ref = self.buf.at[block, self.rows(part)]
        return to_grp(
            ref,
            ref,
            self.send.at[way, block // 2, part],
            self.recv.at[block, part],
            self.devices[way],
        )

    def own(self, way):
        for part in range(self.parts):
            self.copy(way, self.me, part).start()

    def begin(self):
        self.own(2)
        pl.when(self.place == 0)(lambda: self.own(0))
        pl.when(self.place == self.chips - 1)(lambda: self.own(1))

    def pass_on(self, way, at, part, onward):
        block = 2 * at + self.core
        arrived(self.buf.at[block, self.rows(part)], self.recv.at[block, part])
        pl.when(onward)(lambda: self.copy(way, block, part).start())
        self.copy(2, block, part).start()

    def up(self, r, part):
        pl.when(r < self.place)(
            lambda: self.pass_on(0, r, part, self.place < self.chips - 1)
        )

    def down(self, r, part):
        at = self.chips - 1 - r
        pl.when(at > self.place)(lambda: self.pass_on(1, at, part, self.place > 0))

    def round(self, r):
        def flows(ahead, behind):
            ahead(r, 0)
            for part in range(1, self.parts):
                ahead(r, part)
                behind(r, part - 1)
            behind(r, self.parts - 1)

        lower = 2 * self.place < self.chips
        pl.when(lower)(lambda: flows(self.up, self.down))
        pl.when(jnp.logical_not(lower))(lambda: flows(self.down, self.up))
        last = self.chips - 1
        pl.when((r == self.place - 1) & (self.place < last))(lambda: self.own(0))
        pl.when((last - r == self.place + 1) & (self.place > 0))(lambda: self.own(1))

    def sibling(self, at):
        block = 2 * at + 1 - self.core
        for part in range(self.parts):
            arrived(self.buf.at[block, self.rows(part)], self.recv.at[block, part])

    def finish(self):
        last = self.chips - 1

        def one(at, _):
            block = 2 * at + self.core
            for part in range(self.parts):
                for way, when in (
                    (0, (at <= self.place) & (self.place < last)),
                    (1, (at >= self.place) & (self.place > 0)),
                ):
                    pl.when(when)(
                        lambda way=way, part=part: self.copy(way, block, part).wait_send()
                    )
                self.copy(2, block, part).wait_send()
            return 0

        lax.fori_loop(0, self.chips, one, 0)

    @staticmethod
    def scratch(owners, parts):
        return [
            pltpu.SemaphoreType.DMA((3, owners // 2, parts)),
            pltpu.SemaphoreType.DMA((owners, parts)),
        ]


class Reshard:
    def __init__(self, owners, reps, buf, sems):
        self.owners, self.reps = owners, reps
        self.me, self.rep = lax.axis_index("grp"), lax.axis_index("rep")
        self.buf = buf
        self.send1, self.recv1, self.send2, self.recv2 = sems

    def start(self, pieces):
        for source, columns in pieces(self.me):
            pltpu.make_async_copy(
                source, self.buf.at[self.me, self.rep, :, columns], self.recv1.at[self.me]
            ).start()

        def one(ahead, _):
            device = lax.rem(self.me + ahead, self.owners)
            for source, columns in pieces(device):
                to_grp(
                    source,
                    self.buf.at[self.me, self.rep, :, columns],
                    self.send1.at[device],
                    self.recv1.at[self.me],
                    device,
                ).start()
            return 0

        lax.fori_loop(1, self.owners, one, 0)

    def relay(self):
        def one(ahead, _):
            owner = lax.rem(self.me + ahead, self.owners)
            part = self.buf.at[owner, self.rep]
            arrived(part, self.recv1.at[owner])
            for other in range(1, self.reps):
                to_rep(
                    part,
                    part,
                    self.send2.at[other],
                    self.recv2.at[other],
                    lax.rem(self.rep + other, self.reps),
                ).start()
            return 0

        lax.fori_loop(0, self.owners, one, 0)

    def wait(self):
        for other in range(1, self.reps):
            source = lax.rem(self.rep + self.reps - other, self.reps)
            arrived(self.buf.at[:, source], self.recv2.at[other])

    def finish(self):
        def one(ahead, _):
            device = lax.rem(self.me + ahead, self.owners)
            arrived(self.buf.at[device, self.rep], self.send1.at[device])
            return 0

        lax.fori_loop(1, self.owners, one, 0)
        for other in range(1, self.reps):
            arrived(self.buf.at[:, self.rep], self.send2.at[other])

    @staticmethod
    def scratch(owners, reps):
        return [
            pltpu.SemaphoreType.DMA((owners,)),
            pltpu.SemaphoreType.DMA((owners,)),
            pltpu.SemaphoreType.DMA((reps,)),
            pltpu.SemaphoreType.DMA((reps,)),
        ]


def query_positions(map_ref, s, at):
    row = lax.broadcasted_iota(jnp.int32, (2 * BLOCK_TOKENS, 1), 0)
    return row + jnp.where(
        row < BLOCK_TOKENS,
        map_ref[s, 2 * at] * BLOCK_TOKENS,
        (map_ref[s, 2 * at + 1] - 1) * BLOCK_TOKENS,
    )


def angles(table):
    turned = pltpu.roll(table, HEAD_SIZE // 2, 1)
    low = lax.broadcasted_iota(jnp.int32, table.shape, 1) < HEAD_SIZE // 2
    return jnp.where(low, table, turned), jnp.where(low, -turned, table)


def head_norm(values):
    scale = lax.rsqrt(jnp.mean(values * values, axis=-1, keepdims=True) + norm_epsilon)
    return values * scale, scale


def turn(values, cosine, sine):
    return values * cosine + pltpu.roll(values, HEAD_SIZE // 2, 1) * sine


def turn_back(values, cosine, sine):
    return values * cosine - pltpu.roll(values, HEAD_SIZE // 2, 1) * sine


def first_kernel(
    owners,
    reps,
    heads,
    kv_heads,
    sharers,
    tokens_ref,
    weight_ref,
    small_ref,
    table_ref,
    input_out,
    query_out,
    gate_out,
    key_out,
    value_out,
    query_rot_out,
    key_rot_out,
    columns_out,
    small_out,
    buf,
    weight_buf,
    small_send,
    small_recv,
    local_sem,
    out_sem,
    g_send,
    g_recv,
    *r_sems,
):
    me, rep = lax.axis_index("grp"), lax.axis_index("rep")
    rows, width = tokens_ref.shape
    shard = weight_ref.shape[0]
    share = shard // reps
    q_cols, kv_cols = heads * HEAD_SIZE, kv_heads * HEAD_SIZE
    all_q = QUERY_HEADS * HEAD_SIZE
    all_kv = KEY_VALUE_HEADS * HEAD_SIZE
    gather = Gather(owners, buf, g_send, g_recv)
    reshard = Reshard(owners, reps, weight_buf, r_sems)
    my_rows = pl.ds(pl.multiple_of(rep * share, share), share)

    def pieces(owner):
        out = []
        at = 0
        for base, cols, step in (
            (0, q_cols, owner),
            (all_q, q_cols, owner),
            (2 * all_q, kv_cols, owner // sharers),
            (2 * all_q + all_kv, kv_cols, owner // sharers),
        ):
            first = pl.multiple_of(base + step * cols, HEAD_SIZE)
            out.append((weight_ref.at[my_rows, pl.ds(first, cols)], pl.ds(at, cols)))
            at += cols
        return out

    own = pltpu.make_async_copy(tokens_ref, buf.at[me], local_sem)
    own.start()
    small_out[me] = small_ref[...]
    meet(owners, reps)
    reshard.start(pieces)

    def small_copy(device, index):
        return to_grp(
            small_ref, small_out.at[me], small_send.at[index], small_recv.at[index], device
        )

    for ahead in range(1, owners):
        small_copy(lax.rem(me + ahead, owners), ahead).start()
    gather.forward(me, tokens_ref)
    reshard.relay()
    for ahead in range(1, owners):
        source = lax.rem(me + owners - ahead, owners)
        arrived(small_out.at[source], small_recv.at[ahead])
    own.wait()
    middle = (gather.place > 0) & (gather.place < gather.chips - 1)
    early = jnp.where(middle, gather.chips, gather.chips - 1)

    def step(k, _):
        gather.step(k)
        return 0

    lax.fori_loop(1, early, step, 0)
    reshard.wait()
    columns_copy = pltpu.make_async_copy(weight_buf, columns_out, out_sem)
    columns_copy.start()

    gain = jnp.concatenate([small_out[e][:, :shard] for e in range(owners)], axis=1)
    heads_gain = small_out[0][:, 2 * shard :]
    for e in range(1, owners):
        heads_gain = heads_gain + small_out[e][:, 2 * shard :]
    gain_query = heads_gain[:, :HEAD_SIZE]
    gain_key = heads_gain[:, HEAD_SIZE:]
    total_cols = 2 * q_cols + 2 * kv_cols
    weight = weight_buf.reshape(width, total_cols)

    def block(k, _):
        @pl.when(k >= early)
        def _():
            gather.step(k)

        def core(which, _):
            mine = which == 0

            @pl.when(which == 1)
            def _():
                gather.sibling(k)

            at = 2 * nearest(gather.place, k, gather.chips) + jnp.where(
                mine, gather.core, 1 - gather.core
            )
            values = buf[at].astype(F32)
            normed, _unused = head_norm(values)
            entry = (normed * gain).astype(BF16)
            input_out[at] = entry
            projected = dot(entry, weight[...])
            cosine, sine = angles(table_ref[at])
            for h in range(heads):
                span = slice(h * HEAD_SIZE, (h + 1) * HEAD_SIZE)
                raw = projected[:, span]
                query_out[at, :, span] = raw
                query_rot_out[at, :, span] = turn(
                    head_norm(raw)[0] * gain_query, cosine, sine
                ).astype(BF16)
            gate_out[at] = projected[:, q_cols : 2 * q_cols]
            for h in range(kv_heads):
                span = slice(h * HEAD_SIZE, (h + 1) * HEAD_SIZE)
                raw = projected[:, 2 * q_cols + h * HEAD_SIZE : 2 * q_cols + (h + 1) * HEAD_SIZE]
                key_out[at, :, span] = raw
                key_rot_out[at, :, span] = turn(
                    head_norm(raw)[0] * gain_key, cosine, sine
                ).astype(BF16)
            value_out[at] = projected[:, 2 * q_cols + kv_cols :].astype(BF16)
            return 0

        lax.fori_loop(0, 2, core, 0)
        return 0

    lax.fori_loop(0, gather.chips, block, 0)
    columns_copy.wait()
    gather.finish()
    reshard.finish()
    for ahead in range(1, owners):
        small_copy(lax.rem(me + ahead, owners), ahead).wait_send()


def vmem():
    return pl.BlockSpec(memory_space=pltpu.VMEM)


def smem():
    return pl.BlockSpec(memory_space=pltpu.SMEM)


def anywhere():
    return pl.BlockSpec(memory_space=pl.ANY)


def first(owners, reps, heads, kv_heads, sharers, tokens, w_qkvg, small, table):
    rows, width = tokens.shape
    shard = w_qkvg.shape[0]
    q_cols, kv_cols = heads * HEAD_SIZE, kv_heads * HEAD_SIZE
    cols = 2 * q_cols + 2 * kv_cols
    shape = jax.ShapeDtypeStruct
    outs = (
        shape((owners, rows, width), BF16),
        shape((owners, rows, q_cols), F32),
        shape((owners, rows, q_cols), F32),
        shape((owners, rows, kv_cols), F32),
        shape((owners, rows, kv_cols), BF16),
        shape((owners, rows, q_cols), BF16),
        shape((owners, rows, kv_cols), BF16),
        shape((owners, reps, shard // reps, cols), BF16),
        shape((owners,) + small.shape, F32),
    )
    flops = 2 * owners * rows * width * cols
    return pl.pallas_call(
        functools.partial(first_kernel, owners, reps, heads, kv_heads, sharers),
        out_shape=outs,
        in_specs=[anywhere(), anywhere(), vmem(), vmem()],
        out_specs=(vmem(),) * 7 + (anywhere(), vmem()),
        scratch_shapes=[
            pltpu.VMEM((owners, rows, width), BF16),
            pltpu.VMEM((owners, reps, shard // reps, cols), BF16),
            pltpu.SemaphoreType.DMA((owners,)),
            pltpu.SemaphoreType.DMA((owners,)),
            pltpu.SemaphoreType.DMA,
            pltpu.SemaphoreType.DMA,
        ]
        + Gather.scratch(owners)
        + Reshard.scratch(owners, reps),
        compiler_params=pltpu.CompilerParams(
            collective_id=0, has_side_effects=True, vmem_limit_bytes=60 * 2**20
        ),
        cost_estimate=pl.CostEstimate(
            flops=flops, bytes_accessed=40 * 2**20, transcendentals=0
        ),
        name="first",
    )(tokens, w_qkvg, small, table)


def by_distance(place, step, chips):
    return nearest(place, chips - 1 - step, chips)


class Scatter:
    def __init__(self, owners, bufs, sems, order, parts, half=0):
        self.owners, self.chips = owners, owners // 2
        self.me = lax.axis_index("grp")
        self.place, self.core = self.me // 2, self.me % 2
        self.stage, self.near, self.line, self.both = bufs
        self.acc = self.both.at[self.core]
        self.near_send, self.near_recv, self.line_send, self.line_recv = sems
        self.order, self.parts, self.half = order, parts, half
        self.part = self.both.shape[1] // parts

    def at(self, k):
        return self.order(self.place, k, self.chips)

    def near_copy(self, k):
        at = self.at(k)
        return to_grp(
            self.stage.at[self.half, k % 2],
            self.near.at[self.half, at],
            self.near_send.at[self.half, k % 2],
            self.near_recv.at[self.half, at],
            self.me + 1 - 2 * self.core,
        )

    def rows(self, s):
        return pl.ds(s * self.part, self.part)

    def line_copy(self, at, s):
        target = self.place + jnp.where(at > self.place, 1, -1)
        slot = jnp.where((target == at) & (at < self.place), self.chips, at)
        return to_grp(
            self.near.at[self.half, at, self.rows(s)],
            self.line.at[self.half, slot, self.rows(s)],
            self.line_send.at[self.half, at, s],
            self.line_recv.at[self.half, slot, s],
            2 * target + self.core,
        )

    def prepare(self, k, term):
        @pl.when(k >= 2)
        def _():
            self.near_copy(k - 2).wait_send()

        self.both[...] = term(self.at(k)).reshape(self.both.shape)
        self.stage[self.half, k % 2] = self.both[1 - self.core].astype(BF16)
        self.near_copy(k).start()

    def add(self, slot, s):
        part = self.line.at[self.half, slot, self.rows(s)]
        arrived(part, self.line_recv.at[self.half, slot, s])
        self.acc[self.rows(s)] += part[...].astype(F32)

    def combine(self, k):
        at = self.at(k)
        arrived(self.near.at[self.half, at], self.near_recv.at[self.half, at])
        self.acc[...] += self.near[self.half, at].astype(F32)
        below = self.place > 0
        above = self.place < self.chips - 1

        def one(s, _):
            @pl.when(((at >= self.place) & below) | ((at < self.place) & above))
            def _():
                self.add(at, s)

            @pl.when((at == self.place) & above)
            def _():
                self.add(self.chips, s)

            @pl.when(at != self.place)
            def _():
                self.near[self.half, at, self.rows(s)] = self.acc[self.rows(s)].astype(BF16)
                self.line_copy(at, s).start()

            return 0

        lax.fori_loop(0, self.parts, one, 0)

    def finish(self):
        self.near_copy(self.chips - 2).wait_send()
        self.near_copy(self.chips - 1).wait_send()

        def one(at, _):
            @pl.when(at != self.place)
            def _():
                for s in range(self.parts):
                    self.line_copy(at, s).wait_send()

            return 0

        lax.fori_loop(0, self.chips, one, 0)

    @staticmethod
    def scratch(owners, rows, width, parts, halves=1):
        chips = owners // 2
        rows //= halves
        return [
            pltpu.VMEM((halves, 2, rows, width), BF16),
            pltpu.VMEM((halves, chips, rows, width), BF16),
            pltpu.VMEM((halves, chips + 1, rows, width), BF16),
            pltpu.VMEM((2, rows, width), F32),
            pltpu.SemaphoreType.DMA((halves, 2)),
            pltpu.SemaphoreType.DMA((halves, chips)),
            pltpu.SemaphoreType.DMA((halves, chips, parts)),
            pltpu.SemaphoreType.DMA((halves, chips + 1, parts)),
        ]


PARTS = 4


class RepSum:
    def __init__(self, owners, reps, units, along, held, came, result, sems):
        self.owners, self.reps, self.units, self.along = owners, reps, units, along
        self.me, self.rep = lax.axis_index("grp"), lax.axis_index("rep")
        self.bits = reps.bit_length() - 1
        self.held, self.came, self.result = held, came, result
        self.down_send, self.down_recv, self.own_send, self.own_recv, self.up_send, self.up_recv = sems

    def weight(self, t, j):
        which = (t + j) % self.bits
        return sum(jnp.where(which == b, 1 << b, 0) for b in range(self.bits))

    @staticmethod
    def flip(index, weight):
        return index + weight * (1 - 2 * ((index // weight) % 2))

    def spread(self, index, t, bits):
        out = [index]
        for j in bits:
            out += [self.flip(i, self.weight(t, j)) for i in out]
        return out

    def unit(self, t):
        return lax.rem(self.me + t, self.owners) if self.along else t

    def source(self, t):
        return lax.rem(self.me + self.owners - t, self.owners) if self.along else t

    def downs(self, t, j):
        u = self.unit(t)
        first_index = sum(1 << (self.bits - 1 - i) for i in range(j))
        partner = self.flip(self.rep, self.weight(t, j))
        return [
            to_rep(
                self.held.at[u, s],
                self.came.at[u, first_index + c],
                self.down_send.at[u, first_index + c],
                self.down_recv.at[u, first_index + c],
                partner,
            )
            for c, s in enumerate(self.spread(partner, t, range(j + 1, self.bits)))
        ]

    def ups(self, t, j):
        e = self.source(t)
        held = self.spread(self.rep, t, range(self.bits - 1, self.bits - 1 - j, -1))
        partner = self.flip(self.rep, self.weight(t, self.bits - 1 - j))
        return [
            to_rep(
                self.result.at[e, s],
                self.result.at[e, s],
                self.up_send.at[e, (1 << j) - 1 + c],
                self.up_recv.at[e, s],
                partner,
            )
            for c, s in enumerate(held)
        ]

    def deliver(self, t, sent=False):
        u = self.unit(t)
        source = self.held.at[u, self.rep]
        slot = self.me if self.along else u
        target = self.result.at[slot, self.rep]

        def local():
            if not sent:
                pltpu.make_async_copy(source, target, self.own_recv.at[slot]).start()

        def remote():
            copy = to_grp(source, target, self.own_send.at[u], self.own_recv.at[slot], u)
            copy.wait_send() if sent else copy.start()

        if self.along:
            pl.when(u == self.me)(local)
            pl.when(u != self.me)(remote)
        else:
            local()

    def tick(self, t, term):
        def phase(step, more=0):
            return (t >= LAG * step + more) & (t < self.units + LAG * step + more)

        @pl.when(phase(0))
        def _():
            u = self.unit(t)
            self.held[u] = term(t, u).astype(BF16).reshape(self.held.shape[1:])
            for copy in self.downs(t, 0):
                copy.start()

        for j in range(1, self.bits + 1):

            @pl.when(phase(j))
            def _(j=j, t=t - LAG * j):
                u = self.unit(t)
                first_index = sum(1 << (self.bits - 1 - i) for i in range(j - 1))
                for c, s in enumerate(self.spread(self.rep, t, range(j, self.bits))):
                    part = self.came.at[u, first_index + c]
                    arrived(part, self.down_recv.at[u, first_index + c])
                    self.held[u, s] = (self.held[u, s].astype(F32) + part[...].astype(F32)).astype(
                        BF16
                    )
                if j < self.bits:
                    for copy in self.downs(t, j):
                        copy.start()
                else:
                    self.deliver(t)

        for j in range(self.bits + 1):

            @pl.when(phase(self.bits + 1 + j, FAR_LAG))
            def _(j=j, t=t - LAG * (self.bits + 1 + j) - FAR_LAG):
                e = self.source(t)
                if j == 0:
                    arrived(self.result.at[e, self.rep], self.own_recv.at[e])
                else:
                    bit = self.bits - j
                    held = self.spread(self.rep, t, range(self.bits - 1, bit, -1))
                    for s in held:
                        s = self.flip(s, self.weight(t, bit))
                        arrived(self.result.at[e, s], self.up_recv.at[e, s])
                if j < self.bits:
                    for copy in self.ups(t, j):
                        copy.start()

    def ticks(self):
        return self.units + LAG * (2 * self.bits + 1) + FAR_LAG

    def finish(self):
        def one(t, _):
            for j in range(self.bits):
                for copy in self.downs(t, j) + self.ups(t, j):
                    copy.wait_send()
            self.deliver(t, True)
            return 0

        lax.fori_loop(0, self.units, one, 0)

    @staticmethod
    def scratch(reps, units, share, cols):
        dma = pltpu.SemaphoreType.DMA
        return [
            pltpu.VMEM((units, reps, share, cols), BF16),
            pltpu.VMEM((units, reps - 1, share, cols), BF16),
            dma((units, reps - 1)),
            dma((units, reps - 1)),
            dma((units,)),
            dma((units,)),
            dma((units, reps - 1)),
            dma((units, reps)),
        ]


def staged(scatter, chips, k, term, work):
    middle = (scatter.place > 0) & (scatter.place < chips - 1)
    scatter.prepare(k, term)

    @pl.when(~middle)
    def _():
        scatter.combine(k)

    work()

    @pl.when(middle)
    def _():
        scatter.combine(k)


LAG = 2
FAR_LAG = 0


def interleave(gather, scatter, term, ready=None, then=None):
    chips = gather.chips
    middle = (gather.place > 0) & (gather.place < chips - 1)

    def stage(k, _):
        if ready is not None:
            ready(k)

        def work():
            then(k)

            @pl.when((~middle) & (k + 1 < chips))
            def _():
                gather.step(k + 1)

            @pl.when(middle & (2 * k + 1 < chips))
            def _():
                gather.step(2 * k + 1)

            @pl.when(middle & (2 * k + 2 < chips))
            def _():
                gather.step(2 * k + 2)

        staged(scatter, chips, k, term, work)
        return 0

    lax.fori_loop(0, chips, stage, 0)


def attention_kernel(
    owners,
    reps,
    heads,
    kv_heads,
    tokens_ref,
    query_ref,
    key_ref,
    value_ref,
    gate_ref,
    map_ref,
    position_row_ref,
    out_ref,
    gain_ref,
    cotangent_ref,
    in_pieces_ref,
    attn_out,
    hidden_out,
    entry_out,
    cotangent_out,
    columns_out,
    local_sem,
    *rest,
):
    me, rep = lax.axis_index("grp"), lax.axis_index("rep")
    scatter = Scatter(owners, rest[:4], rest[4:8], by_distance, PARTS)
    gather = Gather(owners, cotangent_out, *rest[8:10])
    reshard = Reshard(owners, reps, columns_out, rest[10:14])
    cols = in_pieces_ref.shape[2]

    def pieces(owner):
        return [(in_pieces_ref.at[owner], pl.ds(0, cols))]

    own = pltpu.make_async_copy(cotangent_ref, cotangent_out.at[me], local_sem)
    own.start()
    meet(owners, reps)
    gather.forward(me, cotangent_ref)
    reshard.start(pieces)
    per_kv = heads // kv_heads
    block_rows = 2 * BLOCK_TOKENS

    def attend(at):
        for s in range(GROUP_SEQUENCES):
            rows = slice(s * block_rows, (s + 1) * block_rows)
            allowed = position_row_ref[s] <= query_positions(map_ref, s, at)
            allowed = jnp.concatenate([allowed] * per_kv, axis=0)
            for kv in range(kv_heads):
                span = slice(kv * HEAD_SIZE, (kv + 1) * HEAD_SIZE)
                spans = [
                    slice(h * HEAD_SIZE, (h + 1) * HEAD_SIZE)
                    for h in range(kv * per_kv, (kv + 1) * per_kv)
                ]
                query = jnp.concatenate([query_ref[at, rows, h] for h in spans], axis=0)
                keys = key_ref[:, rows, span].reshape(-1, HEAD_SIZE)
                values = value_ref[:, rows, span].reshape(-1, HEAD_SIZE)
                scores = dot_nt(query, keys) * HEAD_SIZE ** (-0.5)
                scores = jnp.where(allowed, scores, masked_value)
                exps = jnp.exp(scores - jnp.max(scores, axis=-1, keepdims=True))
                probability = exps / jnp.sum(exps, axis=-1, keepdims=True)
                attended = dot(probability.astype(BF16), values)
                for i, h in enumerate(spans):
                    gated = attended[i * block_rows : (i + 1) * block_rows] * jax.nn.sigmoid(
                        gate_ref[at, rows, h]
                    )
                    attn_out[at, rows, h] = gated.astype(BF16)

    def ready(k):
        at = scatter.at(k)

        def one(core, _):
            attend(2 * at + core)
            return 0

        lax.fori_loop(0, 2, one, 0)

    def term(at):
        both = attn_out[pl.ds(2 * at, 2)]
        return dot(both.reshape(-1, both.shape[-1]), out_ref[...])

    def then(k):
        pl.when(k == 0)(reshard.relay)
        gather.sibling(k)

    interleave(gather, scatter, term, ready, then)
    hidden = tokens_ref[...].astype(F32) + scatter.acc[...]
    hidden_out[...] = hidden
    entry_out[...] = (head_norm(hidden)[0] * gain_ref[...]).astype(BF16)
    own.wait()
    reshard.wait()
    gather.finish()
    scatter.finish()
    reshard.finish()


def attention(
    owners,
    reps,
    heads,
    kv_heads,
    tokens,
    query_rot,
    key_rot,
    value_rows,
    gate_raw,
    block_map,
    position_row,
    w_out,
    gain_mlp,
    cotangent,
    in_pieces,
):
    rows, width = tokens.shape
    shape = jax.ShapeDtypeStruct
    share = in_pieces.shape[1]
    outs = (
        shape(query_rot.shape, BF16),
        shape((rows, width), F32),
        shape((rows, width), BF16),
        shape((owners, rows, width), BF16),
        shape((owners, reps, share, in_pieces.shape[2]), BF16),
    )
    return pl.pallas_call(
        functools.partial(attention_kernel, owners, reps, heads, kv_heads),
        out_shape=outs,
        in_specs=[vmem()] * 5 + [smem()] + [vmem()] * 3 + [anywhere()] * 2,
        out_specs=(vmem(),) * 3 + (anywhere(),) * 2,
        scratch_shapes=[pltpu.SemaphoreType.DMA]
        + Scatter.scratch(owners, rows, width, PARTS)
        + Gather.scratch(owners)
        + Reshard.scratch(owners, reps),
        compiler_params=pltpu.CompilerParams(
            collective_id=1, has_side_effects=True, vmem_limit_bytes=60 * 2**20
        ),
        cost_estimate=pl.CostEstimate(
            flops=4 * owners * rows * width * query_rot.shape[2],
            bytes_accessed=40 * 2**20,
            transcendentals=0,
        ),
        name="attention",
    )(
        tokens,
        query_rot,
        key_rot,
        value_rows,
        gate_raw,
        block_map,
        position_row,
        w_out,
        gain_mlp,
        cotangent,
        in_pieces,
    )


def mlp_kernel(
    owners,
    reps,
    entry_ref,
    cotangent_all_ref,
    in_ref,
    down_ref,
    hidden_ref,
    cotangent_ref,
    gain_ref,
    entry_all,
    activated_out,
    grads_out,
    grad_hidden_out,
    grad_branch_out,
    gain_out,
    down_sum,
    entry_buf,
    cotangent_buf,
    activated_buf,
    local_sem,
    load_sem,
    store_sem,
    *rest,
):
    me = lax.axis_index("grp")
    chips = owners // 2
    gather = FarGather(owners, entry_all, *rest[8:10], PARTS)
    scatter = Scatter(owners, rest[:4], rest[4:8], by_distance, PARTS)
    units = down_ref.shape[0]
    middle = (gather.place > 0) & (gather.place < chips - 1)
    own = pltpu.make_async_copy(entry_ref, entry_all.at[me], local_sem)
    own.start()
    meet(owners, reps)
    own.wait()
    gather.begin()
    down_sum[...] = jnp.zeros_like(down_sum)

    def stores(at):
        return pltpu.make_async_copy(
            activated_buf, activated_out.at[pl.ds(2 * at, 2)], store_sem
        )

    def compute(at, first=False):
        pair = pl.ds(2 * at, 2)
        cotangent_load = pltpu.make_async_copy(
            cotangent_all_ref.at[pair], cotangent_buf, load_sem.at[1]
        )
        cotangent_load.start()
        gather.sibling(at)
        entry_load = pltpu.make_async_copy(entry_all.at[pair], entry_buf, load_sem.at[0])
        entry_load.start()
        cotangent_load.wait()
        cotangent = cotangent_buf[...].reshape(-1, cotangent_buf.shape[-1])
        grad_activated = dot_nt(cotangent, down_ref[...])
        entry_load.wait()
        gate_up = dot(entry_buf[...].reshape(-1, entry_buf.shape[-1]), in_ref[...])
        gate, up = gate_up[:, :units], gate_up[:, units:]
        sig = jax.nn.sigmoid(gate)
        silu = gate * sig
        if not first:
            stores(at).wait()
        activated = (silu * up).astype(BF16)
        shape = activated_buf.shape
        activated_buf[...] = activated.reshape(shape)
        stores(at).start()
        grads_out[pair, :, :units] = (
            (grad_activated * up * sig * (1.0 + gate * (1.0 - sig))).astype(BF16).reshape(shape)
        )
        grads_out[pair, :, units:] = (grad_activated * silu).astype(BF16).reshape(shape)
        down_sum[...] += dot_tn(activated, cotangent)

    def term(at):
        both = grads_out[pl.ds(2 * at, 2)]
        return dot_nt(both.reshape(-1, both.shape[-1]), in_ref[...])

    def step(r, _):
        gather.round(r)
        return 0

    lax.fori_loop(0, jnp.where(middle, chips - 1, 1), step, 0)
    stores(0).start()

    def compute_step(k, _):
        compute(jnp.where(k < 0, gather.place, scatter.at(jnp.maximum(k, 0))))
        return 0

    lax.fori_loop(jnp.where(middle, 0, -1), 1, compute_step, 0)

    def back(k, _):
        more = jnp.where(middle, k + 1 < chips, k + 1 < chips - 1)

        def work():
            @pl.when(more & (~middle))
            def _():
                gather.round(k + 1)

            @pl.when(more)
            def _():
                compute(scatter.at(k + 1))

        staged(scatter, chips, k, term, work)
        return 0

    lax.fori_loop(0, chips, back, 0)
    hidden_buf = scatter.both.at[1 - scatter.core]
    load_hidden = pltpu.make_async_copy(hidden_ref, hidden_buf, local_sem)
    load_hidden.start()
    load_hidden.wait()
    hidden = hidden_buf[...]
    normed, scale = head_norm(hidden)
    grad_entry = scatter.acc[...]
    gain_out[...] = jnp.sum(grad_entry * normed, axis=0, keepdims=True)
    weighted = grad_entry * gain_ref[...]
    grad_hidden = cotangent_ref[...].astype(F32) + scale * (
        weighted - normed * jnp.mean(weighted * normed, axis=-1, keepdims=True)
    )
    grad_hidden_out[...] = grad_hidden
    grad_branch_out[...] = grad_hidden.astype(BF16)
    stores(0).wait()
    gather.finish()
    scatter.finish()


def mlp(owners, reps, entry, cotangent_all, in_cols, w_down, hidden, cotangent, gain_mlp):
    rows, width = entry.shape
    units = w_down.shape[0]
    shape = jax.ShapeDtypeStruct
    outs = (
        shape((owners, rows, width), BF16),
        shape((owners, rows, units), BF16),
        shape((owners, rows, 2 * units), BF16),
        shape((rows, width), F32),
        shape((rows, width), BF16),
        shape((1, width), F32),
        shape((units, width), F32),
    )
    return pl.pallas_call(
        functools.partial(mlp_kernel, owners, reps),
        out_shape=outs,
        in_specs=[anywhere()] * 2 + [vmem()] * 2 + [anywhere()] + [vmem()] * 2,
        out_specs=(anywhere(),) * 2 + (vmem(),) * 5,
        scratch_shapes=[
            pltpu.VMEM((2, rows, width), BF16),
            pltpu.VMEM((2, rows, width), BF16),
            pltpu.VMEM((2, rows, units), BF16),
            pltpu.SemaphoreType.DMA,
            pltpu.SemaphoreType.DMA((2,)),
            pltpu.SemaphoreType.DMA,
        ]
        + Scatter.scratch(owners, rows, width, PARTS)
        + FarGather.scratch(owners, PARTS),
        compiler_params=pltpu.CompilerParams(
            collective_id=2, has_side_effects=True, vmem_limit_bytes=63 * 2**20
        ),
        cost_estimate=pl.CostEstimate(
            flops=12 * owners * rows * width * units,
            bytes_accessed=40 * 2**20,
            transcendentals=0,
        ),
        name="mlp",
    )(entry, cotangent_all, in_cols, w_down, hidden, cotangent, gain_mlp)


def unturned_norm_back(grad, raw, gain, cosine, sine):
    back = turn_back(grad, cosine, sine)
    normed, scale = head_norm(raw)
    weighted = back * gain
    grad_raw = scale * (weighted - normed * jnp.mean(weighted * normed, axis=-1, keepdims=True))
    return grad_raw, jnp.sum(back * normed, axis=0, keepdims=True)


def backward_kernel(
    owners,
    reps,
    heads,
    kv_heads,
    branch_ref,
    activated_ref,
    down_ref,
    out_ref,
    hidden_ref,
    query_ref,
    query_rot_ref,
    gate_ref,
    key_ref,
    key_rot_ref,
    value_ref,
    map_ref,
    position_row_ref,
    table_ref,
    heads_gain_ref,
    attn_out_ref,
    grad_gate_up_ref,
    entry_ref,
    branch_all,
    output_out,
    grads_out,
    gain_out,
    out_term,
    weight_out,
    branch_buf,
    key_sum,
    value_sum,
    entry_buf,
    activated_buf,
    attn_buf,
    grad_attn_buf,
    gate_buf,
    local_sem,
    load_sem,
    activated_sem,
    gate_sem,
    entry_sem,
    *rest,
):
    me = lax.axis_index("grp")
    chips = owners // 2
    scatter = Scatter(owners, rest[:4], rest[4:8], by_distance, PARTS)
    gather = Gather(owners, branch_all, *rest[8:10])
    columns = RepSum(owners, reps, owners, True, rest[10], rest[11], weight_out, rest[12:18])
    load_columns = column_loads(entry_ref, entry_buf, entry_sem, entry_buf.shape[-1])
    load_columns(0, me).start()
    columns_of = columns_term(
        columns,
        load_columns,
        entry_buf,
        lambda: grad_gate_up_ref[...].reshape(-1, grad_gate_up_ref.shape[-1]),
    )

    def tick(t):
        columns.tick(t, columns_of)
    own = pltpu.make_async_copy(branch_ref, branch_all.at[me], local_sem)
    own.start()
    meet(owners, reps)
    gather.forward(me, branch_ref)
    own.wait()
    key_sum[...] = jnp.zeros_like(key_sum)
    value_sum[...] = jnp.zeros_like(value_sum)
    gain_out[...] = jnp.zeros_like(gain_out)
    out_term[...] = jnp.zeros_like(out_term)
    per_kv = heads // kv_heads
    q_cols, kv_cols = heads * HEAD_SIZE, kv_heads * HEAD_SIZE
    block_rows = 2 * BLOCK_TOKENS
    root = HEAD_SIZE ** (-0.5)
    gain_query = heads_gain_ref[:, :HEAD_SIZE]
    gain_key = heads_gain_ref[:, HEAD_SIZE:]

    def block(at, which):
        grad_attn_out = grad_attn_buf[which]
        for s in range(GROUP_SEQUENCES):
            rows = slice(s * block_rows, (s + 1) * block_rows)
            cosine, sine = angles(table_ref[at, rows])
            allowed = position_row_ref[s] <= query_positions(map_ref, s, at)
            allowed = jnp.concatenate([allowed] * per_kv, axis=0)
            for kv in range(kv_heads):
                span = slice(kv * HEAD_SIZE, (kv + 1) * HEAD_SIZE)
                spans = [
                    slice(h * HEAD_SIZE, (h + 1) * HEAD_SIZE)
                    for h in range(kv * per_kv, (kv + 1) * per_kv)
                ]
                query = jnp.concatenate([query_rot_ref[at, rows, h] for h in spans], axis=0)
                keys = key_rot_ref[:, rows, span].reshape(-1, HEAD_SIZE)
                values = value_ref[:, rows, span].reshape(-1, HEAD_SIZE)
                scores = dot_nt(query, keys) * root
                scores = jnp.where(allowed, scores, masked_value)
                exps = jnp.exp(scores - jnp.max(scores, axis=-1, keepdims=True))
                exact = exps / jnp.sum(exps, axis=-1, keepdims=True)
                low = exact.astype(BF16)
                attended = dot(low, values)
                inputs = []
                for i, h in enumerate(spans):
                    grad = grad_attn_out[rows, h]
                    sig = jax.nn.sigmoid(gate_buf[which, rows, h])
                    inputs.append((grad * sig).astype(BF16))
                    gated = slice(q_cols + h.start, q_cols + h.stop)
                    grads_out[at, rows, gated] = (
                        grad
                        * attended[i * block_rows : (i + 1) * block_rows]
                        * sig
                        * (1.0 - sig)
                    ).astype(BF16)
                grad_attended = jnp.concatenate(inputs, axis=0)
                grad_probs = dot_nt(grad_attended, values)
                inner = jnp.sum(exact * grad_probs, axis=-1, keepdims=True)
                grad_scores = (exact * (grad_probs - inner)).astype(BF16)
                grad_query = dot(grad_scores, keys) * root
                key_sum[s, kv] += dot_tn(grad_scores, query)
                value_sum[s, kv] += dot_tn(low, grad_attended)
                for i, h in enumerate(spans):
                    grad_raw, gain_sum = unturned_norm_back(
                        grad_query[i * block_rows : (i + 1) * block_rows],
                        query_ref[at, rows, h],
                        gain_query,
                        cosine,
                        sine,
                    )
                    grads_out[at, rows, h] = grad_raw.astype(BF16)
                    gain_out[:, :HEAD_SIZE] += gain_sum

    def load_activated(k):
        pair = pl.ds(2 * scatter.at(k), 2)
        return pltpu.make_async_copy(activated_ref.at[pair], activated_buf, activated_sem)

    load_activated(0).start()

    def term(at):
        load_activated(0).wait()
        both = activated_buf[...]
        return dot(both.reshape(-1, both.shape[-1]), down_ref[...])

    def then(k):
        @pl.when(k + 1 < chips)
        def _():
            load_activated(k + 1).start()

        at = nearest(gather.place, k, chips)
        pair = pl.ds(2 * at, 2)
        gather.sibling(k)
        load = pltpu.make_async_copy(branch_all.at[pair], branch_buf, load_sem)
        load_attn = pltpu.make_async_copy(attn_out_ref.at[pair], attn_buf, local_sem)
        load_gate = pltpu.make_async_copy(gate_ref.at[pair], gate_buf, gate_sem)
        load.start()
        load_attn.start()
        load_gate.start()
        tick(TICKS * k)
        load.wait()
        load_attn.wait()
        load_gate.wait()
        branch = branch_buf[...].reshape(-1, branch_buf.shape[-1])
        grad_attn_buf[...] = dot_nt(branch, out_ref[...]).reshape(grad_attn_buf.shape)
        out_term[...] += dot_tn(attn_buf[...].reshape(-1, attn_buf.shape[-1]), branch)

        def one(which, _):
            block(2 * at + which, which)
            late_tick(TICKS * k + 1 + TICKS // 2 * which)
            return 0

        lax.fori_loop(0, 2, one, 0)

    def late_tick(t):
        def two(t, _):
            tick(t)
            return 0

        lax.fori_loop(t, t + TICKS // 2, two, 0)

    interleave(gather, scatter, term, then=then)
    hidden = scatter.both.at[1 - scatter.core]
    load_hidden = pltpu.make_async_copy(hidden_ref, hidden, local_sem)
    load_hidden.start()
    load_hidden.wait()
    output_out[...] = (hidden[...] + scatter.acc[...]).astype(BF16)

    key_raw = scatter.both.at[0]

    def key_columns(at):
        return pl.ds(pl.multiple_of(at * kv_cols, HEAD_SIZE), kv_cols)

    def load_keys(at, _):
        pltpu.make_async_copy(key_ref.at[at], key_raw.at[:, key_columns(at)], load_sem).start()
        return 0

    lax.fori_loop(0, owners, load_keys, 0)
    arrived(key_raw.at[:, pl.ds(0, owners * kv_cols)], load_sem)

    def keys(at, _):
        for s in range(GROUP_SEQUENCES):
            rows = slice(s * block_rows, (s + 1) * block_rows)
            for kv in range(kv_heads):
                span = slice(kv * HEAD_SIZE, (kv + 1) * HEAD_SIZE)
                place = pl.ds(pl.multiple_of(at * block_rows, block_rows), block_rows)
                grad_raw, gain_sum = unturned_norm_back(
                    key_sum[s, kv, place] * root,
                    key_raw[
                        rows, pl.ds(pl.multiple_of(at * kv_cols, HEAD_SIZE) + span.start, HEAD_SIZE)
                    ],
                    gain_key,
                    *angles(table_ref[at, rows]),
                )
                first_col = 2 * q_cols + kv * HEAD_SIZE
                grads_out[at, rows, first_col : first_col + HEAD_SIZE] = grad_raw.astype(BF16)
                first_col += kv_cols
                grads_out[at, rows, first_col : first_col + HEAD_SIZE] = value_sum[
                    s, kv, place
                ].astype(BF16)
                gain_out[:, HEAD_SIZE:] += gain_sum
        return 0

    lax.fori_loop(0, owners, keys, 0)

    def late(t, _):
        tick(t)
        return 0

    lax.fori_loop(TICKS * chips, columns.ticks(), late, 0)
    gather.finish()
    scatter.finish()
    columns.finish()


VMEM_LIMIT = 63 * 2**20 + 2**19


def backward(
    owners,
    reps,
    heads,
    kv_heads,
    branch,
    activated,
    w_down,
    w_out,
    hidden,
    query_raw,
    query_rot,
    gate_raw,
    key_raw,
    key_rot,
    value_rows,
    block_map,
    position_row,
    table,
    heads_gain,
    attn_out,
    grad_gate_up,
    entry_all,
):
    rows, width = branch.shape
    cols = 2 * (heads + kv_heads) * HEAD_SIZE
    seq_len = position_row.shape[-1]
    shard = width // owners
    shape = jax.ShapeDtypeStruct
    outs = (
        shape((owners, rows, width), BF16),
        shape((rows, width), BF16),
        shape((owners, rows, cols), BF16),
        shape((1, 2 * HEAD_SIZE), F32),
        shape(w_out.shape, F32),
        shape((owners, reps, shard // reps, grad_gate_up.shape[2]), BF16),
    )
    return pl.pallas_call(
        functools.partial(backward_kernel, owners, reps, heads, kv_heads),
        out_shape=outs,
        in_specs=[anywhere()] * 2
        + [vmem()] * 2
        + [anywhere()]
        + [vmem()] * 2
        + [anywhere()] * 2
        + [vmem()] * 2
        + [smem()]
        + [vmem()] * 3
        + [anywhere()]
        + [vmem()]
        + [anywhere()],
        out_specs=(anywhere(),) + (vmem(),) * 4 + (anywhere(),),
        scratch_shapes=[
            pltpu.VMEM((2, rows, width), BF16),
            pltpu.VMEM((GROUP_SEQUENCES, kv_heads, seq_len, HEAD_SIZE), F32),
            pltpu.VMEM((GROUP_SEQUENCES, kv_heads, seq_len, HEAD_SIZE), F32),
            pltpu.VMEM((2, owners, rows, shard), BF16),
            pltpu.VMEM((2,) + activated.shape[1:], BF16),
            pltpu.VMEM((2,) + attn_out.shape[1:], BF16),
            pltpu.VMEM((2,) + attn_out.shape[1:], F32),
            pltpu.VMEM((2,) + attn_out.shape[1:], F32),
            pltpu.SemaphoreType.DMA,
            pltpu.SemaphoreType.DMA,
            pltpu.SemaphoreType.DMA,
            pltpu.SemaphoreType.DMA,
            pltpu.SemaphoreType.DMA((2,)),
        ]
        + Scatter.scratch(owners, rows, width, PARTS)
        + Gather.scratch(owners)
        + RepSum.scratch(reps, owners, shard // reps, grad_gate_up.shape[2]),
        compiler_params=pltpu.CompilerParams(
            collective_id=3, has_side_effects=True, vmem_limit_bytes=VMEM_LIMIT
        ),
        cost_estimate=pl.CostEstimate(
            flops=4 * owners * rows * width * cols,
            bytes_accessed=40 * 2**20,
            transcendentals=0,
        ),
        name="backward",
    )(
        branch,
        activated,
        w_down,
        w_out,
        hidden,
        query_raw,
        query_rot,
        gate_raw,
        key_raw,
        key_rot,
        value_rows,
        block_map,
        position_row,
        table,
        heads_gain,
        attn_out,
        grad_gate_up,
        entry_all,
    )


def column_loads(source_ref, buf, sem, shard):
    def load(slot, u):
        columns = pl.ds(pl.multiple_of(u * shard, shard), shard)
        return pltpu.make_async_copy(source_ref.at[:, :, columns], buf.at[slot], sem.at[slot])

    return load


def columns_term(total, load, buf, grads):
    def term(t, u):
        @pl.when(t + 1 < total.units)
        def _():
            load((t + 1) % 2, total.unit(t + 1)).start()

        load(t % 2, u).wait()
        entry = buf[t % 2]
        return dot_tn(entry.reshape(-1, entry.shape[-1]), grads())

    return term


def last_kernel(
    owners,
    reps,
    grads_ref,
    weight_ref,
    tokens_ref,
    grad_hidden_ref,
    gain_ref,
    out_term_ref,
    down_term_ref,
    gain_mlp_ref,
    gain_heads_ref,
    entry_ref,
    grad_out,
    gains_out,
    weight_out,
    rows_out,
    entry_buf,
    gains_send,
    gains_came,
    gains_all,
    load_sem,
    g_send,
    g_recv,
    r_send,
    r_recv,
    *rest,
):
    me, rep = lax.axis_index("grp"), lax.axis_index("rep")
    chips = owners // 2
    scatter = Scatter(owners, rest[:4], rest[4:8], by_distance, PARTS)
    columns = RepSum(owners, reps, owners, True, rest[8], rest[9], weight_out, rest[10:16])
    rows = RepSum(
        owners, reps, rows_out.shape[0], False, rest[16], rest[17], rows_out, rest[18:24]
    )
    shard = entry_buf.shape[-1]
    load = column_loads(entry_ref, entry_buf, load_sem, shard)
    load(0, me).start()
    meet(owners, reps)

    def flat(ref):
        return ref[...].reshape(-1, ref.shape[-1])

    columns_of = columns_term(columns, load, entry_buf, lambda: flat(grads_ref))

    down_units = down_term_ref.shape[0] // shard

    def rows_of(t, u):
        at = jnp.minimum(u, down_units - 1) * shard
        down = down_term_ref[pl.ds(pl.multiple_of(at, shard), shard)]
        return jnp.where(u < down_units, down, out_term_ref[...])

    def tick(t):
        rows.tick(t, rows_of)
        columns.tick(t, columns_of)

    def term(at):
        both = grads_ref[pl.ds(2 * at, 2)]
        return dot_nt(both.reshape(-1, both.shape[-1]), weight_ref[...])

    def stage(k, _):
        def one(t, _):
            tick(t)
            return 0

        staged(
            scatter,
            chips,
            k,
            term,
            lambda: lax.fori_loop(LAST_TICKS * k, LAST_TICKS * (k + 1), one, 0),
        )
        return 0

    lax.fori_loop(0, chips, stage, 0)
    grad = scatter.acc[...]
    normed, scale = head_norm(tokens_ref[...].astype(F32))
    gain_attn = jnp.sum(grad * normed, axis=0, keepdims=True)
    gain_mlp = gain_mlp_ref[...]
    for e in range(owners):
        span = slice(e * shard, (e + 1) * shard)
        gains_send[e] = jnp.concatenate(
            [gain_attn[:, span], gain_mlp[:, span], gain_heads_ref[...]], axis=1
        )

    def gains_copy(ahead):
        device = lax.rem(me + ahead, owners)
        return to_grp(
            gains_send.at[device],
            gains_came.at[me],
            g_send.at[ahead],
            g_recv.at[me],
            device,
        )

    def gains_up(ahead):
        return to_rep(
            gains_all.at[rep],
            gains_all.at[rep],
            r_send.at[ahead],
            r_recv.at[rep],
            lax.rem(rep + ahead, reps),
        )

    for ahead in range(1, owners):
        gains_copy(ahead).start()
    gains_came[me] = gains_send[me]
    weighted = grad * gain_ref[...]
    grad_out[...] = (
        grad_hidden_ref[...]
        + scale * (weighted - normed * jnp.mean(weighted * normed, axis=-1, keepdims=True))
    ).astype(BF16)
    for ahead in range(1, owners):
        source = lax.rem(me + ahead, owners)
        arrived(gains_came.at[source], g_recv.at[source])
    gains_all[rep] = jnp.sum(gains_came[...], axis=0)
    for ahead in range(1, reps):
        gains_up(ahead).start()

    def one(t, _):
        tick(t)
        return 0

    lax.fori_loop(LAST_TICKS * chips, max(columns.ticks(), rows.ticks()), one, 0)
    for ahead in range(1, reps):
        source = lax.rem(rep + ahead, reps)
        arrived(gains_all.at[source], r_recv.at[source])
    gains_out[...] = jnp.sum(gains_all[...], axis=0)
    for ahead in range(1, owners):
        gains_copy(ahead).wait_send()
    for ahead in range(1, reps):
        gains_up(ahead).wait_send()
    scatter.finish()
    columns.finish()
    rows.finish()


TICKS = 3
LAST_TICKS = 4


def last(
    owners,
    reps,
    grads,
    weight,
    tokens,
    grad_hidden,
    gain,
    out_term,
    down_term,
    gain_mlp,
    gain_heads,
    entry_all,
):
    rows, width = tokens.shape
    cols = grads.shape[2]
    shard = width // owners
    share = shard // reps
    small = 2 * shard + gain_heads.shape[1]
    units = (out_term.shape[0] + down_term.shape[0]) // shard
    shape = jax.ShapeDtypeStruct
    dma = pltpu.SemaphoreType.DMA
    return pl.pallas_call(
        functools.partial(last_kernel, owners, reps),
        out_shape=(
            shape((rows, width), BF16),
            shape((1, small), F32),
            shape((owners, reps, share, cols), BF16),
            shape((units, reps, share, width), BF16),
        ),
        in_specs=[vmem()] * 9 + [anywhere()],
        out_specs=(vmem(),) * 2 + (anywhere(),) * 2,
        scratch_shapes=[
            pltpu.VMEM((2, owners, rows, shard), BF16),
            pltpu.VMEM((owners, 1, small), F32),
            pltpu.VMEM((owners, 1, small), F32),
            pltpu.VMEM((reps, 1, small), F32),
            dma((2,)),
            dma((owners,)),
            dma((owners,)),
            dma((reps,)),
            dma((reps,)),
        ]
        + Scatter.scratch(owners, rows, width, PARTS)
        + RepSum.scratch(reps, owners, share, cols)
        + RepSum.scratch(reps, units, share, width),
        compiler_params=pltpu.CompilerParams(
            collective_id=4, has_side_effects=True, vmem_limit_bytes=60 * 2**20
        ),
        cost_estimate=pl.CostEstimate(
            flops=4 * owners * rows * width * cols,
            bytes_accessed=40 * 2**20,
            transcendentals=0,
        ),
        name="last",
    )(
        grads,
        weight,
        tokens,
        grad_hidden,
        gain,
        out_term,
        down_term,
        gain_mlp,
        gain_heads,
        entry_all,
    )


def in_rows_kernel(grads_ref, out_ref):
    units = out_ref.shape[2]
    grads = grads_ref[0].reshape(-1, 2 * units).astype(F32)
    out_ref[:, 0, :] = grads[:, :units]
    out_ref[:, 1, :] = grads[:, units:]


def in_rows(grads):
    owners, reps, share, cols = grads.shape
    units = cols // 2
    return pl.pallas_call(
        in_rows_kernel,
        grid=(owners,),
        out_shape=jax.ShapeDtypeStruct((reps * share, 2, owners * units), F32),
        in_specs=[pl.BlockSpec((1, reps, share, cols), lambda e: (e, 0, 0, 0))],
        out_specs=pl.BlockSpec((reps * share, 2, units), lambda e: (0, 0, e)),
        compiler_params=pltpu.CompilerParams(vmem_limit_bytes=40 * 2**20),
        name="in_rows",
    )(grads)


def qkvg_rows_kernel(groups, grads_ref, out_ref, buf, sem):
    e = pl.program_id(0)
    owners = pl.num_programs(0)

    def copies(e):
        slot = e % 2
        for i, (base, at, cols) in enumerate(groups):
            yield pltpu.make_async_copy(
                buf.at[slot, :, pl.ds(at, cols)],
                out_ref.at[:, pl.ds(pl.multiple_of(base + e * cols, HEAD_SIZE), cols)],
                sem.at[slot, i],
            )

    @pl.when(e >= 2)
    def _():
        for copy in copies(e - 2):
            copy.wait()

    buf[e % 2] = grads_ref[0].reshape(buf.shape[1:]).astype(F32)
    for copy in copies(e):
        copy.start()

    @pl.when(e == owners - 1)
    def _():
        for late in (e - 1, e):
            for copy in copies(late):
                copy.wait()


def qkvg_rows(grads, heads, kv_heads):
    owners, reps, share, cols = grads.shape
    q_cols, kv_cols = heads * HEAD_SIZE, kv_heads * HEAD_SIZE
    groups, base, at = [], 0, 0
    for width in (q_cols, q_cols, kv_cols, kv_cols):
        groups.append((base, at, width))
        base += width * owners
        at += width
    return pl.pallas_call(
        functools.partial(qkvg_rows_kernel, tuple(groups)),
        grid=(owners,),
        out_shape=jax.ShapeDtypeStruct((reps * share, owners * cols), F32),
        in_specs=[pl.BlockSpec((1, reps, share, cols), lambda e: (e, 0, 0, 0))],
        out_specs=anywhere(),
        scratch_shapes=[
            pltpu.VMEM((2, reps * share, cols), F32),
            pltpu.SemaphoreType.DMA((2, len(groups))),
        ],
        compiler_params=pltpu.CompilerParams(vmem_limit_bytes=40 * 2**20),
        name="qkvg_rows",
    )(grads)


def positions_of(block_ids):
    offsets = jnp.arange(BLOCK_TOKENS, dtype=jnp.int32)
    return (block_ids[:, :, None] * BLOCK_TOKENS + offsets[None, None, :]).reshape(
        block_ids.shape[0], -1
    )


def body(
    tokens,
    block_map,
    w_qkvg,
    w_out,
    w_in,
    w_down,
    norm_attn,
    norm_query,
    norm_key,
    norm_mlp,
    cotangent,
):
    owners = lax.axis_size("grp")
    me = lax.axis_index("grp")
    heads = QUERY_HEADS // owners
    sharers = max(1, owners // KEY_VALUE_HEADS)
    kv_heads = KEY_VALUE_HEADS * sharers // owners
    per_kv = heads // kv_heads
    q_cols = heads * HEAD_SIZE
    kv_cols = kv_heads * HEAD_SIZE
    rows_here, width = tokens.shape
    shard = w_qkvg.shape[0]
    block_rows = 2 * BLOCK_TOKENS
    seq_len = owners * block_rows
    all_q = QUERY_HEADS * HEAD_SIZE
    all_kv = KEY_VALUE_HEADS * HEAD_SIZE
    hidden_units = w_down.shape[0]

    reps = lax.axis_size("rep")
    share = shard // reps
    in_pieces = lax.dynamic_slice_in_dim(w_in, lax.axis_index("rep") * share, share, 0)
    in_pieces = in_pieces.reshape(share, 2, owners, hidden_units).transpose(2, 0, 1, 3)
    in_pieces = in_pieces.reshape(owners, share, 2 * hidden_units)
    head_part = norm_query.shape[0]
    spread = jnp.zeros((2, HEAD_SIZE), jnp.float32)
    spread = lax.dynamic_update_slice(
        spread, jnp.stack([norm_query, norm_key]).astype(jnp.float32), (0, me * head_part)
    )
    small = jnp.concatenate(
        [norm_attn.astype(jnp.float32), norm_mlp.astype(jnp.float32), spread.reshape(-1)]
    )[None]

    positions = positions_of(block_map)
    table = rotary_table(positions)
    table = table.reshape(GROUP_SEQUENCES, owners, block_rows, HEAD_SIZE)
    table = jnp.swapaxes(table, 0, 1).reshape(owners, rows_here, HEAD_SIZE)
    (
        attn_input,
        query_raw,
        gate_raw,
        key_raw,
        value_rows,
        query_rot,
        key_rot,
        qkvg_cols,
        small_all,
    ) = first(
        owners,
        reps,
        heads,
        kv_heads,
        sharers,
        tokens,
        w_qkvg,
        small,
        table,
    )
    small_all = small_all[:, 0]
    gain_attn = small_all[:, :shard].reshape(-1)
    gain_mlp = small_all[:, shard : 2 * shard].reshape(-1)
    spread = jnp.sum(small_all[:, 2 * shard :], axis=0)
    attn_out, hidden, mlp_own, cotangent_all, in_cols = attention(
        owners,
        reps,
        heads,
        kv_heads,
        tokens,
        query_rot,
        key_rot,
        value_rows,
        gate_raw,
        block_map,
        positions[:, None, :],
        w_out,
        gain_mlp[None],
        cotangent,
        in_pieces,
    )
    in_cols = in_cols.reshape(width, -1)
    (
        mlp_input,
        activated,
        grad_gate_up,
        grad_hidden,
        branch_own,
        gain_mlp_sum,
        down_term,
    ) = mlp(
        owners, reps, mlp_own, cotangent_all, in_cols, w_down, hidden, cotangent, gain_mlp[None]
    )
    _, output, grad_projected, gain_heads_sum, out_term, rows_in = backward(
        owners,
        reps,
        heads,
        kv_heads,
        branch_own,
        activated.reshape(owners, rows_here, hidden_units),
        w_down,
        w_out,
        hidden,
        query_raw,
        query_rot,
        gate_raw,
        key_raw,
        key_rot,
        value_rows,
        block_map,
        positions[:, None, :],
        table,
        spread[None],
        attn_out,
        grad_gate_up.reshape(owners, rows_here, 2 * hidden_units),
        mlp_input.reshape(owners, rows_here, width),
    )
    grad_tokens, gains, rows_qkvg, rows_both = last(
        owners,
        reps,
        grad_projected,
        qkvg_cols.reshape(width, -1),
        tokens,
        grad_hidden,
        gain_attn[None],
        out_term,
        down_term,
        gain_mlp_sum,
        gain_heads_sum,
        attn_input,
    )
    shard_in = in_rows(rows_in)
    down_units = w_down.shape[0] // shard
    shard_down = rows_both[:down_units].reshape(w_down.shape).astype(jnp.float32)
    shard_out = rows_both[down_units:].reshape(w_out.shape).astype(jnp.float32)
    if sharers == 1:
        shard_qkvg = qkvg_rows(rows_qkvg, heads, kv_heads)
    else:
        rows_qkvg = rows_qkvg.reshape(owners, shard, -1).swapaxes(0, 1).astype(jnp.float32)
        queries = [rows_qkvg[:, :, i * q_cols : (i + 1) * q_cols] for i in range(2)]
        others = [
            rows_qkvg[:, :, 2 * q_cols + i * kv_cols : 2 * q_cols + (i + 1) * kv_cols]
            .reshape(shard, owners // sharers, sharers, kv_cols)
            .sum(2)
            for i in range(2)
        ]
        shard_qkvg = jnp.concatenate(
            [part.reshape(shard, -1) for part in queries + others], axis=1
        )
    return (
        output,
        grad_tokens,
        shard_qkvg,
        shard_out,
        shard_in,
        shard_down,
        gains[0, :shard],
        lax.dynamic_slice_in_dim(gains[0], 2 * shard + me * head_part, head_part),
        lax.dynamic_slice_in_dim(gains[0], 2 * shard + HEAD_SIZE + me * head_part, head_part),
        gains[0, shard : 2 * shard],
    )


def solution(mesh):
    placed = (
        P(("rep", "grp"), None),
        P("rep", None),
        P("grp", None),
        P("grp", None),
        P("grp", None, None),
        P("grp", None),
        P("grp"),
        P("grp"),
        P("grp"),
        P("grp"),
        P(("rep", "grp"), None),
    )
    return jax.shard_map(
        body,
        mesh=mesh,
        in_specs=placed,
        out_specs=(
            P(("rep", "grp"), None),
            P(("rep", "grp"), None),
            P("grp", None),
            P("grp", None),
            P("grp", None, None),
            P("grp", None),
            P("grp"),
            P("grp"),
            P("grp"),
            P("grp"),
        ),
        check_vma=False,
    )
```

```python
import functools

import jax
import jax.numpy as jnp
from jax import lax
from jax.experimental import pallas as pl
from jax.experimental.pallas import tpu as pltpu
from jax.sharding import PartitionSpec as P

QUERY_HEADS = 16
KEY_VALUE_HEADS = 8
HEAD_SIZE = 128
BLOCK_TOKENS = 64
GROUP_SEQUENCES = 2


norm_epsilon = 1e-06
rotary_base = 1000000.0
masked_value = -1e30


def rotary_table(positions):
    exponent = jnp.arange(HEAD_SIZE // 2, dtype=jnp.float32) * (2.0 / HEAD_SIZE)
    inverse = jnp.power(jnp.float32(rotary_base), -exponent)
    angle = positions.astype(jnp.float32)[..., None] * inverse
    return jnp.concatenate([jnp.cos(angle), jnp.sin(angle)], axis=-1)


MESH = pl.DeviceIdType.MESH
F32 = jnp.float32
BF16 = jnp.bfloat16


def nearest(place, step, chips):
    low = jnp.minimum(place, chips - 1 - place)
    near = (step + 1) // 2
    side = jnp.where(2 * place < chips, near, -near)
    both = jnp.where(step % 2 == 1, place + side, place - side)
    past = step - low
    rest = jnp.where(place > chips - 1 - place, place - past, place + past)
    return jnp.where(step <= 2 * low, both, rest)


def meet(owners, reps):
    barrier = pltpu.get_barrier_semaphore()
    me, rep = lax.axis_index("grp"), lax.axis_index("rep")
    for ahead in range(1, owners):
        pl.semaphore_signal(
            barrier, 1, device_id={"grp": lax.rem(me + ahead, owners)}, device_id_type=MESH
        )
    for ahead in range(1, reps):
        pl.semaphore_signal(
            barrier, 1, device_id={"rep": lax.rem(rep + ahead, reps)}, device_id_type=MESH
        )
    pl.semaphore_wait(barrier, owners + reps - 2)


def to_grp(source, target, send, recv, device):
    return pltpu.make_async_remote_copy(
        src_ref=source,
        dst_ref=target,
        send_sem=send,
        recv_sem=recv,
        device_id={"grp": device},
        device_id_type=MESH,
    )


def to_rep(source, target, send, recv, device):
    return pltpu.make_async_remote_copy(
        src_ref=source,
        dst_ref=target,
        send_sem=send,
        recv_sem=recv,
        device_id={"rep": device},
        device_id_type=MESH,
    )


def arrived(ref, sem):
    pltpu.make_async_copy(ref, ref, sem).wait()


def dot(a, b):
    return jnp.dot(a, b, preferred_element_type=F32)


def dot_nt(a, b):
    return lax.dot_general(a, b, (((1,), (1,)), ((), ())), preferred_element_type=F32)


def dot_tn(a, b):
    return lax.dot_general(a, b, (((0,), (0,)), ((), ())), preferred_element_type=F32)


class Gather:
    def __init__(self, owners, buf, send, recv, half=0):
        self.owners, self.chips = owners, owners // 2
        self.me = lax.axis_index("grp")
        self.place, self.core = self.me // 2, self.me % 2
        self.buf, self.send, self.recv, self.half = buf, send, recv, half

    def of(self, block):
        return self.buf.at[block, self.half] if len(self.buf.shape) == 4 else self.buf.at[block]

    def sent(self, way, at):
        return self.send.at[self.half, way, at]

    def got(self, block):
        return self.recv.at[self.half, block]

    def copies(self, block, source=None):
        src = self.of(block) if source is None else source
        at = block // 2
        ways = (
            ((at <= self.place) & (self.place < self.chips - 1), self.me + 2),
            ((at >= self.place) & (self.place > 0), self.me - 2),
            (None, self.me + 1 - 2 * self.core),
        )
        return [
            (
                when,
                to_grp(src, self.of(block), self.sent(way, at), self.got(block), device),
            )
            for way, (when, device) in enumerate(ways)
        ]

    def forward(self, block, source=None):
        for when, copy in self.copies(block, source):
            if when is None:
                copy.start()
            else:
                pl.when(when)(copy.start)

    def step(self, k):
        block = 2 * nearest(self.place, k, self.chips) + self.core
        arrived(self.of(block), self.got(block))
        self.forward(block)

    def sibling(self, k):
        block = 2 * nearest(self.place, k, self.chips) + 1 - self.core
        arrived(self.of(block), self.got(block))

    def finish(self):
        def one(at, _):
            for when, copy in self.copies(2 * at + self.core):
                if when is None:
                    copy.wait_send()
                else:
                    pl.when(when)(copy.wait_send)
            return 0

        lax.fori_loop(0, self.chips, one, 0)

    @staticmethod
    def scratch(owners, halves=1):
        return [
            pltpu.SemaphoreType.DMA((halves, 3, owners // 2)),
            pltpu.SemaphoreType.DMA((halves, owners)),
        ]


class FarGather:
    def __init__(self, owners, buf, send, recv, parts):
        self.owners, self.chips, self.parts = owners, owners // 2, parts
        self.me = lax.axis_index("grp")
        self.place, self.core = self.me // 2, self.me % 2
        self.buf, self.send, self.recv = buf, send, recv
        self.part = buf.shape[1] // parts
        self.devices = (self.me + 2, self.me - 2, self.me + 1 - 2 * self.core)

    def rows(self, part):
        return pl.ds(part * self.part, self.part)

    def copy(self, way, block, part):
        ref = self.buf.at[block, self.rows(part)]
        return to_grp(
            ref,
            ref,
            self.send.at[way, block // 2, part],
            self.recv.at[block, part],
            self.devices[way],
        )

    def own(self, way):
        for part in range(self.parts):
            self.copy(way, self.me, part).start()

    def begin(self):
        self.own(2)
        pl.when(self.place == 0)(lambda: self.own(0))
        pl.when(self.place == self.chips - 1)(lambda: self.own(1))

    def pass_on(self, way, at, part, onward):
        block = 2 * at + self.core
        arrived(self.buf.at[block, self.rows(part)], self.recv.at[block, part])
        pl.when(onward)(lambda: self.copy(way, block, part).start())
        self.copy(2, block, part).start()

    def up(self, r, part):
        pl.when(r < self.place)(
            lambda: self.pass_on(0, r, part, self.place < self.chips - 1)
        )

    def down(self, r, part):
        at = self.chips - 1 - r
        pl.when(at > self.place)(lambda: self.pass_on(1, at, part, self.place > 0))

    def round(self, r):
        def flows(ahead, behind):
            ahead(r, 0)
            for part in range(1, self.parts):
                ahead(r, part)
                behind(r, part - 1)
            behind(r, self.parts - 1)

        lower = 2 * self.place < self.chips
        pl.when(lower)(lambda: flows(self.up, self.down))
        pl.when(jnp.logical_not(lower))(lambda: flows(self.down, self.up))
        last = self.chips - 1
        pl.when((r == self.place - 1) & (self.place < last))(lambda: self.own(0))
        pl.when((last - r == self.place + 1) & (self.place > 0))(lambda: self.own(1))

    def sibling(self, at):
        block = 2 * at + 1 - self.core
        for part in range(self.parts):
            arrived(self.buf.at[block, self.rows(part)], self.recv.at[block, part])

    def finish(self):
        last = self.chips - 1

        def one(at, _):
            block = 2 * at + self.core
            for part in range(self.parts):
                for way, when in (
                    (0, (at <= self.place) & (self.place < last)),
                    (1, (at >= self.place) & (self.place > 0)),
                ):
                    pl.when(when)(
                        lambda way=way, part=part: self.copy(way, block, part).wait_send()
                    )
                self.copy(2, block, part).wait_send()
            return 0

        lax.fori_loop(0, self.chips, one, 0)

    @staticmethod
    def scratch(owners, parts):
        return [
            pltpu.SemaphoreType.DMA((3, owners // 2, parts)),
            pltpu.SemaphoreType.DMA((owners, parts)),
        ]


class Reshard:
    def __init__(self, owners, reps, buf, sems):
        self.owners, self.reps = owners, reps
        self.me, self.rep = lax.axis_index("grp"), lax.axis_index("rep")
        self.buf = buf
        self.send1, self.recv1, self.send2, self.recv2 = sems

    def start(self, pieces):
        for source, columns in pieces(self.me):
            pltpu.make_async_copy(
                source, self.buf.at[self.me, self.rep, :, columns], self.recv1.at[self.me]
            ).start()

        def one(ahead, _):
            device = lax.rem(self.me + ahead, self.owners)
            for source, columns in pieces(device):
                to_grp(
                    source,
                    self.buf.at[self.me, self.rep, :, columns],
                    self.send1.at[device],
                    self.recv1.at[self.me],
                    device,
                ).start()
            return 0

        lax.fori_loop(1, self.owners, one, 0)

    def relay(self):
        def one(ahead, _):
            owner = lax.rem(self.me + ahead, self.owners)
            part = self.buf.at[owner, self.rep]
            arrived(part, self.recv1.at[owner])
            for other in range(1, self.reps):
                to_rep(
                    part,
                    part,
                    self.send2.at[other],
                    self.recv2.at[other],
                    lax.rem(self.rep + other, self.reps),
                ).start()
            return 0

        lax.fori_loop(0, self.owners, one, 0)

    def wait(self):
        for other in range(1, self.reps):
            source = lax.rem(self.rep + self.reps - other, self.reps)
            arrived(self.buf.at[:, source], self.recv2.at[other])

    def finish(self):
        def one(ahead, _):
            device = lax.rem(self.me + ahead, self.owners)
            arrived(self.buf.at[device, self.rep], self.send1.at[device])
            return 0

        lax.fori_loop(1, self.owners, one, 0)
        for other in range(1, self.reps):
            arrived(self.buf.at[:, self.rep], self.send2.at[other])

    @staticmethod
    def scratch(owners, reps):
        return [
            pltpu.SemaphoreType.DMA((owners,)),
            pltpu.SemaphoreType.DMA((owners,)),
            pltpu.SemaphoreType.DMA((reps,)),
            pltpu.SemaphoreType.DMA((reps,)),
        ]


def query_positions(map_ref, s, at):
    row = lax.broadcasted_iota(jnp.int32, (2 * BLOCK_TOKENS, 1), 0)
    return row + jnp.where(
        row < BLOCK_TOKENS,
        map_ref[s, 2 * at] * BLOCK_TOKENS,
        (map_ref[s, 2 * at + 1] - 1) * BLOCK_TOKENS,
    )


def angles(table):
    turned = pltpu.roll(table, HEAD_SIZE // 2, 1)
    low = lax.broadcasted_iota(jnp.int32, table.shape, 1) < HEAD_SIZE // 2
    return jnp.where(low, table, turned), jnp.where(low, -turned, table)


def head_norm(values):
    scale = lax.rsqrt(jnp.mean(values * values, axis=-1, keepdims=True) + norm_epsilon)
    return values * scale, scale


def turn(values, cosine, sine):
    return values * cosine + pltpu.roll(values, HEAD_SIZE // 2, 1) * sine


def turn_back(values, cosine, sine):
    return values * cosine - pltpu.roll(values, HEAD_SIZE // 2, 1) * sine


def first_kernel(
    owners,
    reps,
    heads,
    kv_heads,
    sharers,
    tokens_ref,
    weight_ref,
    small_ref,
    table_ref,
    input_out,
    query_out,
    gate_out,
    key_out,
    value_out,
    query_rot_out,
    key_rot_out,
    columns_out,
    small_out,
    buf,
    weight_buf,
    entry_buf,
    entry_sem,
    small_send,
    small_recv,
    local_sem,
    out_sem,
    g_send,
    g_recv,
    *r_sems,
):
    me, rep = lax.axis_index("grp"), lax.axis_index("rep")
    rows, width = tokens_ref.shape
    shard = weight_ref.shape[0]
    share = shard // reps
    q_cols, kv_cols = heads * HEAD_SIZE, kv_heads * HEAD_SIZE
    all_q = QUERY_HEADS * HEAD_SIZE
    all_kv = KEY_VALUE_HEADS * HEAD_SIZE
    gather = Gather(owners, buf, g_send, g_recv)
    reshard = Reshard(owners, reps, weight_buf, r_sems)
    my_rows = pl.ds(pl.multiple_of(rep * share, share), share)

    def pieces(owner):
        out = []
        at = 0
        for base, cols, step in (
            (0, q_cols, owner),
            (all_q, q_cols, owner),
            (2 * all_q, kv_cols, owner // sharers),
            (2 * all_q + all_kv, kv_cols, owner // sharers),
        ):
            first = pl.multiple_of(base + step * cols, HEAD_SIZE)
            out.append((weight_ref.at[my_rows, pl.ds(first, cols)], pl.ds(at, cols)))
            at += cols
        return out

    own = pltpu.make_async_copy(tokens_ref, buf.at[me], local_sem)
    own.start()
    small_out[me] = small_ref[...]
    meet(owners, reps)
    reshard.start(pieces)

    def small_copy(device, index):
        return to_grp(
            small_ref, small_out.at[me], small_send.at[index], small_recv.at[index], device
        )

    for ahead in range(1, owners):
        small_copy(lax.rem(me + ahead, owners), ahead).start()
    gather.forward(me, tokens_ref)
    reshard.relay()
    for ahead in range(1, owners):
        source = lax.rem(me + owners - ahead, owners)
        arrived(small_out.at[source], small_recv.at[ahead])
    own.wait()
    middle = (gather.place > 0) & (gather.place < gather.chips - 1)
    early = jnp.where(middle, gather.chips, gather.chips - 1)

    def step(k, _):
        gather.step(k)
        return 0

    lax.fori_loop(1, early, step, 0)
    reshard.wait()
    columns_copy = pltpu.make_async_copy(weight_buf, columns_out, out_sem)
    columns_copy.start()

    gain = jnp.concatenate([small_out[e][:, :shard] for e in range(owners)], axis=1)
    heads_gain = small_out[0][:, 2 * shard :]
    for e in range(1, owners):
        heads_gain = heads_gain + small_out[e][:, 2 * shard :]
    gain_query = heads_gain[:, :HEAD_SIZE]
    gain_key = heads_gain[:, HEAD_SIZE:]
    total_cols = 2 * q_cols + 2 * kv_cols
    weight = weight_buf.reshape(width, total_cols)

    def block(k, _):
        @pl.when(k >= early)
        def _():
            gather.step(k)

        def core(which, _):
            mine = which == 0

            @pl.when(which == 1)
            def _():
                gather.sibling(k)

            at = 2 * nearest(gather.place, k, gather.chips) + jnp.where(
                mine, gather.core, 1 - gather.core
            )
            values = buf[at].astype(F32)
            normed, _unused = head_norm(values)
            entry = (normed * gain).astype(BF16)
            store = pltpu.make_async_copy(entry_buf.at[which], input_out.at[at], entry_sem.at[which])
            pl.when(k > 0)(store.wait)
            entry_buf[which] = entry
            store.start()
            projected = dot(entry, weight[...])
            cosine, sine = angles(table_ref[at])
            for h in range(heads):
                span = slice(h * HEAD_SIZE, (h + 1) * HEAD_SIZE)
                raw = projected[:, span]
                query_out[at, :, span] = raw
                query_rot_out[at, :, span] = turn(
                    head_norm(raw)[0] * gain_query, cosine, sine
                ).astype(BF16)
            gate_out[at] = projected[:, q_cols : 2 * q_cols]
            for h in range(kv_heads):
                span = slice(h * HEAD_SIZE, (h + 1) * HEAD_SIZE)
                raw = projected[:, 2 * q_cols + h * HEAD_SIZE : 2 * q_cols + (h + 1) * HEAD_SIZE]
                key_out[at, :, span] = raw
                key_rot_out[at, :, span] = turn(
                    head_norm(raw)[0] * gain_key, cosine, sine
                ).astype(BF16)
            value_out[at] = projected[:, 2 * q_cols + kv_cols :].astype(BF16)
            return 0

        lax.fori_loop(0, 2, core, 0)
        return 0

    lax.fori_loop(0, gather.chips, block, 0)
    for which in range(2):
        pltpu.make_async_copy(entry_buf.at[which], input_out.at[0], entry_sem.at[which]).wait()
    columns_copy.wait()
    gather.finish()
    reshard.finish()
    for ahead in range(1, owners):
        small_copy(lax.rem(me + ahead, owners), ahead).wait_send()


def vmem():
    return pl.BlockSpec(memory_space=pltpu.VMEM)


def smem():
    return pl.BlockSpec(memory_space=pltpu.SMEM)


def anywhere():
    return pl.BlockSpec(memory_space=pl.ANY)


def first(owners, reps, heads, kv_heads, sharers, tokens, w_qkvg, small, table):
    rows, width = tokens.shape
    shard = w_qkvg.shape[0]
    q_cols, kv_cols = heads * HEAD_SIZE, kv_heads * HEAD_SIZE
    cols = 2 * q_cols + 2 * kv_cols
    shape = jax.ShapeDtypeStruct
    outs = (
        shape((owners, rows, width), BF16),
        shape((owners, rows, q_cols), F32),
        shape((owners, rows, q_cols), F32),
        shape((owners, rows, kv_cols), F32),
        shape((owners, rows, kv_cols), BF16),
        shape((owners, rows, q_cols), BF16),
        shape((owners, rows, kv_cols), BF16),
        shape((owners, reps, shard // reps, cols), BF16),
        shape((owners,) + small.shape, F32),
    )
    flops = 2 * owners * rows * width * cols
    return pl.pallas_call(
        functools.partial(first_kernel, owners, reps, heads, kv_heads, sharers),
        out_shape=outs,
        in_specs=[anywhere(), anywhere(), vmem(), vmem()],
        out_specs=(anywhere(),) + (vmem(),) * 6 + (anywhere(), vmem()),
        scratch_shapes=[
            pltpu.VMEM((owners, rows, width), BF16),
            pltpu.VMEM((owners, reps, shard // reps, cols), BF16),
            pltpu.VMEM((2, rows, width), BF16),
            pltpu.SemaphoreType.DMA((2,)),
            pltpu.SemaphoreType.DMA((owners,)),
            pltpu.SemaphoreType.DMA((owners,)),
            pltpu.SemaphoreType.DMA,
            pltpu.SemaphoreType.DMA,
        ]
        + Gather.scratch(owners)
        + Reshard.scratch(owners, reps),
        compiler_params=pltpu.CompilerParams(
            collective_id=0, has_side_effects=True, vmem_limit_bytes=60 * 2**20
        ),
        cost_estimate=pl.CostEstimate(
            flops=flops, bytes_accessed=40 * 2**20, transcendentals=0
        ),
        name="first",
    )(tokens, w_qkvg, small, table)


def by_distance(place, step, chips):
    return nearest(place, chips - 1 - step, chips)


class Scatter:
    def __init__(self, owners, bufs, sems, order, parts, half=0):
        self.owners, self.chips = owners, owners // 2
        self.me = lax.axis_index("grp")
        self.place, self.core = self.me // 2, self.me % 2
        self.stage, self.near, self.line, self.both = bufs
        self.acc = self.both.at[self.core]
        self.near_send, self.near_recv, self.line_send, self.line_recv = sems
        self.order, self.parts, self.half = order, parts, half
        self.part = self.both.shape[1] // parts

    def at(self, k):
        return self.order(self.place, k, self.chips)

    def near_copy(self, k):
        at = self.at(k)
        return to_grp(
            self.stage.at[self.half, k % 2],
            self.near.at[self.half, at],
            self.near_send.at[self.half, k % 2],
            self.near_recv.at[self.half, at],
            self.me + 1 - 2 * self.core,
        )

    def rows(self, s):
        return pl.ds(s * self.part, self.part)

    def line_copy(self, at, s):
        target = self.place + jnp.where(at > self.place, 1, -1)
        slot = jnp.where((target == at) & (at < self.place), self.chips, at)
        return to_grp(
            self.near.at[self.half, at, self.rows(s)],
            self.line.at[self.half, slot, self.rows(s)],
            self.line_send.at[self.half, at, s],
            self.line_recv.at[self.half, slot, s],
            2 * target + self.core,
        )

    def prepare(self, k, term):
        @pl.when(k >= 2)
        def _():
            self.near_copy(k - 2).wait_send()

        self.both[...] = term(self.at(k)).reshape(self.both.shape)
        self.stage[self.half, k % 2] = self.both[1 - self.core].astype(BF16)
        self.near_copy(k).start()

    def add(self, slot, s):
        part = self.line.at[self.half, slot, self.rows(s)]
        arrived(part, self.line_recv.at[self.half, slot, s])
        self.acc[self.rows(s)] += part[...].astype(F32)

    def combine(self, k):
        at = self.at(k)
        arrived(self.near.at[self.half, at], self.near_recv.at[self.half, at])
        self.acc[...] += self.near[self.half, at].astype(F32)
        below = self.place > 0
        above = self.place < self.chips - 1

        def one(s, _):
            @pl.when(((at >= self.place) & below) | ((at < self.place) & above))
            def _():
                self.add(at, s)

            @pl.when((at == self.place) & above)
            def _():
                self.add(self.chips, s)

            @pl.when(at != self.place)
            def _():
                self.near[self.half, at, self.rows(s)] = self.acc[self.rows(s)].astype(BF16)
                self.line_copy(at, s).start()

            return 0

        lax.fori_loop(0, self.parts, one, 0)

    def finish(self):
        self.near_copy(self.chips - 2).wait_send()
        self.near_copy(self.chips - 1).wait_send()

        def one(at, _):
            @pl.when(at != self.place)
            def _():
                for s in range(self.parts):
                    self.line_copy(at, s).wait_send()

            return 0

        lax.fori_loop(0, self.chips, one, 0)

    @staticmethod
    def scratch(owners, rows, width, parts, halves=1):
        chips = owners // 2
        rows //= halves
        return [
            pltpu.VMEM((halves, 2, rows, width), BF16),
            pltpu.VMEM((halves, chips, rows, width), BF16),
            pltpu.VMEM((halves, chips + 1, rows, width), BF16),
            pltpu.VMEM((2, rows, width), F32),
            pltpu.SemaphoreType.DMA((halves, 2)),
            pltpu.SemaphoreType.DMA((halves, chips)),
            pltpu.SemaphoreType.DMA((halves, chips, parts)),
            pltpu.SemaphoreType.DMA((halves, chips + 1, parts)),
        ]


PARTS = 4


class RepSum:
    def __init__(self, owners, reps, units, along, held, came, result, sems):
        self.owners, self.reps, self.units, self.along = owners, reps, units, along
        self.me, self.rep = lax.axis_index("grp"), lax.axis_index("rep")
        self.bits = reps.bit_length() - 1
        self.held, self.came, self.result = held, came, result
        self.down_send, self.down_recv, self.own_send, self.own_recv, self.up_send, self.up_recv = sems

    def weight(self, t, j):
        which = (t + j) % self.bits
        return sum(jnp.where(which == b, 1 << b, 0) for b in range(self.bits))

    @staticmethod
    def flip(index, weight):
        return index + weight * (1 - 2 * ((index // weight) % 2))

    def spread(self, index, t, bits):
        out = [index]
        for j in bits:
            out += [self.flip(i, self.weight(t, j)) for i in out]
        return out

    def unit(self, t):
        return lax.rem(self.me + t, self.owners) if self.along else t

    def source(self, t):
        return lax.rem(self.me + self.owners - t, self.owners) if self.along else t

    def downs(self, t, j):
        u = self.unit(t)
        first_index = sum(1 << (self.bits - 1 - i) for i in range(j))
        partner = self.flip(self.rep, self.weight(t, j))
        return [
            to_rep(
                self.held.at[u, s],
                self.came.at[u, first_index + c],
                self.down_send.at[u, first_index + c],
                self.down_recv.at[u, first_index + c],
                partner,
            )
            for c, s in enumerate(self.spread(partner, t, range(j + 1, self.bits)))
        ]

    def ups(self, t, j):
        e = self.source(t)
        held = self.spread(self.rep, t, range(self.bits - 1, self.bits - 1 - j, -1))
        partner = self.flip(self.rep, self.weight(t, self.bits - 1 - j))
        return [
            to_rep(
                self.result.at[e, s],
                self.result.at[e, s],
                self.up_send.at[e, (1 << j) - 1 + c],
                self.up_recv.at[e, s],
                partner,
            )
            for c, s in enumerate(held)
        ]

    def deliver(self, t, sent=False):
        u = self.unit(t)
        source = self.held.at[u, self.rep]
        slot = self.me if self.along else u
        target = self.result.at[slot, self.rep]

        def local():
            if not sent:
                pltpu.make_async_copy(source, target, self.own_recv.at[slot]).start()

        def remote():
            copy = to_grp(source, target, self.own_send.at[u], self.own_recv.at[slot], u)
            copy.wait_send() if sent else copy.start()

        if self.along:
            pl.when(u == self.me)(local)
            pl.when(u != self.me)(remote)
        else:
            local()

    def tick(self, t, term):
        def phase(step, more=0):
            return (t >= LAG * step + more) & (t < self.units + LAG * step + more)

        @pl.when(phase(0))
        def _():
            u = self.unit(t)
            self.held[u] = term(t, u).astype(BF16).reshape(self.held.shape[1:])
            for copy in self.downs(t, 0):
                copy.start()

        for j in range(1, self.bits + 1):

            @pl.when(phase(j))
            def _(j=j, t=t - LAG * j):
                u = self.unit(t)
                first_index = sum(1 << (self.bits - 1 - i) for i in range(j - 1))
                for c, s in enumerate(self.spread(self.rep, t, range(j, self.bits))):
                    part = self.came.at[u, first_index + c]
                    arrived(part, self.down_recv.at[u, first_index + c])
                    self.held[u, s] = (self.held[u, s].astype(F32) + part[...].astype(F32)).astype(
                        BF16
                    )
                if j < self.bits:
                    for copy in self.downs(t, j):
                        copy.start()
                else:
                    self.deliver(t)

        for j in range(self.bits + 1):

            @pl.when(phase(self.bits + 1 + j, FAR_LAG))
            def _(j=j, t=t - LAG * (self.bits + 1 + j) - FAR_LAG):
                e = self.source(t)
                if j == 0:
                    arrived(self.result.at[e, self.rep], self.own_recv.at[e])
                else:
                    bit = self.bits - j
                    held = self.spread(self.rep, t, range(self.bits - 1, bit, -1))
                    for s in held:
                        s = self.flip(s, self.weight(t, bit))
                        arrived(self.result.at[e, s], self.up_recv.at[e, s])
                if j < self.bits:
                    for copy in self.ups(t, j):
                        copy.start()

    def ticks(self):
        return self.units + LAG * (2 * self.bits + 1) + FAR_LAG

    def finish(self):
        def one(t, _):
            for j in range(self.bits):
                for copy in self.downs(t, j) + self.ups(t, j):
                    copy.wait_send()
            self.deliver(t, True)
            return 0

        lax.fori_loop(0, self.units, one, 0)

    @staticmethod
    def scratch(reps, units, share, cols):
        dma = pltpu.SemaphoreType.DMA
        return [
            pltpu.VMEM((units, reps, share, cols), BF16),
            pltpu.VMEM((units, reps - 1, share, cols), BF16),
            dma((units, reps - 1)),
            dma((units, reps - 1)),
            dma((units,)),
            dma((units,)),
            dma((units, reps - 1)),
            dma((units, reps)),
        ]


def staged(scatter, chips, k, term, work):
    middle = (scatter.place > 0) & (scatter.place < chips - 1)
    scatter.prepare(k, term)

    @pl.when(~middle)
    def _():
        scatter.combine(k)

    work()

    @pl.when(middle)
    def _():
        scatter.combine(k)


LAG = 2
FAR_LAG = 0


def interleave(gather, scatter, term, ready=None, then=None):
    chips = gather.chips
    middle = (gather.place > 0) & (gather.place < chips - 1)

    def stage(k, _):
        if ready is not None:
            ready(k)

        def work():
            then(k)

            @pl.when((~middle) & (k + 1 < chips))
            def _():
                gather.step(k + 1)

            @pl.when(middle & (2 * k + 1 < chips))
            def _():
                gather.step(2 * k + 1)

            @pl.when(middle & (2 * k + 2 < chips))
            def _():
                gather.step(2 * k + 2)

        staged(scatter, chips, k, term, work)
        return 0

    lax.fori_loop(0, chips, stage, 0)


def attention_kernel(
    owners,
    reps,
    heads,
    kv_heads,
    tokens_ref,
    query_ref,
    key_ref,
    value_ref,
    gate_ref,
    map_ref,
    position_row_ref,
    out_ref,
    gain_ref,
    cotangent_ref,
    in_pieces_ref,
    attn_out,
    hidden_out,
    entry_out,
    cotangent_out,
    columns_out,
    local_sem,
    *rest,
):
    me, rep = lax.axis_index("grp"), lax.axis_index("rep")
    scatter = Scatter(owners, rest[:4], rest[4:8], by_distance, PARTS)
    gather = Gather(owners, cotangent_out, *rest[8:10])
    reshard = Reshard(owners, reps, columns_out, rest[10:14])
    cols = in_pieces_ref.shape[2]

    def pieces(owner):
        return [(in_pieces_ref.at[owner], pl.ds(0, cols))]

    own = pltpu.make_async_copy(cotangent_ref, cotangent_out.at[me], local_sem)
    own.start()
    meet(owners, reps)
    gather.forward(me, cotangent_ref)
    reshard.start(pieces)
    per_kv = heads // kv_heads
    block_rows = 2 * BLOCK_TOKENS

    def attend(at):
        for s in range(GROUP_SEQUENCES):
            rows = slice(s * block_rows, (s + 1) * block_rows)
            allowed = position_row_ref[s] <= query_positions(map_ref, s, at)
            allowed = jnp.concatenate([allowed] * per_kv, axis=0)
            for kv in range(kv_heads):
                span = slice(kv * HEAD_SIZE, (kv + 1) * HEAD_SIZE)
                spans = [
                    slice(h * HEAD_SIZE, (h + 1) * HEAD_SIZE)
                    for h in range(kv * per_kv, (kv + 1) * per_kv)
                ]
                query = jnp.concatenate([query_ref[at, rows, h] for h in spans], axis=0)
                keys = key_ref[:, rows, span].reshape(-1, HEAD_SIZE)
                values = value_ref[:, rows, span].reshape(-1, HEAD_SIZE)
                scores = dot_nt(query, keys) * HEAD_SIZE ** (-0.5)
                scores = jnp.where(allowed, scores, masked_value)
                exps = jnp.exp(scores - jnp.max(scores, axis=-1, keepdims=True))
                probability = exps / jnp.sum(exps, axis=-1, keepdims=True)
                attended = dot(probability.astype(BF16), values)
                for i, h in enumerate(spans):
                    gated = attended[i * block_rows : (i + 1) * block_rows] * jax.nn.sigmoid(
                        gate_ref[at, rows, h]
                    )
                    attn_out[at, rows, h] = gated.astype(BF16)

    def ready(k):
        at = scatter.at(k)

        def one(core, _):
            attend(2 * at + core)
            return 0

        lax.fori_loop(0, 2, one, 0)

    def term(at):
        both = attn_out[pl.ds(2 * at, 2)]
        return dot(both.reshape(-1, both.shape[-1]), out_ref[...])

    def then(k):
        pl.when(k == 0)(reshard.relay)
        gather.sibling(k)

    interleave(gather, scatter, term, ready, then)
    hidden = tokens_ref[...].astype(F32) + scatter.acc[...]
    hidden_out[...] = hidden
    entry_out[...] = (head_norm(hidden)[0] * gain_ref[...]).astype(BF16)
    own.wait()
    reshard.wait()
    gather.finish()
    scatter.finish()
    reshard.finish()


def attention(
    owners,
    reps,
    heads,
    kv_heads,
    tokens,
    query_rot,
    key_rot,
    value_rows,
    gate_raw,
    block_map,
    position_row,
    w_out,
    gain_mlp,
    cotangent,
    in_pieces,
):
    rows, width = tokens.shape
    shape = jax.ShapeDtypeStruct
    share = in_pieces.shape[1]
    outs = (
        shape(query_rot.shape, BF16),
        shape((rows, width), F32),
        shape((rows, width), BF16),
        shape((owners, rows, width), BF16),
        shape((owners, reps, share, in_pieces.shape[2]), BF16),
    )
    return pl.pallas_call(
        functools.partial(attention_kernel, owners, reps, heads, kv_heads),
        out_shape=outs,
        in_specs=[vmem()] * 5 + [smem()] + [vmem()] * 3 + [anywhere()] * 2,
        out_specs=(vmem(),) * 3 + (anywhere(),) * 2,
        scratch_shapes=[pltpu.SemaphoreType.DMA]
        + Scatter.scratch(owners, rows, width, PARTS)
        + Gather.scratch(owners)
        + Reshard.scratch(owners, reps),
        compiler_params=pltpu.CompilerParams(
            collective_id=1, has_side_effects=True, vmem_limit_bytes=60 * 2**20
        ),
        cost_estimate=pl.CostEstimate(
            flops=4 * owners * rows * width * query_rot.shape[2],
            bytes_accessed=40 * 2**20,
            transcendentals=0,
        ),
        name="attention",
    )(
        tokens,
        query_rot,
        key_rot,
        value_rows,
        gate_raw,
        block_map,
        position_row,
        w_out,
        gain_mlp,
        cotangent,
        in_pieces,
    )


def mlp_kernel(
    owners,
    reps,
    entry_ref,
    cotangent_all_ref,
    in_ref,
    down_ref,
    hidden_ref,
    cotangent_ref,
    gain_ref,
    entry_all,
    activated_out,
    grads_all,
    grad_hidden_out,
    grad_branch_out,
    gain_out,
    down_out,
    grads_out,
    down_sum,
    out_sem,
    entry_buf,
    cotangent_buf,
    activated_buf,
    local_sem,
    load_sem,
    store_sem,
    *rest,
):
    me = lax.axis_index("grp")
    chips = owners // 2
    gather = FarGather(owners, entry_all, *rest[8:10], PARTS)
    scatter = Scatter(owners, rest[:4], rest[4:8], by_distance, PARTS)
    units = down_ref.shape[0]
    middle = (gather.place > 0) & (gather.place < chips - 1)
    own = pltpu.make_async_copy(entry_ref, entry_all.at[me], local_sem)
    own.start()
    meet(owners, reps)
    own.wait()
    gather.begin()
    down_sum[...] = jnp.zeros_like(down_sum)

    def stores(at):
        return pltpu.make_async_copy(
            activated_buf, activated_out.at[pl.ds(2 * at, 2)], store_sem
        )

    def grads_store(at):
        pair = pl.ds(2 * at, 2)
        return pltpu.make_async_copy(grads_out.at[pair], grads_all.at[pair], out_sem.at[at])

    def compute(at, first=False):
        pair = pl.ds(2 * at, 2)
        cotangent_load = pltpu.make_async_copy(
            cotangent_all_ref.at[pair], cotangent_buf, load_sem.at[1]
        )
        cotangent_load.start()
        gather.sibling(at)
        entry_load = pltpu.make_async_copy(entry_all.at[pair], entry_buf, load_sem.at[0])
        entry_load.start()
        cotangent_load.wait()
        cotangent = cotangent_buf[...].reshape(-1, cotangent_buf.shape[-1])
        grad_activated = dot_nt(cotangent, down_ref[...])
        entry_load.wait()
        gate_up = dot(entry_buf[...].reshape(-1, entry_buf.shape[-1]), in_ref[...])
        gate, up = gate_up[:, :units], gate_up[:, units:]
        sig = jax.nn.sigmoid(gate)
        silu = gate * sig
        if not first:
            stores(at).wait()
        activated = (silu * up).astype(BF16)
        shape = activated_buf.shape
        activated_buf[...] = activated.reshape(shape)
        stores(at).start()
        grads_out[pair, :, :units] = (
            (grad_activated * up * sig * (1.0 + gate * (1.0 - sig))).astype(BF16).reshape(shape)
        )
        grads_out[pair, :, units:] = (grad_activated * silu).astype(BF16).reshape(shape)
        grads_store(at).start()
        down_sum[...] += dot_tn(activated, cotangent)

    def term(at):
        both = grads_out[pl.ds(2 * at, 2)]
        return dot_nt(both.reshape(-1, both.shape[-1]), in_ref[...])

    def step(r, _):
        gather.round(r)
        return 0

    lax.fori_loop(0, jnp.where(middle, chips - 1, 1), step, 0)
    stores(0).start()

    def compute_step(k, _):
        compute(jnp.where(k < 0, gather.place, scatter.at(jnp.maximum(k, 0))))
        return 0

    lax.fori_loop(jnp.where(middle, 0, -1), 1, compute_step, 0)

    def back(k, _):
        more = jnp.where(middle, k + 1 < chips, k + 1 < chips - 1)

        def work():
            @pl.when(more & (~middle))
            def _():
                gather.round(k + 1)

            @pl.when(more)
            def _():
                compute(scatter.at(k + 1))

        staged(scatter, chips, k, term, work)
        return 0

    lax.fori_loop(0, chips - 1, back, 0)
    down_store = pltpu.make_async_copy(down_sum, down_out, out_sem.at[chips])
    down_store.start()
    back(chips - 1, 0)
    hidden_buf = scatter.both.at[1 - scatter.core]
    load_hidden = pltpu.make_async_copy(hidden_ref, hidden_buf, local_sem)
    load_hidden.start()
    load_hidden.wait()
    hidden = hidden_buf[...]
    normed, scale = head_norm(hidden)
    grad_entry = scatter.acc[...]
    gain_out[...] = jnp.sum(grad_entry * normed, axis=0, keepdims=True)
    weighted = grad_entry * gain_ref[...]
    grad_hidden = cotangent_ref[...].astype(F32) + scale * (
        weighted - normed * jnp.mean(weighted * normed, axis=-1, keepdims=True)
    )
    grad_hidden_out[...] = grad_hidden
    grad_branch_out[...] = grad_hidden.astype(BF16)
    stores(0).wait()
    for at in range(chips):
        grads_store(at).wait()
    down_store.wait()
    gather.finish()
    scatter.finish()


def mlp(owners, reps, entry, cotangent_all, in_cols, w_down, hidden, cotangent, gain_mlp):
    rows, width = entry.shape
    units = w_down.shape[0]
    shape = jax.ShapeDtypeStruct
    outs = (
        shape((owners, rows, width), BF16),
        shape((owners, rows, units), BF16),
        shape((owners, rows, 2 * units), BF16),
        shape((rows, width), F32),
        shape((rows, width), BF16),
        shape((1, width), F32),
        shape((units, width), F32),
    )
    return pl.pallas_call(
        functools.partial(mlp_kernel, owners, reps),
        out_shape=outs,
        in_specs=[anywhere()] * 2 + [vmem()] * 2 + [anywhere()] + [vmem()] * 2,
        out_specs=(anywhere(),) * 3 + (vmem(),) * 3 + (anywhere(),),
        scratch_shapes=[
            pltpu.VMEM((owners, rows, 2 * units), BF16),
            pltpu.VMEM((units, width), F32),
            pltpu.SemaphoreType.DMA((owners // 2 + 1,)),
            pltpu.VMEM((2, rows, width), BF16),
            pltpu.VMEM((2, rows, width), BF16),
            pltpu.VMEM((2, rows, units), BF16),
            pltpu.SemaphoreType.DMA,
            pltpu.SemaphoreType.DMA((2,)),
            pltpu.SemaphoreType.DMA,
        ]
        + Scatter.scratch(owners, rows, width, PARTS)
        + FarGather.scratch(owners, PARTS),
        compiler_params=pltpu.CompilerParams(
            collective_id=2, has_side_effects=True, vmem_limit_bytes=63 * 2**20
        ),
        cost_estimate=pl.CostEstimate(
            flops=12 * owners * rows * width * units,
            bytes_accessed=40 * 2**20,
            transcendentals=0,
        ),
        name="mlp",
    )(entry, cotangent_all, in_cols, w_down, hidden, cotangent, gain_mlp)


def unturned_norm_back(grad, raw, gain, cosine, sine):
    back = turn_back(grad, cosine, sine)
    normed, scale = head_norm(raw)
    weighted = back * gain
    grad_raw = scale * (weighted - normed * jnp.mean(weighted * normed, axis=-1, keepdims=True))
    return grad_raw, jnp.sum(back * normed, axis=0, keepdims=True)


def backward_kernel(
    owners,
    reps,
    heads,
    kv_heads,
    branch_ref,
    activated_ref,
    down_ref,
    out_ref,
    hidden_ref,
    query_ref,
    query_rot_ref,
    gate_ref,
    key_ref,
    key_rot_ref,
    value_ref,
    map_ref,
    position_row_ref,
    table_ref,
    heads_gain_ref,
    attn_out_ref,
    grad_gate_up_ref,
    entry_ref,
    branch_all,
    output_out,
    grads_out,
    gain_out,
    out_term,
    weight_out,
    branch_buf,
    key_sum,
    value_sum,
    entry_buf,
    activated_buf,
    attn_buf,
    grad_attn_buf,
    gate_buf,
    local_sem,
    load_sem,
    activated_sem,
    gate_sem,
    entry_sem,
    *rest,
):
    me = lax.axis_index("grp")
    chips = owners // 2
    scatter = Scatter(owners, rest[:4], rest[4:8], by_distance, PARTS)
    gather = Gather(owners, branch_all, *rest[8:10])
    columns = RepSum(owners, reps, owners, True, rest[10], rest[11], weight_out, rest[12:18])
    load_columns = column_loads(entry_ref, entry_buf, entry_sem, entry_buf.shape[-1])
    load_columns(0, me).start()
    columns_of = columns_term(
        columns,
        load_columns,
        entry_buf,
        lambda: grad_gate_up_ref[...].reshape(-1, grad_gate_up_ref.shape[-1]),
    )

    def tick(t):
        columns.tick(t, columns_of)
    own = pltpu.make_async_copy(branch_ref, branch_all.at[me], local_sem)
    own.start()
    meet(owners, reps)
    gather.forward(me, branch_ref)
    own.wait()
    key_sum[...] = jnp.zeros_like(key_sum)
    value_sum[...] = jnp.zeros_like(value_sum)
    gain_out[...] = jnp.zeros_like(gain_out)
    out_term[...] = jnp.zeros_like(out_term)
    per_kv = heads // kv_heads
    q_cols, kv_cols = heads * HEAD_SIZE, kv_heads * HEAD_SIZE
    block_rows = 2 * BLOCK_TOKENS
    root = HEAD_SIZE ** (-0.5)
    gain_query = heads_gain_ref[:, :HEAD_SIZE]
    gain_key = heads_gain_ref[:, HEAD_SIZE:]

    def block(at, which):
        grad_attn_out = grad_attn_buf[which]
        for s in range(GROUP_SEQUENCES):
            rows = slice(s * block_rows, (s + 1) * block_rows)
            cosine, sine = angles(table_ref[at, rows])
            allowed = position_row_ref[s] <= query_positions(map_ref, s, at)
            allowed = jnp.concatenate([allowed] * per_kv, axis=0)
            for kv in range(kv_heads):
                span = slice(kv * HEAD_SIZE, (kv + 1) * HEAD_SIZE)
                spans = [
                    slice(h * HEAD_SIZE, (h + 1) * HEAD_SIZE)
                    for h in range(kv * per_kv, (kv + 1) * per_kv)
                ]
                query = jnp.concatenate([query_rot_ref[at, rows, h] for h in spans], axis=0)
                keys = key_rot_ref[:, rows, span].reshape(-1, HEAD_SIZE)
                values = value_ref[:, rows, span].reshape(-1, HEAD_SIZE)
                scores = dot_nt(query, keys) * root
                scores = jnp.where(allowed, scores, masked_value)
                exps = jnp.exp(scores - jnp.max(scores, axis=-1, keepdims=True))
                exact = exps / jnp.sum(exps, axis=-1, keepdims=True)
                low = exact.astype(BF16)
                attended = dot(low, values)
                inputs = []
                for i, h in enumerate(spans):
                    grad = grad_attn_out[rows, h]
                    sig = jax.nn.sigmoid(gate_buf[which, rows, h])
                    inputs.append((grad * sig).astype(BF16))
                    gated = slice(q_cols + h.start, q_cols + h.stop)
                    grads_out[at, rows, gated] = (
                        grad
                        * attended[i * block_rows : (i + 1) * block_rows]
                        * sig
                        * (1.0 - sig)
                    ).astype(BF16)
                grad_attended = jnp.concatenate(inputs, axis=0)
                grad_probs = dot_nt(grad_attended, values)
                inner = jnp.sum(exact * grad_probs, axis=-1, keepdims=True)
                grad_scores = (exact * (grad_probs - inner)).astype(BF16)
                grad_query = dot(grad_scores, keys) * root
                key_sum[s, kv] += dot_tn(grad_scores, query)
                value_sum[s, kv] += dot_tn(low, grad_attended)
                for i, h in enumerate(spans):
                    grad_raw, gain_sum = unturned_norm_back(
                        grad_query[i * block_rows : (i + 1) * block_rows],
                        query_ref[at, rows, h],
                        gain_query,
                        cosine,
                        sine,
                    )
                    grads_out[at, rows, h] = grad_raw.astype(BF16)
                    gain_out[:, :HEAD_SIZE] += gain_sum

    def load_activated(k):
        pair = pl.ds(2 * scatter.at(k), 2)
        return pltpu.make_async_copy(activated_ref.at[pair], activated_buf, activated_sem)

    load_activated(0).start()

    def term(at):
        load_activated(0).wait()
        both = activated_buf[...]
        return dot(both.reshape(-1, both.shape[-1]), down_ref[...])

    def then(k):
        @pl.when(k + 1 < chips)
        def _():
            load_activated(k + 1).start()

        at = nearest(gather.place, k, chips)
        pair = pl.ds(2 * at, 2)
        gather.sibling(k)
        load = pltpu.make_async_copy(branch_all.at[pair], branch_buf, load_sem)
        load_attn = pltpu.make_async_copy(attn_out_ref.at[pair], attn_buf, local_sem)
        load_gate = pltpu.make_async_copy(gate_ref.at[pair], gate_buf, gate_sem)
        load.start()
        load_attn.start()
        load_gate.start()
        tick(TICKS * k)
        load.wait()
        load_attn.wait()
        load_gate.wait()
        branch = branch_buf[...].reshape(-1, branch_buf.shape[-1])
        grad_attn_buf[...] = dot_nt(branch, out_ref[...]).reshape(grad_attn_buf.shape)
        out_term[...] += dot_tn(attn_buf[...].reshape(-1, attn_buf.shape[-1]), branch)

        def one(which, _):
            block(2 * at + which, which)
            late_tick(TICKS * k + 1 + TICKS // 2 * which)
            return 0

        lax.fori_loop(0, 2, one, 0)

    def late_tick(t):
        def two(t, _):
            tick(t)
            return 0

        lax.fori_loop(t, t + TICKS // 2, two, 0)

    interleave(gather, scatter, term, then=then)
    hidden = scatter.both.at[1 - scatter.core]
    load_hidden = pltpu.make_async_copy(hidden_ref, hidden, local_sem)
    load_hidden.start()
    load_hidden.wait()
    output_out[...] = (hidden[...] + scatter.acc[...]).astype(BF16)

    key_raw = scatter.both.at[0]

    def key_columns(at):
        return pl.ds(pl.multiple_of(at * kv_cols, HEAD_SIZE), kv_cols)

    def load_keys(at, _):
        pltpu.make_async_copy(key_ref.at[at], key_raw.at[:, key_columns(at)], load_sem).start()
        return 0

    lax.fori_loop(0, owners, load_keys, 0)
    arrived(key_raw.at[:, pl.ds(0, owners * kv_cols)], load_sem)

    def keys(at, _):
        for s in range(GROUP_SEQUENCES):
            rows = slice(s * block_rows, (s + 1) * block_rows)
            for kv in range(kv_heads):
                span = slice(kv * HEAD_SIZE, (kv + 1) * HEAD_SIZE)
                place = pl.ds(pl.multiple_of(at * block_rows, block_rows), block_rows)
                grad_raw, gain_sum = unturned_norm_back(
                    key_sum[s, kv, place] * root,
                    key_raw[
                        rows, pl.ds(pl.multiple_of(at * kv_cols, HEAD_SIZE) + span.start, HEAD_SIZE)
                    ],
                    gain_key,
                    *angles(table_ref[at, rows]),
                )
                first_col = 2 * q_cols + kv * HEAD_SIZE
                grads_out[at, rows, first_col : first_col + HEAD_SIZE] = grad_raw.astype(BF16)
                first_col += kv_cols
                grads_out[at, rows, first_col : first_col + HEAD_SIZE] = value_sum[
                    s, kv, place
                ].astype(BF16)
                gain_out[:, HEAD_SIZE:] += gain_sum
        return 0

    lax.fori_loop(0, owners, keys, 0)

    def late(t, _):
        tick(t)
        return 0

    lax.fori_loop(TICKS * chips, columns.ticks(), late, 0)
    gather.finish()
    scatter.finish()
    columns.finish()


VMEM_LIMIT = 63 * 2**20 + 2**19


def backward(
    owners,
    reps,
    heads,
    kv_heads,
    branch,
    activated,
    w_down,
    w_out,
    hidden,
    query_raw,
    query_rot,
    gate_raw,
    key_raw,
    key_rot,
    value_rows,
    block_map,
    position_row,
    table,
    heads_gain,
    attn_out,
    grad_gate_up,
    entry_all,
):
    rows, width = branch.shape
    cols = 2 * (heads + kv_heads) * HEAD_SIZE
    seq_len = position_row.shape[-1]
    shard = width // owners
    shape = jax.ShapeDtypeStruct
    outs = (
        shape((owners, rows, width), BF16),
        shape((rows, width), BF16),
        shape((owners, rows, cols), BF16),
        shape((1, 2 * HEAD_SIZE), F32),
        shape(w_out.shape, F32),
        shape((owners, reps, shard // reps, grad_gate_up.shape[2]), BF16),
    )
    return pl.pallas_call(
        functools.partial(backward_kernel, owners, reps, heads, kv_heads),
        out_shape=outs,
        in_specs=[anywhere()] * 2
        + [vmem()] * 2
        + [anywhere()]
        + [vmem()] * 2
        + [anywhere()] * 2
        + [vmem()] * 2
        + [smem()]
        + [vmem()] * 3
        + [anywhere()]
        + [vmem()]
        + [anywhere()],
        out_specs=(anywhere(),) + (vmem(),) * 4 + (anywhere(),),
        scratch_shapes=[
            pltpu.VMEM((2, rows, width), BF16),
            pltpu.VMEM((GROUP_SEQUENCES, kv_heads, seq_len, HEAD_SIZE), F32),
            pltpu.VMEM((GROUP_SEQUENCES, kv_heads, seq_len, HEAD_SIZE), F32),
            pltpu.VMEM((2, owners, rows, shard), BF16),
            pltpu.VMEM((2,) + activated.shape[1:], BF16),
            pltpu.VMEM((2,) + attn_out.shape[1:], BF16),
            pltpu.VMEM((2,) + attn_out.shape[1:], F32),
            pltpu.VMEM((2,) + attn_out.shape[1:], F32),
            pltpu.SemaphoreType.DMA,
            pltpu.SemaphoreType.DMA,
            pltpu.SemaphoreType.DMA,
            pltpu.SemaphoreType.DMA,
            pltpu.SemaphoreType.DMA((2,)),
        ]
        + Scatter.scratch(owners, rows, width, PARTS)
        + Gather.scratch(owners)
        + RepSum.scratch(reps, owners, shard // reps, grad_gate_up.shape[2]),
        compiler_params=pltpu.CompilerParams(
            collective_id=3, has_side_effects=True, vmem_limit_bytes=VMEM_LIMIT
        ),
        cost_estimate=pl.CostEstimate(
            flops=4 * owners * rows * width * cols,
            bytes_accessed=40 * 2**20,
            transcendentals=0,
        ),
        name="backward",
    )(
        branch,
        activated,
        w_down,
        w_out,
        hidden,
        query_raw,
        query_rot,
        gate_raw,
        key_raw,
        key_rot,
        value_rows,
        block_map,
        position_row,
        table,
        heads_gain,
        attn_out,
        grad_gate_up,
        entry_all,
    )


def column_loads(source_ref, buf, sem, shard):
    def load(slot, u):
        columns = pl.ds(pl.multiple_of(u * shard, shard), shard)
        return pltpu.make_async_copy(source_ref.at[:, :, columns], buf.at[slot], sem.at[slot])

    return load


def columns_term(total, load, buf, grads):
    def term(t, u):
        @pl.when(t + 1 < total.units)
        def _():
            load((t + 1) % 2, total.unit(t + 1)).start()

        load(t % 2, u).wait()
        entry = buf[t % 2]
        return dot_tn(entry.reshape(-1, entry.shape[-1]), grads())

    return term


def last_kernel(
    owners,
    reps,
    grads_ref,
    weight_ref,
    tokens_ref,
    grad_hidden_ref,
    gain_ref,
    out_term_ref,
    down_term_ref,
    gain_mlp_ref,
    gain_heads_ref,
    entry_ref,
    grad_out,
    gains_out,
    weight_out,
    rows_out,
    entry_buf,
    gains_send,
    gains_came,
    gains_all,
    load_sem,
    g_send,
    g_recv,
    r_send,
    r_recv,
    *rest,
):
    me, rep = lax.axis_index("grp"), lax.axis_index("rep")
    chips = owners // 2
    scatter = Scatter(owners, rest[:4], rest[4:8], by_distance, PARTS)
    columns = RepSum(owners, reps, owners, True, rest[8], rest[9], weight_out, rest[10:16])
    rows = RepSum(
        owners, reps, rows_out.shape[0], False, rest[16], rest[17], rows_out, rest[18:24]
    )
    shard = entry_buf.shape[-1]
    load = column_loads(entry_ref, entry_buf, load_sem, shard)
    load(0, me).start()
    meet(owners, reps)

    def flat(ref):
        return ref[...].reshape(-1, ref.shape[-1])

    columns_of = columns_term(columns, load, entry_buf, lambda: flat(grads_ref))

    down_units = down_term_ref.shape[0] // shard

    def rows_of(t, u):
        at = jnp.minimum(u, down_units - 1) * shard
        down = down_term_ref[pl.ds(pl.multiple_of(at, shard), shard)]
        return jnp.where(u < down_units, down, out_term_ref[...])

    def tick(t):
        rows.tick(t, rows_of)
        columns.tick(t, columns_of)

    def term(at):
        both = grads_ref[pl.ds(2 * at, 2)]
        return dot_nt(both.reshape(-1, both.shape[-1]), weight_ref[...])

    def stage(k, _):
        def one(t, _):
            tick(t)
            return 0

        staged(
            scatter,
            chips,
            k,
            term,
            lambda: lax.fori_loop(LAST_TICKS * k, LAST_TICKS * (k + 1), one, 0),
        )
        return 0

    lax.fori_loop(0, chips, stage, 0)
    grad = scatter.acc[...]
    normed, scale = head_norm(tokens_ref[...].astype(F32))
    gain_attn = jnp.sum(grad * normed, axis=0, keepdims=True)
    gain_mlp = gain_mlp_ref[...]
    for e in range(owners):
        span = slice(e * shard, (e + 1) * shard)
        gains_send[e] = jnp.concatenate(
            [gain_attn[:, span], gain_mlp[:, span], gain_heads_ref[...]], axis=1
        )

    def gains_copy(ahead):
        device = lax.rem(me + ahead, owners)
        return to_grp(
            gains_send.at[device],
            gains_came.at[me],
            g_send.at[ahead],
            g_recv.at[me],
            device,
        )

    def gains_up(ahead):
        return to_rep(
            gains_all.at[rep],
            gains_all.at[rep],
            r_send.at[ahead],
            r_recv.at[rep],
            lax.rem(rep + ahead, reps),
        )

    for ahead in range(1, owners):
        gains_copy(ahead).start()
    gains_came[me] = gains_send[me]
    weighted = grad * gain_ref[...]
    grad_out[...] = (
        grad_hidden_ref[...]
        + scale * (weighted - normed * jnp.mean(weighted * normed, axis=-1, keepdims=True))
    ).astype(BF16)
    for ahead in range(1, owners):
        source = lax.rem(me + ahead, owners)
        arrived(gains_came.at[source], g_recv.at[source])
    gains_all[rep] = jnp.sum(gains_came[...], axis=0)
    for ahead in range(1, reps):
        gains_up(ahead).start()

    def one(t, _):
        tick(t)
        return 0

    lax.fori_loop(LAST_TICKS * chips, max(columns.ticks(), rows.ticks()), one, 0)
    for ahead in range(1, reps):
        source = lax.rem(rep + ahead, reps)
        arrived(gains_all.at[source], r_recv.at[source])
    gains_out[...] = jnp.sum(gains_all[...], axis=0)
    for ahead in range(1, owners):
        gains_copy(ahead).wait_send()
    for ahead in range(1, reps):
        gains_up(ahead).wait_send()
    scatter.finish()
    columns.finish()
    rows.finish()


TICKS = 3
LAST_TICKS = 4


def last(
    owners,
    reps,
    grads,
    weight,
    tokens,
    grad_hidden,
    gain,
    out_term,
    down_term,
    gain_mlp,
    gain_heads,
    entry_all,
):
    rows, width = tokens.shape
    cols = grads.shape[2]
    shard = width // owners
    share = shard // reps
    small = 2 * shard + gain_heads.shape[1]
    units = (out_term.shape[0] + down_term.shape[0]) // shard
    shape = jax.ShapeDtypeStruct
    dma = pltpu.SemaphoreType.DMA
    return pl.pallas_call(
        functools.partial(last_kernel, owners, reps),
        out_shape=(
            shape((rows, width), BF16),
            shape((1, small), F32),
            shape((owners, reps, share, cols), BF16),
            shape((units, reps, share, width), BF16),
        ),
        in_specs=[vmem()] * 9 + [anywhere()],
        out_specs=(vmem(),) * 2 + (anywhere(),) * 2,
        scratch_shapes=[
            pltpu.VMEM((2, owners, rows, shard), BF16),
            pltpu.VMEM((owners, 1, small), F32),
            pltpu.VMEM((owners, 1, small), F32),
            pltpu.VMEM((reps, 1, small), F32),
            dma((2,)),
            dma((owners,)),
            dma((owners,)),
            dma((reps,)),
            dma((reps,)),
        ]
        + Scatter.scratch(owners, rows, width, PARTS)
        + RepSum.scratch(reps, owners, share, cols)
        + RepSum.scratch(reps, units, share, width),
        compiler_params=pltpu.CompilerParams(
            collective_id=4, has_side_effects=True, vmem_limit_bytes=60 * 2**20
        ),
        cost_estimate=pl.CostEstimate(
            flops=4 * owners * rows * width * cols,
            bytes_accessed=40 * 2**20,
            transcendentals=0,
        ),
        name="last",
    )(
        grads,
        weight,
        tokens,
        grad_hidden,
        gain,
        out_term,
        down_term,
        gain_mlp,
        gain_heads,
        entry_all,
    )


def in_rows_kernel(grads_ref, out_ref):
    units = out_ref.shape[2]
    grads = grads_ref[0].reshape(-1, 2 * units).astype(F32)
    out_ref[:, 0, :] = grads[:, :units]
    out_ref[:, 1, :] = grads[:, units:]


def in_rows(grads):
    owners, reps, share, cols = grads.shape
    units = cols // 2
    return pl.pallas_call(
        in_rows_kernel,
        grid=(owners,),
        out_shape=jax.ShapeDtypeStruct((reps * share, 2, owners * units), F32),
        in_specs=[pl.BlockSpec((1, reps, share, cols), lambda e: (e, 0, 0, 0))],
        out_specs=pl.BlockSpec((reps * share, 2, units), lambda e: (0, 0, e)),
        compiler_params=pltpu.CompilerParams(vmem_limit_bytes=40 * 2**20),
        name="in_rows",
    )(grads)


def qkvg_rows_kernel(groups, grads_ref, out_ref, buf, sem):
    e = pl.program_id(0)
    owners = pl.num_programs(0)

    def copies(e):
        slot = e % 2
        for i, (base, at, cols) in enumerate(groups):
            yield pltpu.make_async_copy(
                buf.at[slot, :, pl.ds(at, cols)],
                out_ref.at[:, pl.ds(pl.multiple_of(base + e * cols, HEAD_SIZE), cols)],
                sem.at[slot, i],
            )

    @pl.when(e >= 2)
    def _():
        for copy in copies(e - 2):
            copy.wait()

    buf[e % 2] = grads_ref[0].reshape(buf.shape[1:]).astype(F32)
    for copy in copies(e):
        copy.start()

    @pl.when(e == owners - 1)
    def _():
        for late in (e - 1, e):
            for copy in copies(late):
                copy.wait()


def qkvg_rows(grads, heads, kv_heads):
    owners, reps, share, cols = grads.shape
    q_cols, kv_cols = heads * HEAD_SIZE, kv_heads * HEAD_SIZE
    groups, base, at = [], 0, 0
    for width in (q_cols, q_cols, kv_cols, kv_cols):
        groups.append((base, at, width))
        base += width * owners
        at += width
    return pl.pallas_call(
        functools.partial(qkvg_rows_kernel, tuple(groups)),
        grid=(owners,),
        out_shape=jax.ShapeDtypeStruct((reps * share, owners * cols), F32),
        in_specs=[pl.BlockSpec((1, reps, share, cols), lambda e: (e, 0, 0, 0))],
        out_specs=anywhere(),
        scratch_shapes=[
            pltpu.VMEM((2, reps * share, cols), F32),
            pltpu.SemaphoreType.DMA((2, len(groups))),
        ],
        compiler_params=pltpu.CompilerParams(vmem_limit_bytes=40 * 2**20),
        name="qkvg_rows",
    )(grads)


def positions_of(block_ids):
    offsets = jnp.arange(BLOCK_TOKENS, dtype=jnp.int32)
    return (block_ids[:, :, None] * BLOCK_TOKENS + offsets[None, None, :]).reshape(
        block_ids.shape[0], -1
    )


def body(
    tokens,
    block_map,
    w_qkvg,
    w_out,
    w_in,
    w_down,
    norm_attn,
    norm_query,
    norm_key,
    norm_mlp,
    cotangent,
):
    owners = lax.axis_size("grp")
    me = lax.axis_index("grp")
    heads = QUERY_HEADS // owners
    sharers = max(1, owners // KEY_VALUE_HEADS)
    kv_heads = KEY_VALUE_HEADS * sharers // owners
    per_kv = heads // kv_heads
    q_cols = heads * HEAD_SIZE
    kv_cols = kv_heads * HEAD_SIZE
    rows_here, width = tokens.shape
    shard = w_qkvg.shape[0]
    block_rows = 2 * BLOCK_TOKENS
    seq_len = owners * block_rows
    all_q = QUERY_HEADS * HEAD_SIZE
    all_kv = KEY_VALUE_HEADS * HEAD_SIZE
    hidden_units = w_down.shape[0]

    reps = lax.axis_size("rep")
    share = shard // reps
    in_pieces = lax.dynamic_slice_in_dim(w_in, lax.axis_index("rep") * share, share, 0)
    in_pieces = in_pieces.reshape(share, 2, owners, hidden_units).transpose(2, 0, 1, 3)
    in_pieces = in_pieces.reshape(owners, share, 2 * hidden_units)
    head_part = norm_query.shape[0]
    spread = jnp.zeros((2, HEAD_SIZE), jnp.float32)
    spread = lax.dynamic_update_slice(
        spread, jnp.stack([norm_query, norm_key]).astype(jnp.float32), (0, me * head_part)
    )
    small = jnp.concatenate(
        [norm_attn.astype(jnp.float32), norm_mlp.astype(jnp.float32), spread.reshape(-1)]
    )[None]

    positions = positions_of(block_map)
    table = rotary_table(positions)
    table = table.reshape(GROUP_SEQUENCES, owners, block_rows, HEAD_SIZE)
    table = jnp.swapaxes(table, 0, 1).reshape(owners, rows_here, HEAD_SIZE)
    (
        attn_input,
        query_raw,
        gate_raw,
        key_raw,
        value_rows,
        query_rot,
        key_rot,
        qkvg_cols,
        small_all,
    ) = first(
        owners,
        reps,
        heads,
        kv_heads,
        sharers,
        tokens,
        w_qkvg,
        small,
        table,
    )
    small_all = small_all[:, 0]
    gain_attn = small_all[:, :shard].reshape(-1)
    gain_mlp = small_all[:, shard : 2 * shard].reshape(-1)
    spread = jnp.sum(small_all[:, 2 * shard :], axis=0)
    attn_out, hidden, mlp_own, cotangent_all, in_cols = attention(
        owners,
        reps,
        heads,
        kv_heads,
        tokens,
        query_rot,
        key_rot,
        value_rows,
        gate_raw,
        block_map,
        positions[:, None, :],
        w_out,
        gain_mlp[None],
        cotangent,
        in_pieces,
    )
    in_cols = in_cols.reshape(width, -1)
    (
        mlp_input,
        activated,
        grad_gate_up,
        grad_hidden,
        branch_own,
        gain_mlp_sum,
        down_term,
    ) = mlp(
        owners, reps, mlp_own, cotangent_all, in_cols, w_down, hidden, cotangent, gain_mlp[None]
    )
    _, output, grad_projected, gain_heads_sum, out_term, rows_in = backward(
        owners,
        reps,
        heads,
        kv_heads,
        branch_own,
        activated.reshape(owners, rows_here, hidden_units),
        w_down,
        w_out,
        hidden,
        query_raw,
        query_rot,
        gate_raw,
        key_raw,
        key_rot,
        value_rows,
        block_map,
        positions[:, None, :],
        table,
        spread[None],
        attn_out,
        grad_gate_up.reshape(owners, rows_here, 2 * hidden_units),
        mlp_input.reshape(owners, rows_here, width),
    )
    grad_tokens, gains, rows_qkvg, rows_both = last(
        owners,
        reps,
        grad_projected,
        qkvg_cols.reshape(width, -1),
        tokens,
        grad_hidden,
        gain_attn[None],
        out_term,
        down_term,
        gain_mlp_sum,
        gain_heads_sum,
        attn_input,
    )
    shard_in = in_rows(rows_in)
    down_units = w_down.shape[0] // shard
    shard_down = rows_both[:down_units].reshape(w_down.shape).astype(jnp.float32)
    shard_out = rows_both[down_units:].reshape(w_out.shape).astype(jnp.float32)
    if sharers == 1:
        shard_qkvg = qkvg_rows(rows_qkvg, heads, kv_heads)
    else:
        rows_qkvg = rows_qkvg.reshape(owners, shard, -1).swapaxes(0, 1).astype(jnp.float32)
        queries = [rows_qkvg[:, :, i * q_cols : (i + 1) * q_cols] for i in range(2)]
        others = [
            rows_qkvg[:, :, 2 * q_cols + i * kv_cols : 2 * q_cols + (i + 1) * kv_cols]
            .reshape(shard, owners // sharers, sharers, kv_cols)
            .sum(2)
            for i in range(2)
        ]
        shard_qkvg = jnp.concatenate(
            [part.reshape(shard, -1) for part in queries + others], axis=1
        )
    return (
        output,
        grad_tokens,
        shard_qkvg,
        shard_out,
        shard_in,
        shard_down,
        gains[0, :shard],
        lax.dynamic_slice_in_dim(gains[0], 2 * shard + me * head_part, head_part),
        lax.dynamic_slice_in_dim(gains[0], 2 * shard + HEAD_SIZE + me * head_part, head_part),
        gains[0, shard : 2 * shard],
    )


def solution(mesh):
    placed = (
        P(("rep", "grp"), None),
        P("rep", None),
        P("grp", None),
        P("grp", None),
        P("grp", None, None),
        P("grp", None),
        P("grp"),
        P("grp"),
        P("grp"),
        P("grp"),
        P(("rep", "grp"), None),
    )
    return jax.shard_map(
        body,
        mesh=mesh,
        in_specs=placed,
        out_specs=(
            P(("rep", "grp"), None),
            P(("rep", "grp"), None),
            P("grp", None),
            P("grp", None),
            P("grp", None, None),
            P("grp", None),
            P("grp"),
            P("grp"),
            P("grp"),
            P("grp"),
        ),
        check_vma=False,
    )
```
